32 devices in a mesh: cfg: 2 (over core), img: 4 (over y, x), seq: 4 (over z).
Axes of the slice: x: 2, y: 2, z: 4, core: 2. Of those that a mesh axis runs over, the one named last changes fastest.
Arguments:
- img_qkv: bfloat16 [2, 4, 512, 3, 2048], P('cfg', 'img', 'seq'), may hold values from -5 to 5
- txt_kv: bfloat16 [2, 4, 32, 2, 2048], P('cfg', 'img', 'seq'), may hold values from -5 to 5
- readout: bfloat16 [2048, 64], replicated, may hold values from -0.125 to 0.125
- old_velocity: float32 [4, 512, 64], P('img', 'seq'), may hold values from -6 to 6
- noise: float32 [4, 512, 64], P('img', 'seq'), may hold values from -5 to 5
- step_ratio: float32 [4], P('img'), may hold values from 0.2 to 0.8
- rewards: float32 [4], P('img'), may hold values from -6 to 6
- guidance: float32 [], replicated, may hold values from 1.5 to 3
Outputs:
- img_grad: bfloat16 [2, 4, 512, 3, 2048], P('cfg', 'img', 'seq')
- txt_grad: bfloat16 [2, 4, 32, 2, 2048], P('cfg', 'img', 'seq')
- readout_grad: float32 [2048, 64], replicated
- ratio: float32 [4], P('img')
The draws below stay inside these ranges and needn't reach their ends.
All inputs are finite; a program needn't handle non-finite values.
Results may differ from the reference program's by a relative error of at most 0.009.
Values may be sent and summed in bfloat16 or wider, within the bound.
No kernel may reach another device: no remote copies, remote signals or barrier semaphores. Data moves between devices by JAX's collectives and lax.ppermute only.
A program may use at most 128 MiB of HBM per device.

```python
import math
import jax
import jax.numpy as jnp
from jax import lax

HEADS = 16
HEAD_DIM = 128
CH = 64
IMAGES = 4
IMGTOK = 512
TXTTOK = 32
HD = 2048


def draw_img_qkv(key, part):
    width = HEADS * HEAD_DIM
    shape = (2, IMAGES, IMGTOK, 3, width)
    base_key = jax.random.fold_in(key, 11)
    slot_scale = jnp.array([1.6, 1.6, 1.0], jnp.float32).reshape(1, 1, 1, 3, 1)
    values = jnp.clip(jax.random.normal(base_key, shape, jnp.float32) * slot_scale, -5.0, 5.0)
    return values.astype(jnp.bfloat16)


def draw_old_velocity(key, part):
    shape = (IMAGES, IMGTOK, CH)
    first_key = jax.random.fold_in(key, 21)
    place = jnp.arange(IMGTOK, dtype=jnp.float32) / max(IMGTOK - 1, 1)
    rising = (0.35 * 3.0 ** place).reshape(1, IMGTOK, 1)
    values = jax.random.normal(first_key, shape, jnp.float32) * rising
    return jnp.clip(values, -6.0, 6.0)


def levels(stream_key, shape, split, smallest, high):
    def one(axis_at, blocks):
        steps = jax.random.uniform(jax.random.fold_in(jax.random.fold_in(stream_key, 6), axis_at), (blocks,), jnp.float32, smallest / len(split), high / len(split))
        return jnp.repeat(jnp.exp(steps), shape[axis_at] // blocks).reshape((-1,) + (1,) * (len(shape) - axis_at - 1))

    factor_of = one(*split[0])
    for cut in split[1:]:
        factor_of = factor_of * one(*cut)
    return factor_of


def gaussian(own_key, extent, scale, reach, shards=(), held_as=jnp.bfloat16):
    level = levels(own_key, extent, shards, -0.22, 0.18) if shards else 1.0
    drawn = jax.random.normal(own_key, extent, jnp.float32) * scale * level
    return jnp.minimum(jnp.maximum(drawn, -reach), reach).astype(held_as)


def setup_inputs(seed: int = 0) -> dict:
    splits = jax.random.split(jax.random.key(seed), 9)
    return {
        "img_qkv": draw_img_qkv(jax.random.fold_in(splits[8], 71), 0),
        "txt_kv": gaussian(splits[1], (2, IMAGES, TXTTOK, 2, HD), 1.3, 5.0, ((0, 2), (1, 4), (2, 4))),
        "readout": gaussian(splits[2], (HD, CH), HD ** -0.5, 0.125),
        "old_velocity": draw_old_velocity(jax.random.fold_in(splits[8], 71), 0),
        "noise": gaussian(splits[4], (IMAGES, IMGTOK, CH), 1.0, 5.0, ((0, 4), (1, 4)), jnp.float32),
        "step_ratio": jnp.clip(jnp.exp(math.log(0.8) - 1.3862944 * jax.random.uniform(splits[5], (IMAGES,), jnp.float32) ** levels(splits[5], (IMAGES,), ((0, 4),), -0.2, 0.2)), 0.2, 0.8),
        "rewards": gaussian(splits[6], (IMAGES,), 2.0, 6.0, ((0, 4),), jnp.float32),
        "guidance": jnp.clip(jax.random.uniform(splits[7], (), jnp.float32, 1.5, 3.0), 1.5, 3.0),
    }


def probabilities(query, keys):
    scores = jnp.dot(query, keys.T, preferred_element_type=jnp.float32) * HEAD_DIM ** (-0.5)
    top = lax.optimization_barrier(jnp.max(scores, axis=-1, keepdims=True))
    raised = jnp.exp(scores - top)
    return (raised / lax.optimization_barrier(jnp.sum(raised, axis=-1, keepdims=True))).astype(jnp.bfloat16)

def per_head(x):
    return x.reshape(x.shape[0], HEADS, HEAD_DIM).transpose(1, 0, 2)

def join_heads(x):
    return x.transpose(1, 0, 2).reshape(x.shape[1], HEADS * HEAD_DIM)

def forward_pair(pair):
    qkv, text = pair
    query = per_head(qkv[:, 0])
    keys = per_head(jnp.concatenate([text[:, 0], qkv[:, 1]], axis=0))
    values = per_head(jnp.concatenate([text[:, 1], qkv[:, 2]], axis=0))

    def one_head(item):
        head_q, head_k, head_v = item
        return jnp.dot(probabilities(head_q, head_k), head_v, preferred_element_type=jnp.float32).astype(jnp.bfloat16)
    return join_heads(lax.map(one_head, (query, keys, values)))

def backward_pair(pair):
    qkv, text, grad_out = pair
    query = per_head(qkv[:, 0])
    keys = per_head(jnp.concatenate([text[:, 0], qkv[:, 1]], axis=0))
    values = per_head(jnp.concatenate([text[:, 1], qkv[:, 2]], axis=0))
    grads = per_head(grad_out)

    def one_head(item):
        head_q, head_k, head_v, head_g = item
        probs = probabilities(head_q, head_k)
        grad_probs = jnp.dot(head_g, head_v.T, preferred_element_type=jnp.float32)
        weights = probs.astype(jnp.float32)
        delta = lax.optimization_barrier(jnp.sum(weights * grad_probs, axis=-1, keepdims=True))
        grad_scores = (weights * (grad_probs - delta) * HEAD_DIM ** (-0.5)).astype(jnp.bfloat16)
        grad_query = jnp.dot(grad_scores, head_k, preferred_element_type=jnp.float32).astype(jnp.bfloat16)
        grad_keys = jnp.dot(grad_scores.T, head_q, preferred_element_type=jnp.float32)
        grad_values = jnp.dot(probs.T, head_g, preferred_element_type=jnp.float32)
        return (grad_query, grad_keys, grad_values)
    grad_query, grad_keys, grad_values = lax.map(one_head, (query, keys, values, grads))
    return (join_heads(grad_query), join_heads(grad_keys), join_heads(grad_values))

def surrogate_gain(ratio, advantage):
    clipped = jnp.clip(ratio, 0.8, 1.2)
    keep = ratio * advantage <= clipped * advantage
    return jnp.where(keep, -ratio * advantage, jnp.zeros_like(ratio))

def reference(img_qkv, txt_kv, readout, old_velocity, noise, step_ratio, rewards, guidance):
    width = HEADS * HEAD_DIM
    pairs_img = img_qkv.reshape(2 * IMAGES, IMGTOK, 3, width)
    pairs_txt = txt_kv.reshape(2 * IMAGES, TXTTOK, 2, width)
    attended = lax.map(forward_pair, (pairs_img, pairs_txt))
    velocity = jnp.einsum('pnd,dc->pnc', attended.astype(jnp.float32), readout.astype(jnp.float32), precision=lax.Precision.HIGHEST).reshape(2, IMAGES, IMGTOK, CH)
    guided = velocity[1] + guidance * (velocity[0] - velocity[1])
    rate = step_ratio[:, None, None]
    deviation = rate * (guided - old_velocity)
    log_ratio = lax.optimization_barrier(jnp.sum(noise * deviation - 0.5 * deviation * deviation, axis=(1, 2))) / (IMGTOK * CH)
    ratio = jnp.exp(log_ratio)
    mean = jnp.sum(rewards) / IMAGES
    square = jnp.sum(rewards * rewards) / IMAGES
    spread = jnp.sqrt(jnp.maximum(square - mean * mean, 0.0))
    advantage = (rewards - mean) / jnp.maximum(spread, 1.0)
    gain = surrogate_gain(ratio, advantage)
    grad_guided = gain[:, None, None] * rate * (noise - deviation)
    grad_velocity = jnp.stack([guidance * grad_guided, (1.0 - guidance) * grad_guided]).reshape(2 * IMAGES, IMGTOK, CH)
    readout_grad = jnp.einsum('pnd,pnc->dc', attended.astype(jnp.float32), grad_velocity, precision=lax.Precision.HIGHEST)
    grad_attended = jnp.einsum('pnc,dc->pnd', grad_velocity, readout.astype(jnp.float32), precision=lax.Precision.HIGHEST).astype(jnp.bfloat16)
    grad_query, grad_keys, grad_values = lax.map(backward_pair, (pairs_img, pairs_txt, grad_attended))
    img_grad = jnp.stack([grad_query, grad_keys[:, TXTTOK:].astype(jnp.bfloat16), grad_values[:, TXTTOK:].astype(jnp.bfloat16)], axis=2).reshape(2, IMAGES, IMGTOK, 3, width)
    txt_grad = jnp.stack([grad_keys[:, :TXTTOK], grad_values[:, :TXTTOK]], axis=2).astype(jnp.bfloat16).reshape(2, IMAGES, TXTTOK, 2, width)
    return (img_grad, txt_grad, readout_grad, ratio)
```

```python
import functools

import jax
import jax.numpy as jnp
from jax import lax
from jax.experimental import pallas as pl
from jax.experimental.pallas import tpu as pltpu
from jax.sharding import PartitionSpec as P

HEADS = 16
HEAD_DIM = 128
SCALE = HEAD_DIM ** (-0.5)
F32 = jnp.float32
BF16 = jnp.bfloat16
PARAMS = pltpu.CompilerParams(vmem_limit_bytes=40 * 1024 * 1024)
SMEM = pl.BlockSpec(memory_space=pltpu.SMEM)


def dot(a, b):
    return jnp.dot(a, b, preferred_element_type=F32)


def dot_nt(a, b):
    return lax.dot_general(a, b, (((1,), (1,)), ((), ())), preferred_element_type=F32)


def dot_tn(a, b):
    return lax.dot_general(a, b, (((0,), (0,)), ((), ())), preferred_element_type=F32)


def whole(shape):
    return pl.BlockSpec(shape, lambda *_: (0,) * len(shape))


def at(refs, slot):
    return refs[slot].at[0] if len(refs) > 1 else refs[0].at[slot]


def cols(start, size):
    return pl.ds(pl.multiple_of(start, 128), size)


def tree_sum(terms):
    while len(terms) > 1:
        terms = [terms[k] + terms[k + 1] for k in range(0, len(terms), 2)]
    return terms[0]


def mirror(x, axis, apart):
    count = lax.axis_size(axis)
    return lax.ppermute(x, axis, [(i, i ^ apart) for i in range(count)])


class Sizes:
    def __init__(self, img_rows, txt_rows, features, channels):
        self.parts = lax.axis_size("seq")
        self.copies = max(1, self.parts // HEADS)
        self.groups = self.parts // self.copies
        self.features = features
        self.ch = channels
        self.width = features // self.groups
        self.heads = self.width // HEAD_DIM
        self.rows = img_rows
        self.txt = txt_rows
        self.sub = img_rows // self.copies
        self.img_keys = self.parts * img_rows
        self.keys = self.img_keys + self.parts * txt_rows
        self.queries = self.parts * self.sub
        self.block_rows = self.sub + self.rows + 2 * self.txt
        self.mirrored = self.parts in (1, 2, 4, 8) and self.copies == 1
        self.lists = self.parts if self.mirrored else 1
        self.each = self.parts // self.lists
        block = self.queries
        while block % 256 == 0 and self.keys * block > 600_000:
            block //= 2
        self.q_block = block
        self.q_blocks = self.queries // block

    def head_specs(self, rows, width):
        return [
            pl.BlockSpec((self.each, rows, width), lambda h, b: (0, 0, h))
            for _ in range(self.lists)
        ]

    def shapes(self, rows, width, dtype):
        return [
            jax.ShapeDtypeStruct((self.each, rows, width), dtype) for _ in range(self.lists)
        ]

    def specs(self, rows, width):
        return [whole((self.each, rows, width)) for _ in range(self.lists)]


def exchange(size, blocks):
    if size.mirrored:
        return [blocks[0]] + [mirror(blocks[k], "seq", k) for k in range(1, size.parts)]
    return [lax.all_to_all(blocks[0], "seq", split_axis=0, concat_axis=0, tiled=True)]


def pack_kernel(size, ints, qk, text, *outs):
    for slot in range(size.parts):
        dest = ints[0] ^ slot
        group = dest // size.copies
        place = cols(group * size.width, size.width)
        out = at(outs, slot)
        if size.copies == 1:
            out[: size.sub] = qk[0, :, place]
        else:
            first = pl.multiple_of((dest % size.copies) * size.sub, 16)
            out[: size.sub] = qk[0, pl.ds(first, size.sub), place]
        out[size.sub : size.sub + size.rows] = qk[1, :, place]
        out[size.sub + size.rows :] = text[:, place]


def pack(size, ints, slots, text):
    return pl.pallas_call(
        functools.partial(pack_kernel, size),
        grid=(1,),
        in_specs=[SMEM, whole((2,) + slots.shape[1:]), whole(text.shape)],
        out_specs=size.specs(size.block_rows, size.width),
        out_shape=size.shapes(size.block_rows, size.width, BF16),
        compiler_params=PARAMS,
        name="pack_queries_keys",
    )(ints, slots, text)


def project_kernel(size, ints, floats, value, readout, noise, old, mixed_out, *outs):
    for slot in range(size.parts):
        group = (ints[0] ^ slot) // size.copies
        out = at(outs, slot)
        for head in range(size.heads):
            place = cols(group * size.width + head * HEAD_DIM, HEAD_DIM)
            projected = dot(value[0, :, place], readout[place, :])
            out[:, head * size.rows : (head + 1) * size.rows] = projected.T.astype(BF16)
    mixed = noise[...] + floats[0] * old[...]
    squares = jnp.sum(noise[...] * noise[...], axis=(0, 1), keepdims=True)
    mixed_out[: size.ch] = mixed.T
    mixed_out[size.ch :] = jnp.broadcast_to(squares, (8, size.rows))


def project(size, ints, floats, slots, readout, noise, old):
    outs = pl.pallas_call(
        functools.partial(project_kernel, size),
        grid=(1,),
        in_specs=[
            SMEM,
            SMEM,
            pl.BlockSpec((1,) + slots.shape[1:], lambda *_: (2, 0, 0)),
            whole(readout.shape),
            whole(noise.shape),
            whole(old.shape),
        ],
        out_specs=[whole((size.ch + 8, size.rows))] + size.specs(size.ch, size.heads * size.rows),
        out_shape=[jax.ShapeDtypeStruct((size.ch + 8, size.rows), F32)]
        + size.shapes(size.ch, size.heads * size.rows, BF16),
        compiler_params=PARAMS,
        name="project_values",
    )(ints, floats, slots, readout, noise, old)
    return outs[0], outs[1:]


def gather_queries(size, blocks, queries):
    for slot in range(size.parts):
        queries[slot * size.sub : (slot + 1) * size.sub] = at(blocks, slot)[: size.sub]


def text_rows(size, blocks, second):
    first = size.sub + size.rows
    found = []
    for slot in range(size.parts):
        pair = at(blocks, slot)[first : first + 2 * size.txt].astype(F32)
        found.append(pair[size.txt :] if second else pair[: size.txt])
    return jnp.concatenate(found, axis=0).astype(BF16)


def gather_keys(size, blocks, keys):
    for slot in range(size.parts):
        part = at(blocks, slot)[size.sub : size.sub + size.rows]
        keys[slot * size.rows : (slot + 1) * size.rows] = part
    keys[size.img_keys :] = text_rows(size, blocks, False)


def probs_kernel(size, *refs):
    blocks = refs[: size.lists]
    probs, keys, queries = refs[size.lists :]
    step = pl.program_id(1)

    @pl.when(step == 0)
    def _():
        gather_queries(size, blocks, queries)
        gather_keys(size, blocks, keys)

    first = pl.multiple_of(step * size.q_block, 128)
    scores = dot_nt(keys[...], queries[pl.ds(first, size.q_block), :]) * SCALE
    top = jnp.max(scores, axis=0, keepdims=True)
    raised = jnp.exp(scores - top)
    total = jnp.sum(raised, axis=0, keepdims=True)
    probs[0] = (raised * (1.0 / total)).astype(BF16)


def probabilities(size, blocks):
    return pl.pallas_call(
        functools.partial(probs_kernel, size),
        grid=(size.heads, size.q_blocks),
        in_specs=size.head_specs(size.block_rows, HEAD_DIM),
        out_specs=pl.BlockSpec((1, size.keys, size.q_block), lambda h, b: (h, 0, b)),
        out_shape=jax.ShapeDtypeStruct((size.heads, size.keys, size.queries), BF16),
        scratch_shapes=[
            pltpu.VMEM((size.keys, HEAD_DIM), BF16),
            pltpu.VMEM((size.queries, HEAD_DIM), BF16),
        ],
        compiler_params=PARAMS,
        name="attention_probs",
    )(*blocks)


def joined_projection(size, projected):
    return jnp.concatenate([at(projected, slot)[...] for slot in range(size.parts)], axis=1)


def guided_kernel(size, ints, floats, *refs):
    blocks = refs[: size.lists]
    projected = refs[size.lists : 2 * size.lists]
    readout, probs, out = refs[2 * size.lists :]
    head = pl.program_id(1)
    place = cols(ints[1] * size.width + head * HEAD_DIM, HEAD_DIM)
    text = dot(text_rows(size, blocks, True), readout[place, :]).astype(BF16)
    image = joined_projection(size, projected)
    part = dot(image, probs[0, : size.img_keys]) + dot_tn(text, probs[0, size.img_keys :])
    part = part * floats[1]

    @pl.when(head == 0)
    def _():
        out[...] = part

    @pl.when(head > 0)
    def _():
        out[...] += part


def guided_part(size, ints, floats, blocks, projected, readout, probs):
    def swap(spec):
        index = spec.index_map
        return pl.BlockSpec(spec.block_shape, lambda b, h: index(h, b))

    return pl.pallas_call(
        functools.partial(guided_kernel, size),
        grid=(size.q_blocks, size.heads),
        in_specs=[SMEM, SMEM]
        + [swap(s) for s in size.head_specs(size.block_rows, HEAD_DIM)]
        + [swap(s) for s in size.head_specs(size.ch, size.rows)]
        + [
            whole(readout.shape),
            pl.BlockSpec((1, size.keys, size.q_block), lambda b, h: (h, 0, b)),
        ],
        out_specs=pl.BlockSpec((size.ch, size.q_block), lambda b, h: (0, b)),
        out_shape=jax.ShapeDtypeStruct((size.ch, size.queries), F32),
        compiler_params=PARAMS,
        name="guided_part",
    )(ints, floats, *blocks, *projected, readout, probs)


def surrogate_gain(ratio, advantage):
    clipped = jnp.clip(ratio, 0.8, 1.2)
    keep = ratio * advantage <= clipped * advantage
    return jnp.where(keep, -ratio * advantage, jnp.zeros_like(ratio))


def grad_values_kernel(size, floats, *refs):
    if size.mirrored:
        guided_parts = refs[: size.parts]
        mixed = refs[size.parts : 2 * size.parts]
        refs = refs[2 * size.parts :]
    else:
        given, refs = refs[0], refs[1:]
    probs, grad_out, ratio_out = refs[:3]
    outs = refs[3 : 3 + size.lists]
    total = refs[3 + size.lists]
    head, step = pl.program_id(0), pl.program_id(1)

    @pl.when((head == 0) & (step == 0))
    def _():
        if size.mirrored:
            rest = []
            for slot in range(size.parts):
                parts = []
                for apart in range(size.parts):
                    other = slot ^ apart
                    part = guided_parts[apart][:, other * size.sub : (other + 1) * size.sub]
                    parts.append(part.astype(F32))
                rest.append(mixed[slot][: size.ch] - floats[0] * tree_sum(parts))
            norm = tree_sum([jnp.sum(x * x, axis=(0, 1), keepdims=True) for x in rest])
            squares = tree_sum([x[size.ch : size.ch + 1, :1] for x in mixed])
            count = size.queries * size.ch
            ratio = jnp.exp((squares - norm) * (0.5 / count))
            gain = surrogate_gain(ratio, jnp.full((1, 1), floats[2], F32))
            factor = gain * (floats[0] * floats[1])
            for slot in range(size.parts):
                place = slice(slot * size.sub, (slot + 1) * size.sub)
                grad_out[:, place] = (rest[slot] * factor).astype(BF16)
            ratio_out[...] = jnp.broadcast_to(ratio, ratio_out.shape)
        else:
            grad_out[...] = given[...]
            ratio_out[...] = jnp.zeros(ratio_out.shape, F32)

    first = pl.multiple_of(step * size.q_block, 128)
    part = dot_nt(grad_out[:, pl.ds(first, size.q_block)], probs[0])
    if size.q_blocks == 1:
        done = part
    else:

        @pl.when(step == 0)
        def _():
            total[...] = part

        @pl.when(step > 0)
        def _():
            total[...] += part

        done = total[...]
    for slot in range(size.parts):
        at(outs, slot)[...] = done[:, slot * size.rows : (slot + 1) * size.rows].astype(BF16)


def grad_values(size, floats, given, probs):
    specs = [whole(x.shape) for x in given]
    outs = pl.pallas_call(
        functools.partial(grad_values_kernel, size),
        grid=(size.heads, size.q_blocks),
        in_specs=[SMEM]
        + specs
        + [pl.BlockSpec((1, size.img_keys, size.q_block), lambda h, b: (h, 0, b))],
        out_specs=[whole((size.ch, size.queries)), whole((8, 128))]
        + size.head_specs(size.ch, size.rows),
        out_shape=[
            jax.ShapeDtypeStruct((size.ch, size.queries), BF16),
            jax.ShapeDtypeStruct((8, 128), F32),
        ]
        + size.shapes(size.ch, size.heads * size.rows, BF16),
        scratch_shapes=[pltpu.VMEM((size.ch, size.img_keys), F32)],
        compiler_params=PARAMS,
        name="grad_values",
    )(floats, *given, probs)
    return outs[0], outs[1], outs[2:]


def backward_kernel(size, ints, *refs):
    blocks = refs[: size.lists]
    projected = refs[size.lists : 2 * size.lists]
    readout, probs_ref, grad_ref, text_out = refs[2 * size.lists : 2 * size.lists + 4]
    outs = refs[2 * size.lists + 4 : 3 * size.lists + 4]
    keys, queries, grad_keys, grad_queries, grad_text = refs[3 * size.lists + 4 :]
    head, step = pl.program_id(0), pl.program_id(1)

    @pl.when(step == 0)
    def _():
        gather_queries(size, blocks, queries)
        gather_keys(size, blocks, keys)

    place = cols(ints[1] * size.width + head * HEAD_DIM, HEAD_DIM)
    first = pl.multiple_of(step * size.q_block, 128)
    text_values = text_rows(size, blocks, True)
    text = dot(text_values, readout[place, :]).astype(BF16)
    image = joined_projection(size, projected)
    grad = grad_ref[:, pl.ds(first, size.q_block)]
    probs = probs_ref[0]
    weights = probs.astype(F32)
    grad_probs = jnp.concatenate([dot_tn(image, grad), dot(text, grad)], axis=0)
    delta = jnp.sum(weights * grad_probs, axis=0, keepdims=True)
    grad_scores = (weights * (grad_probs - delta) * SCALE).astype(BF16)
    key_part = dot(grad_scores, queries[pl.ds(first, size.q_block), :])
    text_part = dot_nt(probs[size.img_keys :], grad)
    query_part = dot_tn(keys[...], grad_scores).T

    @pl.when(step == 0)
    def _():
        grad_keys[...] = key_part
        grad_text[...] = text_part

    @pl.when(step > 0)
    def _():
        grad_keys[...] += key_part
        grad_text[...] += text_part

    grad_queries[pl.ds(first, size.q_block), :] = query_part.astype(BF16)

    @pl.when(step == size.q_blocks - 1)
    def _():
        summed = grad_text[...].astype(BF16)
        value_text = dot_nt(summed, readout[place, :])
        text_out[...] = dot_tn(summed, text_values)
        for slot in range(size.parts):
            out = at(outs, slot)
            out[: size.sub] = grad_queries[slot * size.sub : (slot + 1) * size.sub]
            out[size.sub : size.sub + size.rows] = grad_keys[
                slot * size.rows : (slot + 1) * size.rows
            ].astype(BF16)
            start = size.img_keys + slot * size.txt
            pair = [
                grad_keys[start : start + size.txt],
                value_text[slot * size.txt : (slot + 1) * size.txt],
            ]
            out[size.sub + size.rows :] = jnp.concatenate(pair, axis=0).astype(BF16)


def backward(size, ints, blocks, projected, readout, probs, grad):
    outs = pl.pallas_call(
        functools.partial(backward_kernel, size),
        grid=(size.heads, size.q_blocks),
        in_specs=[SMEM]
        + size.head_specs(size.block_rows, HEAD_DIM)
        + size.head_specs(size.ch, size.rows)
        + [
            whole(readout.shape),
            pl.BlockSpec((1, size.keys, size.q_block), lambda h, b: (h, 0, b)),
            whole(grad.shape),
        ],
        out_specs=[pl.BlockSpec((size.ch, HEAD_DIM), lambda h, b: (0, h))]
        + size.head_specs(size.block_rows, HEAD_DIM),
        out_shape=[jax.ShapeDtypeStruct((size.ch, size.width), F32)]
        + size.shapes(size.block_rows, size.width, BF16),
        scratch_shapes=[
            pltpu.VMEM((size.keys, HEAD_DIM), BF16),
            pltpu.VMEM((size.queries, HEAD_DIM), BF16),
            pltpu.VMEM((size.keys, HEAD_DIM), F32),
            pltpu.VMEM((size.queries, HEAD_DIM), BF16),
            pltpu.VMEM((size.parts * size.txt, size.ch), F32),
        ],
        compiler_params=PARAMS,
        name="attention_backward",
    )(ints, *blocks, *projected, readout, probs, grad)
    return outs[0], outs[1:]


def home_values_kernel(size, pieces, ints, *refs):
    blocks = refs[: size.lists]
    value, readout, text, grad_out, part_out = refs[size.lists :]
    piece_width = size.features // pieces

    def target(start):
        piece = (start // piece_width) ^ ints[2]
        return piece * piece_width + start % piece_width

    for group in range(size.groups):
        held = [
            at(blocks, group * size.copies + copy)[...].astype(F32) for copy in range(size.copies)
        ]
        summed = sum(held[1:], held[0])
        owner = ints[0] ^ group
        for head in range(size.heads):
            start = owner * size.width + head * HEAD_DIM
            place = cols(start, HEAD_DIM)
            part = summed[:, head * size.rows : (head + 1) * size.rows]
            grad_out[:, place] = dot_nt(part.T.astype(BF16), readout[place, :]).astype(BF16)
            product = dot(part.astype(BF16), value[0, :, place])
            part_out[:, cols(target(start), HEAD_DIM)] = product
    for head in range(size.heads):
        start = ints[1] * size.width + head * HEAD_DIM
        part_out[:, cols(target(start), HEAD_DIM)] += text[
            :, head * HEAD_DIM : (head + 1) * HEAD_DIM
        ]


def home_values(size, pieces, ints, blocks, slots, readout, text):
    shape = slots.shape[1:]
    return pl.pallas_call(
        functools.partial(home_values_kernel, size, pieces),
        grid=(1,),
        in_specs=[SMEM]
        + size.specs(size.ch, size.heads * size.rows)
        + [
            pl.BlockSpec((1,) + shape, lambda *_: (2, 0, 0)),
            whole(readout.shape),
            whole(text.shape),
        ],
        out_specs=[whole(shape), whole((size.ch, size.features))],
        out_shape=[
            jax.ShapeDtypeStruct(shape, BF16),
            jax.ShapeDtypeStruct((size.ch, size.features), F32),
        ],
        compiler_params=PARAMS,
        name="home_values",
    )(ints, *blocks, slots, readout, text)


def home_kernel(size, ints, *refs):
    blocks = refs[: size.lists]
    out, text_out = refs[size.lists :]
    for group in range(size.groups):
        place = cols((ints[0] ^ group) * size.width, size.width)
        held = [at(blocks, group * size.copies + copy) for copy in range(size.copies)]
        for copy in range(size.copies):
            out[0, copy * size.sub : (copy + 1) * size.sub, place] = held[copy][: size.sub]
        if size.copies == 1:
            out[1, :, place] = held[0][size.sub : size.sub + size.rows]
            text_out[:, place] = held[0][size.sub + size.rows :]
        else:
            rest = sum([x[size.sub :].astype(F32) for x in held]).astype(BF16)
            out[1, :, place] = rest[: size.rows]
            text_out[:, place] = rest[size.rows :]


def home(size, ints, blocks):
    return pl.pallas_call(
        functools.partial(home_kernel, size),
        grid=(1,),
        in_specs=[SMEM] + size.specs(size.block_rows, size.width),
        out_specs=[
            whole((2, size.rows, size.features)),
            whole((2 * size.txt, size.features)),
        ],
        out_shape=[
            jax.ShapeDtypeStruct((2, size.rows, size.features), BF16),
            jax.ShapeDtypeStruct((2 * size.txt, size.features), BF16),
        ],
        compiler_params=PARAMS,
        name="home_queries_keys",
    )(ints, *blocks)


def turn_kernel(ints, *refs):
    pieces, out = refs[:-1], refs[-1]
    per = pieces[0].shape[1]
    for slot, piece in enumerate(pieces):
        first = pl.multiple_of((slot ^ ints[2]) * per, 128)
        out[pl.ds(first, per), :] = piece[...].astype(F32).T


def sum_readout(size, ints, part):
    branches, images = lax.axis_size("cfg"), lax.axis_size("img")
    half = part.shape[1] // branches
    own = part[:, :half] + mirror(part[:, half:], "cfg", 1)
    per = half // images
    sent = own.astype(BF16)
    mine = own[:, :per]
    for k in range(1, images):
        mine = mine + mirror(sent[:, k * per : (k + 1) * per], "img", k).astype(F32)
    sent = mine.astype(BF16)
    held = [sent] + [mirror(sent, "seq", k) for k in range(1, size.parts)]
    total = tree_sum([x.astype(F32) for x in held]).astype(BF16)
    found = [total] + [mirror(total, "img", k) for k in range(1, images)]
    found = found + [mirror(x, "cfg", 1) for x in found]
    return pl.pallas_call(
        turn_kernel,
        grid=(1,),
        in_specs=[SMEM] + [whole(x.shape) for x in found],
        out_specs=whole((part.shape[1], part.shape[0])),
        out_shape=jax.ShapeDtypeStruct((part.shape[1], part.shape[0]), F32),
        compiler_params=PARAMS,
        name="turn_readout_grad",
    )(ints, *found)


def on_device(img_qkv, txt_kv, readout, old_velocity, noise, step_ratio, rewards, guidance):
    features, channels = readout.shape
    size = Sizes(img_qkv.shape[2], txt_kv.shape[2], features, channels)
    branches, images = lax.axis_size("cfg"), lax.axis_size("img")
    pieces = branches * images
    split = size.mirrored and branches == 2 and images in (1, 2, 4, 8)
    branch = lax.axis_index("cfg")
    place = lax.axis_index("seq")
    piece = branch * images + lax.axis_index("img")
    ints = jnp.stack(
        [
            place if size.mirrored else jnp.zeros_like(place),
            place // size.copies,
            piece if split else jnp.zeros_like(piece),
        ]
    ).astype(jnp.int32)
    slots = img_qkv[0, 0].transpose(1, 0, 2)
    text = txt_kv[0, 0].transpose(1, 0, 2).reshape(2 * size.txt, features)
    blocks = exchange(size, pack(size, ints, slots, text))

    reward = rewards[0]
    if images in (2, 4, 8):
        every = [reward] + [mirror(rewards, "img", k)[0] for k in range(1, images)]
        mean = tree_sum(every) / images
        square = tree_sum([x * x for x in every]) / images
    else:
        mean = lax.psum(reward, "img") / images
        square = lax.psum(reward * reward, "img") / images
    spread = jnp.sqrt(jnp.maximum(square - mean * mean, 0.0))
    advantage = (reward - mean) / jnp.maximum(spread, 1.0)
    rate = step_ratio[0]
    weight = jnp.where(branch == 0, guidance, 1.0 - guidance)
    early = jnp.stack([rate, weight])
    mixed, projected = project(size, ints, early, slots, readout, noise[0], old_velocity[0])
    projected = exchange(size, projected)
    floats = jnp.stack([rate, weight, advantage])

    probs = probabilities(size, blocks)
    part = guided_part(size, ints, early, blocks, projected, readout, probs)
    summed = part + mirror(part, "cfg", 1)
    if size.mirrored:
        all_mixed = [mixed] + [mirror(mixed, "seq", k) for k in range(1, size.parts)]
        sent = summed.astype(BF16)
        given = [sent] + [mirror(sent, "seq", k) for k in range(1, size.parts)] + all_mixed
    else:
        copy = place % size.copies
        chosen = jnp.arange(size.copies).reshape(-1, 1, 1) == copy
        guided = lax.psum(jnp.where(chosen, summed[None], 0.0), "seq")
        guided = lax.dynamic_index_in_dim(guided, copy, 0, False)
        all_mixed = lax.all_gather(mixed, "seq", axis=0)
        squares = jnp.sum(all_mixed[:, channels, 0])
        near = lax.dynamic_slice_in_dim(all_mixed[:, :channels], copy * size.sub, size.sub, 2)
        near = near.transpose(1, 0, 2).reshape(channels, size.queries)
        left = near - rate * guided
        norm = lax.psum(jnp.sum(left * left), "seq") / size.groups
        ratio = jnp.exp((squares - norm) * (0.5 / (size.parts * size.rows * channels)))
        gain = surrogate_gain(ratio, advantage)
        given = [(left * (gain * (rate * weight))).astype(BF16)]
    grad, found_ratio, value_blocks = grad_values(size, floats, given, probs)
    if size.mirrored:
        ratio = found_ratio[0, 0]
    value_home = exchange(size, value_blocks)
    text_part, grad_blocks = backward(size, ints, blocks, projected, readout, probs, grad)
    grad_home = exchange(size, grad_blocks)
    value_grad, readout_part = home_values(
        size, pieces if split else 1, ints, value_home, slots, readout, text_part
    )
    if split:
        readout_grad = sum_readout(size, ints, readout_part)
    else:
        readout_grad = lax.psum(readout_part, ("cfg", "img", "seq")).T
    token_grads, text_grads = home(size, ints, grad_home)
    img_grad = jnp.stack([token_grads[0], token_grads[1], value_grad], axis=1)[None, None]
    txt_grad = text_grads.reshape(2, size.txt, features).transpose(1, 0, 2)[None, None]
    return (img_grad, txt_grad, readout_grad, ratio.reshape(1))


def solution(mesh):
    return jax.shard_map(
        on_device,
        mesh=mesh,
        in_specs=(
            P("cfg", "img", "seq", None, None),
            P("cfg", "img", "seq", None, None),
            P(),
            P("img", "seq", None),
            P("img", "seq", None),
            P("img"),
            P("img"),
            P(),
        ),
        out_specs=(
            P("cfg", "img", "seq", None, None),
            P("cfg", "img", "seq", None, None),
            P(),
            P("img"),
        ),
        check_vma=False,
    )
```

```python
import functools
import math

import jax
import jax.numpy as jnp
from jax import lax
from jax.experimental import pallas as pl
from jax.experimental.pallas import tpu as pltpu
from jax.sharding import PartitionSpec as P

HEADS = 16
HEAD_DIM = 128
SCALE = HEAD_DIM ** (-0.5)
EXP2_SCALE = SCALE * math.log2(math.e)
F32 = jnp.float32
BF16 = jnp.bfloat16
MIB = 1024 * 1024
SMEM = pl.BlockSpec(memory_space=pltpu.SMEM)
ANY = pl.BlockSpec(memory_space=pl.ANY)


def dot(a, b):
    return jnp.dot(a, b, preferred_element_type=F32)


def dot_nt(a, b):
    return lax.dot_general(a, b, (((1,), (1,)), ((), ())), preferred_element_type=F32)


def dot_tn(a, b):
    return lax.dot_general(a, b, (((0,), (0,)), ((), ())), preferred_element_type=F32)


def whole(shape):
    return pl.BlockSpec(shape, lambda *_: (0,) * len(shape))


def at(refs, slot):
    return refs[slot].at[0] if len(refs) > 1 else refs[0].at[slot]


def cols(start, size):
    return pl.ds(pl.multiple_of(start, 128), size)


def tree_sum(terms):
    while len(terms) > 1:
        terms = [terms[k] + terms[k + 1] for k in range(0, len(terms), 2)]
    return terms[0]


def mirror(x, axis, apart):
    count = lax.axis_size(axis)
    return lax.ppermute(x, axis, [(i, i ^ apart) for i in range(count)])


class Sizes:
    def __init__(self, img_rows, txt_rows, features, channels):
        self.parts = lax.axis_size("seq")
        self.images = lax.axis_size("img")
        self.copies = max(1, self.parts // HEADS)
        self.groups = self.parts // self.copies
        self.features = features
        self.ch = channels
        self.width = features // self.groups
        self.heads = self.width // HEAD_DIM
        self.rows = img_rows
        self.txt = txt_rows
        self.sub = img_rows // self.copies
        self.img_keys = self.parts * img_rows
        self.keys = self.img_keys + self.parts * txt_rows
        self.queries = self.parts * self.sub
        self.mirrored = self.parts in (1, 2, 4, 8) and self.copies == 1
        self.lists = self.parts if self.mirrored else 1
        self.each = self.parts // self.lists
        self.at_keys = self.sub
        self.at_values = self.sub + self.rows
        self.at_text = self.sub + 2 * self.rows
        self.at_mixed = self.at_text + 2 * self.txt
        self.folds = self.width // (2 * self.rows)
        self.per_fold = self.ch // max(1, self.folds)
        self.at_squares = self.at_mixed + (self.per_fold if self.folds else 2 * self.ch)
        self.sent_rows = self.at_squares + 16
        self.at_pair = self.sub + self.rows
        self.at_small = self.at_pair + 2 * self.txt
        self.home_rows = self.at_small + self.ch
        block = self.queries
        while block % 256 == 0 and self.keys * block > 600_000:
            block //= 2
        self.q_block = block
        self.q_blocks = self.queries // block
        limit = (16 if self.mirrored else 48) * MIB
        self.params = pltpu.CompilerParams(vmem_limit_bytes=limit)

    def tiles(self):
        edges = list(range(0, self.img_keys, self.rows)) + [self.img_keys, self.keys]
        return list(zip(edges[:-1], edges[1:]))

    def shapes(self, rows):
        shape = (self.each, rows, self.width)
        return [jax.ShapeDtypeStruct(shape, BF16) for _ in range(self.lists)]

    def specs(self, rows):
        return [whole((self.each, rows, self.width)) for _ in range(self.lists)]

    def head_specs(self, rows, index):
        return [
            pl.BlockSpec((self.each, rows, HEAD_DIM), lambda *g: (0, 0, index(*g)))
            for _ in range(self.lists)
        ]

    def base(self):
        place = lax.axis_index("seq")
        return place if self.mirrored else jnp.zeros_like(place)

    def group(self):
        return lax.axis_index("seq") // self.copies


def exchange(size, blocks):
    if size.mirrored:
        return [blocks[0]] + [mirror(blocks[k], "seq", k) for k in range(1, size.parts)]
    return [lax.all_to_all(blocks[0], "seq", split_axis=0, concat_axis=0, tiled=True)]


def branch_weight(guidance):
    return jnp.where(lax.axis_index("cfg") == 0, guidance, 1.0 - guidance)


def pack_kernel(size, rate, slots, text, noise, old, readout, *refs):
    outs = refs[: size.lists]
    held, block, arrived, left = refs[size.lists :]
    incoming = []
    places = []
    for slot in range(size.parts):
        dest = size.base() ^ slot
        place = cols((dest // size.copies) * size.width, size.width)
        places.append(place)
        if size.copies == 1:
            queries = slots.at[0, :, place]
        else:
            first = pl.multiple_of((dest % size.copies) * size.sub, 16)
            queries = slots.at[0, pl.ds(first, size.sub), place]
        ends = (
            (queries, block.at[slot, pl.ds(0, size.sub)]),
            (slots.at[1, :, place], block.at[slot, pl.ds(size.at_keys, size.rows)]),
            (slots.at[2, :, place], block.at[slot, pl.ds(size.at_values, size.rows)]),
        )
        copies = [
            pltpu.make_async_copy(source, target, arrived.at[slot, index])
            for index, (source, target) in enumerate(ends)
        ]
        for copy in copies:
            copy.start()
        incoming.append(copies)
    held[...] = readout[:, cols(size.group() * size.width, size.width)]
    mixed = noise[...] + rate[0] * old[...]
    high = mixed.astype(BF16)
    low = (mixed - high.astype(F32)).astype(BF16)
    squares = jnp.sum(noise[...] * noise[...], axis=(0, 1), keepdims=True)
    near = squares.astype(BF16).astype(F32)
    far = (squares - near).astype(BF16).astype(F32)
    row = lax.broadcasted_iota(jnp.int32, (16, size.width), 0)
    three = jnp.where(row == 0, near, jnp.where(row == 1, far, squares - near - far))
    outgoing = []
    for slot in range(size.parts):
        pair = text[:, :, places[slot]].astype(F32)
        pair = jnp.concatenate([pair[:, 0], pair[:, 1]], axis=0)
        block[slot, size.at_text : size.at_mixed] = pair.astype(BF16)
        if size.folds:
            for fold in range(size.folds):
                part = slice(fold * size.per_fold, (fold + 1) * size.per_fold)
                lane = 2 * fold * size.rows
                block[slot, size.at_mixed : size.at_squares, lane : lane + size.rows] = high[part]
                lane = lane + size.rows
                block[slot, size.at_mixed : size.at_squares, lane : lane + size.rows] = low[part]
        else:
            middle = size.at_mixed + size.ch
            block[slot, size.at_mixed : middle, : size.rows] = high
            block[slot, middle : size.at_squares, : size.rows] = low
        block[slot, size.at_squares :] = three.astype(BF16)
        for copy in incoming[slot]:
            copy.wait()
        outgoing.append(pltpu.make_async_copy(block.at[slot], at(outs, slot), left.at[slot]))
        outgoing[-1].start()
    for copy in outgoing:
        copy.wait()


def pack(size, rate, slots, text, noise, old, readout):
    outs = pl.pallas_call(
        functools.partial(pack_kernel, size),
        in_specs=[SMEM, ANY]
        + [whole(x.shape) for x in (text, noise, old, readout)],
        out_specs=[ANY] * size.lists + [whole((size.ch, size.width))],
        out_shape=size.shapes(size.sent_rows)
        + [jax.ShapeDtypeStruct((size.ch, size.width), BF16)],
        scratch_shapes=[
            pltpu.VMEM((size.parts, size.sent_rows, size.width), BF16),
            pltpu.SemaphoreType.DMA((size.parts, 3)),
            pltpu.SemaphoreType.DMA((size.parts,)),
        ],
        grid=(1,),
        compiler_params=pltpu.CompilerParams(vmem_limit_bytes=60 * MIB),
        name="pack_tokens",
    )(rate, slots, text, noise, old, readout)
    return outs[:-1], outs[-1]


def text_rows(size, blocks, second):
    found = []
    for slot in range(size.parts):
        pair = at(blocks, slot)[size.at_text : size.at_text + 2 * size.txt].astype(F32)
        found.append(pair[size.txt :] if second else pair[: size.txt])
    return jnp.concatenate(found, axis=0).astype(BF16)


def gather_queries(size, blocks, queries):
    for slot in range(size.parts):
        queries[slot * size.sub : (slot + 1) * size.sub] = at(blocks, slot)[: size.sub]


def gather_keys(size, blocks, first, second, keys):
    for slot in range(size.parts):
        part = at(blocks, slot)[first : first + size.rows]
        keys[slot * size.rows : (slot + 1) * size.rows] = part
    keys[size.img_keys :] = text_rows(size, blocks, second)


def folded(x, combine):
    return combine(x.reshape(x.shape[0] // 8, 8, x.shape[1]), axis=0)


def forward_kernel(size, guidance, *refs):
    blocks = refs[: size.lists]
    readout, raised, each, inverse, out, scores, keys, values, queries = refs[size.lists :]
    step, head = pl.program_id(0), pl.program_id(1)
    gather_queries(size, blocks, queries)
    gather_keys(size, blocks, size.at_keys, False, keys)
    gather_keys(size, blocks, size.at_values, True, values)
    query = queries[pl.ds(pl.multiple_of(step * size.q_block, 128), size.q_block), :]
    peaks = []
    for lo, hi in size.tiles():
        tile = dot_nt(keys[lo:hi], query)
        scores[lo:hi] = tile
        peaks.append(folded(tile, jnp.max))
    top = jnp.max(functools.reduce(jnp.maximum, peaks), axis=0, keepdims=True)
    sums = []
    for lo, hi in size.tiles():
        tile = jnp.exp2((scores[lo:hi] - top) * EXP2_SCALE)
        sums.append(folded(tile, jnp.sum))
        raised[0, lo:hi] = tile.astype(BF16)
    inverted = 1.0 / jnp.sum(sum(sums[1:], sums[0]), axis=0, keepdims=True)
    held = readout[:, cols(head * HEAD_DIM, HEAD_DIM)]
    projected = dot_nt(held, values[...]).astype(BF16)
    velocity = dot(projected, raised[0]) * inverted
    each[0] = velocity
    inverse[0] = inverted
    part = velocity * branch_weight(guidance[0])

    @pl.when(head == 0)
    def _():
        out[...] = part

    @pl.when(head > 0)
    def _():
        out[...] += part


def forward(size, guidance, blocks, readout):
    return pl.pallas_call(
        functools.partial(forward_kernel, size),
        grid=(size.q_blocks, size.heads),
        in_specs=[SMEM]
        + size.head_specs(size.sent_rows, lambda b, h: h)
        + [whole(readout.shape)],
        out_specs=[
            pl.BlockSpec((1, size.keys, size.q_block), lambda b, h: (h, 0, b)),
            pl.BlockSpec((1, size.ch, size.q_block), lambda b, h: (h, 0, b)),
            pl.BlockSpec((1, 1, size.q_block), lambda b, h: (h, 0, b)),
            pl.BlockSpec((size.ch, size.q_block), lambda b, h: (0, b)),
        ],
        out_shape=[
            jax.ShapeDtypeStruct((size.heads, size.keys, size.queries), BF16),
            jax.ShapeDtypeStruct((size.heads, size.ch, size.queries), F32),
            jax.ShapeDtypeStruct((size.heads, 1, size.queries), F32),
            jax.ShapeDtypeStruct((size.ch, size.queries), F32),
        ],
        scratch_shapes=[
            pltpu.VMEM((size.keys, size.q_block), F32),
            pltpu.VMEM((size.keys, HEAD_DIM), BF16),
            pltpu.VMEM((size.keys, HEAD_DIM), BF16),
            pltpu.VMEM((size.queries, HEAD_DIM), BF16),
        ],
        compiler_params=size.params,
        name="attention_forward",
    )(guidance, *blocks, readout)


def surrogate_gain(ratio, advantage):
    clipped = jnp.clip(ratio, 0.8, 1.2)
    keep = ratio * advantage <= clipped * advantage
    return jnp.where(keep, -ratio * advantage, jnp.zeros_like(ratio))


def relative_reward(every, own):
    count = len(every)
    mean = sum(every[1:], every[0]) / count
    square = sum([x * x for x in every[1:]], every[0] * every[0]) / count
    spread = jnp.sqrt(jnp.maximum(square - mean * mean, 0.0))
    return (own - mean) / jnp.maximum(spread, 1.0)


def split_mixed(size, block):
    start = size.at_mixed
    if not size.folds:
        both = block[start : size.at_squares, : size.rows].astype(F32)
        return both[: size.ch] + both[size.ch :]
    found = []
    for fold in range(size.folds):
        lane = 2 * fold * size.rows
        near = block[start : size.at_squares, lane : lane + 2 * size.rows].astype(F32)
        found.append(near[:, : size.rows] + near[:, size.rows :])
    return jnp.concatenate(found, axis=0)


def split_squares(size, block):
    three = block[size.at_squares :, : size.rows].astype(F32)
    return three[:1, :1] + three[1:2, :1] + three[2:3, :1]


def velocity_grad(size, rate, guidance, stats, guided_parts, mixed, grad, ratio_out):
    rest = []
    for slot in range(size.parts):
        parts = []
        for apart in range(size.parts):
            other = slot ^ apart
            part = guided_parts[apart][:, other * size.sub : (other + 1) * size.sub]
            parts.append(part.astype(F32))
        rest.append(split_mixed(size, at(mixed, slot)) - rate[0] * tree_sum(parts))
    norm = tree_sum([jnp.sum(x * x, axis=(0, 1), keepdims=True) for x in rest])
    own = lax.axis_index("img")

    def spread(value):
        return jnp.full((1, 1), value, F32)

    every = [spread(stats[k]) for k in range(size.images)]
    advantage = relative_reward(every, spread(stats[own]))
    squares = tree_sum([split_squares(size, at(mixed, slot)) for slot in range(size.parts)])
    ratio = jnp.exp((squares - norm) * (0.5 / (size.queries * size.ch)))
    gain = surrogate_gain(ratio, advantage)
    factor = gain * (rate[0] * branch_weight(guidance[0]))
    for slot in range(size.parts):
        grad[:, slot * size.sub : (slot + 1) * size.sub] = rest[slot] * factor
    ratio_out[...] = ratio


def backward_kernel(size, *refs):
    if size.mirrored:
        rate, guidance, stats = refs[:3]
        guided_parts = refs[3 : 3 + size.parts]
        mixed = refs[3 + size.parts : 3 + size.parts + size.lists]
        refs = refs[3 + size.parts + size.lists :]
    else:
        given, refs = refs[0], refs[1:]
    blocks = refs[: size.lists]
    readout, raised, each, inverse, ratio_out, readout_out = refs[size.lists : size.lists + 6]
    outs = refs[size.lists + 6 : 2 * size.lists + 6]
    grad_ref, scores, keys, values, queries, grad_keys, grad_queries, small = refs[
        2 * size.lists + 6 :
    ]
    head, step = pl.program_id(0), pl.program_id(1)

    @pl.when((head == 0) & (step == 0))
    def _():
        if size.mirrored:
            velocity_grad(
                size, rate, guidance, stats, guided_parts, mixed, grad_ref, ratio_out
            )
        else:
            grad_ref[...] = given[...]
            ratio_out[...] = jnp.zeros(ratio_out.shape, F32)

    @pl.when(step == 0)
    def _():
        gather_queries(size, blocks, queries)
        gather_keys(size, blocks, size.at_keys, False, keys)
        gather_keys(size, blocks, size.at_values, True, values)

    first = pl.multiple_of(step * size.q_block, 128)
    held = readout[:, cols(head * HEAD_DIM, HEAD_DIM)]
    projected = dot_nt(values[...], held).astype(BF16)
    grad = (grad_ref[:, pl.ds(first, size.q_block)] * inverse[0]).astype(BF16)
    delta = jnp.sum(grad.astype(F32) * each[0], axis=0, keepdims=True)
    for lo, hi in size.tiles():
        tile = dot(projected[lo:hi], grad) - delta
        scores[lo:hi] = (raised[0, lo:hi].astype(F32) * tile).astype(BF16)
    key_part = dot(scores[...], queries[pl.ds(first, size.q_block), :]) * SCALE
    query_part = dot_tn(keys[...], scores[...]) * SCALE
    grad_queries[pl.ds(first, size.q_block), :] = query_part.T.astype(BF16)
    small_part = dot_nt(grad, raised[0])
    if size.q_blocks == 1:
        grad_keys[...] = key_part
        small[...] = small_part
    else:

        @pl.when(step == 0)
        def _():
            grad_keys[...] = key_part
            small[...] = small_part

        @pl.when(step > 0)
        def _():
            grad_keys[...] += key_part
            small[...] += small_part

    @pl.when(step == size.q_blocks - 1)
    def _():
        little = small[...].astype(BF16)
        readout_out[...] = dot(little, values[...])
        value_text = dot_tn(little[:, size.img_keys :], held)
        for slot in range(size.parts):
            out = at(outs, slot)
            near = slice(slot * size.rows, (slot + 1) * size.rows)
            out[: size.sub] = grad_queries[slot * size.sub : (slot + 1) * size.sub]
            out[size.sub : size.sub + size.rows] = grad_keys[near].astype(BF16)
            start = size.img_keys + slot * size.txt
            pair = [
                grad_keys[start : start + size.txt],
                value_text[slot * size.txt : (slot + 1) * size.txt],
            ]
            out[size.at_pair : size.at_small] = jnp.concatenate(pair, axis=0).astype(BF16)
            out[size.at_small :] = little[:, near]


def backward(size, given, blocks, readout, saved):
    if size.mirrored:
        rate, guidance, stats, guided = given
        first = [rate, guidance, stats] + guided + list(blocks)
        specs = [SMEM] * 3 + [whole(x.shape) for x in guided]
        mixed = pl.BlockSpec((1, size.sent_rows, size.width), lambda *_: (0, 0, 0))
        specs = specs + [mixed] * size.lists
    else:
        first, specs = [given], [whole(given.shape)]
    raised, each, inverse = saved
    outs = pl.pallas_call(
        functools.partial(backward_kernel, size),
        grid=(size.heads, size.q_blocks),
        in_specs=specs
        + size.head_specs(size.sent_rows, lambda h, b: h)
        + [
            whole(readout.shape),
            pl.BlockSpec((1, size.keys, size.q_block), lambda h, b: (h, 0, b)),
            pl.BlockSpec((1, size.ch, size.q_block), lambda h, b: (h, 0, b)),
            pl.BlockSpec((1, 1, size.q_block), lambda h, b: (h, 0, b)),
        ],
        out_specs=[whole((1, 1)), pl.BlockSpec((size.ch, HEAD_DIM), lambda h, b: (0, h))]
        + size.head_specs(size.home_rows, lambda h, b: h),
        out_shape=[
            jax.ShapeDtypeStruct((1, 1), F32),
            jax.ShapeDtypeStruct((size.ch, size.width), F32),
        ]
        + size.shapes(size.home_rows),
        scratch_shapes=[
            pltpu.VMEM((size.ch, size.queries), F32),
            pltpu.VMEM((size.keys, size.q_block), BF16),
            pltpu.VMEM((size.keys, HEAD_DIM), BF16),
            pltpu.VMEM((size.keys, HEAD_DIM), BF16),
            pltpu.VMEM((size.queries, HEAD_DIM), BF16),
            pltpu.VMEM((size.keys, HEAD_DIM), F32),
            pltpu.VMEM((size.queries, HEAD_DIM), BF16),
            pltpu.VMEM((size.ch, size.keys), F32),
        ],
        compiler_params=size.params,
        name="attention_backward",
    )(*first, *blocks, readout, raised, each, inverse)
    return outs[0], outs[1], outs[2:]


def home_kernel(size, readout, *refs):
    blocks = refs[: size.lists]
    out, text_out = refs[size.lists :]
    for group in range(size.groups):
        start = (size.base() ^ group) * size.width
        place = cols(start, size.width)
        held = [at(blocks, group * size.copies + copy) for copy in range(size.copies)]
        for copy in range(size.copies):
            out[0, copy * size.sub : (copy + 1) * size.sub, place] = held[copy][: size.sub]
        if size.copies == 1:
            rest = held[0][size.sub :]
        else:
            rest = sum([x[size.sub :].astype(F32) for x in held]).astype(BF16)
        out[1, :, place] = rest[: size.rows]
        pair = rest[size.rows : size.rows + 2 * size.txt].astype(F32)
        pair = jnp.stack([pair[: size.txt], pair[size.txt :]], axis=1)
        text_out[:, :, place] = pair.astype(BF16)
        for head in range(size.heads):
            near = cols(start + head * HEAD_DIM, HEAD_DIM)
            little = rest[size.rows + 2 * size.txt :, head * size.rows : (head + 1) * size.rows]
            out[2, :, near] = dot_tn(little, readout[:, near]).astype(BF16)


def home(size, readout, blocks):
    shapes = ((3, size.rows, size.features), (size.txt, 2, size.features))
    return pl.pallas_call(
        functools.partial(home_kernel, size),
        grid=(1,),
        in_specs=[whole(readout.shape)] + size.specs(size.home_rows),
        out_specs=[whole(x) for x in shapes],
        out_shape=[jax.ShapeDtypeStruct(x, BF16) for x in shapes],
        compiler_params=size.params,
        name="home_tokens",
    )(readout, *blocks)


def place_kernel(size, *refs):
    found, out = refs[:-1], refs[-1]
    for slot in range(size.parts):
        place = cols((size.base() ^ slot) * size.width, size.width)
        out[:, place] = found[slot][...].astype(F32)


def sum_readout(size, part):
    sent = (part + mirror(part, "cfg", 1)).astype(BF16)
    held = lax.all_gather(sent, "img", axis=0)
    total = tree_sum([held[k].astype(F32) for k in range(size.images)]).astype(BF16)
    found = [total] + [mirror(total, "seq", k) for k in range(1, size.parts)]
    return pl.pallas_call(
        functools.partial(place_kernel, size),
        grid=(1,),
        in_specs=[whole(x.shape) for x in found],
        out_specs=whole((size.ch, size.features)),
        out_shape=jax.ShapeDtypeStruct((size.ch, size.features), F32),
        compiler_params=size.params,
        name="place_readout_grad",
    )(*found)


def on_device(img_qkv, txt_kv, readout, old_velocity, noise, step_ratio, rewards, guidance):
    features, channels = readout.shape
    size = Sizes(img_qkv.shape[2], txt_kv.shape[2], features, channels)
    place = lax.axis_index("seq")
    own = lax.axis_index("img")
    slots = img_qkv[0, 0].transpose(1, 0, 2)
    wide = readout.T
    strength = guidance.reshape(1)
    extra = (noise[0].T, old_velocity[0].T, wide)
    packed, held = pack(size, step_ratio, slots, txt_kv[0, 0], *extra)
    blocks = exchange(size, packed)

    mine = jnp.arange(size.images) == own
    stats = lax.psum(jnp.where(mine, rewards[0], 0.0), "img")
    stats, blocks = lax.optimization_barrier((stats, blocks))

    *saved, part = forward(size, strength, blocks, held)
    summed = part + mirror(part, "cfg", 1)
    if size.mirrored:
        sent = summed.astype(BF16)
        guided = [sent] + [mirror(sent, "seq", k) for k in range(1, size.parts)]
        given = (step_ratio, strength, stats, guided)
    else:
        copy = place % size.copies
        rate = step_ratio[0]
        chosen = jnp.arange(size.copies).reshape(-1, 1, 1) == copy
        guided = lax.psum(jnp.where(chosen, summed[None], 0.0), "seq")
        guided = lax.dynamic_index_in_dim(guided, copy, 0, False)
        mixed = jax.vmap(lambda block: split_mixed(size, block))(blocks[0])
        near = lax.dynamic_slice_in_dim(mixed, copy * size.sub, size.sub, 2)
        near = near.transpose(1, 0, 2).reshape(channels, size.queries)
        left = near - rate * guided
        norm = lax.psum(jnp.sum(left * left), "seq") / size.groups
        squares = jnp.sum(jax.vmap(lambda block: split_squares(size, block))(blocks[0]))
        every = [stats[k] for k in range(size.images)]
        advantage = relative_reward(every, rewards[0])
        count = size.parts * size.rows * channels
        ratio = jnp.exp((squares - norm) * (0.5 / count))
        gain = surrogate_gain(ratio, advantage)
        given = left * (gain * (rate * branch_weight(guidance)))
    found, readout_part, sent = backward(size, given, blocks, held, saved)
    if size.mirrored:
        ratio = found
    homes = exchange(size, sent)
    if size.mirrored and lax.axis_size("cfg") == 2 and size.images in (1, 2, 4, 8):
        readout_grad = sum_readout(size, readout_part).T
    else:
        full = jnp.zeros((channels, features), F32)
        start = size.group() * size.width
        full = lax.dynamic_update_slice_in_dim(full, readout_part, start, 1)
        readout_grad = lax.psum(full, ("cfg", "img", "seq")).T
    token_grads, text_grads = home(size, wide, homes)
    img_grad = token_grads.transpose(1, 0, 2)[None, None]
    return (img_grad, text_grads[None, None], readout_grad, ratio.reshape(1))


def solution(mesh):
    return jax.shard_map(
        on_device,
        mesh=mesh,
        in_specs=(
            P("cfg", "img", "seq", None, None),
            P("cfg", "img", "seq", None, None),
            P(),
            P("img", "seq", None),
            P("img", "seq", None),
            P("img"),
            P("img"),
            P(),
        ),
        out_specs=(
            P("cfg", "img", "seq", None, None),
            P("cfg", "img", "seq", None, None),
            P(),
            P("img"),
        ),
        check_vma=False,
    )
```

```python
import functools
import math

import jax
import jax.numpy as jnp
from jax import lax
from jax.experimental import pallas as pl
from jax.experimental.pallas import tpu as pltpu
from jax.sharding import PartitionSpec as P

HEADS = 16
HEAD_DIM = 128
SCALE = HEAD_DIM ** (-0.5)
EXP2_SCALE = SCALE * math.log2(math.e)
F32 = jnp.float32
BF16 = jnp.bfloat16
MIB = 1024 * 1024
SMEM = pl.BlockSpec(memory_space=pltpu.SMEM)
ANY = pl.BlockSpec(memory_space=pl.ANY)


def dot(a, b):
    return jnp.dot(a, b, preferred_element_type=F32)


def dot_nt(a, b):
    return lax.dot_general(a, b, (((1,), (1,)), ((), ())), preferred_element_type=F32)


def dot_tn(a, b):
    return lax.dot_general(a, b, (((0,), (0,)), ((), ())), preferred_element_type=F32)


def whole(shape):
    return pl.BlockSpec(shape, lambda *_: (0,) * len(shape))


def at(refs, slot):
    return refs[slot].at[0] if len(refs) > 1 else refs[0].at[slot]


def cols(start, size):
    return pl.ds(pl.multiple_of(start, 128), size)


def tree_sum(terms):
    while len(terms) > 1:
        terms = [terms[k] + terms[k + 1] for k in range(0, len(terms), 2)]
    return terms[0]


def mirror(x, axis, apart):
    count = lax.axis_size(axis)
    return lax.ppermute(x, axis, [(i, i ^ apart) for i in range(count)])


class Sizes:
    def __init__(self, img_rows, txt_rows, features, channels):
        self.parts = lax.axis_size("seq")
        self.images = lax.axis_size("img")
        self.copies = max(1, self.parts // HEADS)
        self.groups = self.parts // self.copies
        self.features = features
        self.ch = channels
        self.width = features // self.groups
        self.heads = self.width // HEAD_DIM
        self.rows = img_rows
        self.txt = txt_rows
        self.sub = img_rows // self.copies
        self.img_keys = self.parts * img_rows
        self.keys = self.img_keys + self.parts * txt_rows
        self.queries = self.parts * self.sub
        self.mirrored = self.parts in (1, 2, 4, 8) and self.copies == 1
        self.lists = self.parts if self.mirrored else 1
        self.each = self.parts // self.lists
        self.at_keys = self.sub
        self.at_values = self.sub + self.rows
        self.at_text = self.sub + 2 * self.rows
        self.sent_rows = self.at_text + 2 * self.txt
        self.at_pair = self.sub + self.rows
        self.at_small = self.at_pair + 2 * self.txt
        self.home_rows = self.at_small + self.ch
        block = self.queries
        while block % 256 == 0 and self.keys * block > 600_000:
            block //= 2
        self.q_block = block
        self.q_blocks = self.queries // block
        limit = (16 if self.mirrored else 48) * MIB
        self.late = 1 if self.mirrored and self.heads > 1 else 0
        self.params = pltpu.CompilerParams(vmem_limit_bytes=limit)

    def tiles(self):
        edges = list(range(0, self.img_keys, self.rows)) + [self.img_keys, self.keys]
        return list(zip(edges[:-1], edges[1:]))

    def shapes(self, rows, width):
        shape = (self.each, rows, width)
        return [jax.ShapeDtypeStruct(shape, BF16) for _ in range(self.lists)]

    def specs(self, rows, width):
        return [whole((self.each, rows, width)) for _ in range(self.lists)]

    def home_widths(self):
        widths = [(self.heads - self.late) * HEAD_DIM]
        return widths + [self.late * HEAD_DIM] * (self.late > 0)

    def head_specs(self, rows, index):
        return [
            pl.BlockSpec((self.each, rows, HEAD_DIM), lambda *g: (0, 0, index(*g)))
            for _ in range(self.lists)
        ]

    def base(self):
        place = lax.axis_index("seq")
        return place if self.mirrored else jnp.zeros_like(place)

    def group(self):
        return lax.axis_index("seq") // self.copies


def spread(size, blocks):
    found = [mirror(blocks[k], "seq", k) for k in reversed(range(1, size.parts))]
    return [blocks[0]] + found[::-1]


def exchange(size, blocks):
    if size.mirrored:
        return spread(size, blocks)
    return [lax.all_to_all(blocks[0], "seq", split_axis=0, concat_axis=0, tiled=True)]


def branch_weight(guidance):
    return jnp.where(lax.axis_index("cfg") == 0, guidance, 1.0 - guidance)


def pack_kernel(size, slots, text, *refs):
    outs = refs[: size.lists]
    words, block, arrived, left, read = refs[size.lists :]
    incoming = []
    places = []
    for slot in reversed(range(size.parts)):
        dest = size.base() ^ slot
        place = cols((dest // size.copies) * size.width, size.width)
        places.append(place)
        if size.copies == 1:
            queries = slots.at[0, :, place]
        else:
            first = pl.multiple_of((dest % size.copies) * size.sub, 16)
            queries = slots.at[0, pl.ds(first, size.sub), place]
        ends = (
            (queries, block.at[slot, pl.ds(0, size.sub)]),
            (slots.at[1, :, place], block.at[slot, pl.ds(size.at_keys, size.rows)]),
            (slots.at[2, :, place], block.at[slot, pl.ds(size.at_values, size.rows)]),
        )
        copies = [
            pltpu.make_async_copy(source, target, arrived.at[slot, index])
            for index, (source, target) in enumerate(ends)
        ]
        if not incoming:
            fetch = pltpu.make_async_copy(text, words, read)
            fetch.start()
        for copy in copies:
            copy.start()
        incoming.append(copies)
    fetch.wait()
    outgoing = []
    for slot, place, copies in zip(reversed(range(size.parts)), places, incoming):
        pair = words[:, :, place].astype(F32)
        pair = jnp.concatenate([pair[:, 0], pair[:, 1]], axis=0)
        block[slot, size.at_text :] = pair.astype(BF16)
        for copy in copies:
            copy.wait()
        outgoing.append(pltpu.make_async_copy(block.at[slot], at(outs, slot), left.at[slot]))
        outgoing[-1].start()
    for copy in outgoing:
        copy.wait()


def pack(size, slots, text):
    return pl.pallas_call(
        functools.partial(pack_kernel, size),
        in_specs=[ANY, ANY],
        out_specs=[ANY] * size.lists,
        out_shape=size.shapes(size.sent_rows, size.width),
        scratch_shapes=[
            pltpu.VMEM(text.shape, BF16),
            pltpu.VMEM((size.parts, size.sent_rows, size.width), BF16),
            pltpu.SemaphoreType.DMA((size.parts, 3)),
            pltpu.SemaphoreType.DMA((size.parts,)),
            pltpu.SemaphoreType.DMA,
        ],
        compiler_params=pltpu.CompilerParams(vmem_limit_bytes=60 * MIB),
        name="pack_tokens",
    )(slots, text)


def text_rows(size, blocks, second):
    found = []
    for slot in range(size.parts):
        pair = at(blocks, slot)[size.at_text : size.at_text + 2 * size.txt].astype(F32)
        found.append(pair[size.txt :] if second else pair[: size.txt])
    return jnp.concatenate(found, axis=0).astype(BF16)


def gather_queries(size, blocks, queries):
    for slot in range(size.parts):
        queries[slot * size.sub : (slot + 1) * size.sub] = at(blocks, slot)[: size.sub]


def gather_keys(size, blocks, first, second, keys):
    for slot in range(size.parts):
        part = at(blocks, slot)[first : first + size.rows]
        keys[slot * size.rows : (slot + 1) * size.rows] = part
    keys[size.img_keys :] = text_rows(size, blocks, second)


def folded(x, combine):
    return combine(x.reshape(x.shape[0] // 8, 8, x.shape[1]), axis=0)


def forward_kernel(size, guidance, *refs):
    blocks = refs[: size.lists]
    readout, raised, each, inverse, out, scores, keys, values, queries = refs[size.lists :]
    step, head = pl.program_id(0), pl.program_id(1)
    gather_queries(size, blocks, queries)
    gather_keys(size, blocks, size.at_keys, False, keys)
    gather_keys(size, blocks, size.at_values, True, values)
    query = queries[pl.ds(pl.multiple_of(step * size.q_block, 128), size.q_block), :]
    peaks = []
    for lo, hi in size.tiles():
        tile = dot_nt(keys[lo:hi], query)
        scores[lo:hi] = tile
        peaks.append(folded(tile, jnp.max))
    top = jnp.max(functools.reduce(jnp.maximum, peaks), axis=0, keepdims=True)
    sums = []
    for lo, hi in size.tiles():
        tile = jnp.exp2((scores[lo:hi] - top) * EXP2_SCALE)
        sums.append(folded(tile, jnp.sum))
        raised[0, lo:hi] = tile.astype(BF16)
    inverted = 1.0 / jnp.sum(sum(sums[1:], sums[0]), axis=0, keepdims=True)
    held = readout[:, cols(size.group() * size.width + head * HEAD_DIM, HEAD_DIM)]
    projected = dot_nt(held, values[...]).astype(BF16)
    velocity = dot(projected, raised[0]) * inverted
    each[0] = velocity
    inverse[0] = inverted
    part = velocity * branch_weight(guidance[0])

    @pl.when(head == 0)
    def _():
        out[...] = part

    @pl.when(head > 0)
    def _():
        out[...] += part


def forward(size, guidance, blocks, readout):
    return pl.pallas_call(
        functools.partial(forward_kernel, size),
        grid=(size.q_blocks, size.heads),
        in_specs=[SMEM]
        + size.head_specs(size.sent_rows, lambda b, h: h)
        + [whole(readout.shape)],
        out_specs=[
            pl.BlockSpec((1, size.keys, size.q_block), lambda b, h: (h, 0, b)),
            pl.BlockSpec((1, size.ch, size.q_block), lambda b, h: (h, 0, b)),
            pl.BlockSpec((1, 1, size.q_block), lambda b, h: (h, 0, b)),
            pl.BlockSpec((size.ch, size.q_block), lambda b, h: (0, b)),
        ],
        out_shape=[
            jax.ShapeDtypeStruct((size.heads, size.keys, size.queries), BF16),
            jax.ShapeDtypeStruct((size.heads, size.ch, size.queries), F32),
            jax.ShapeDtypeStruct((size.heads, 1, size.queries), F32),
            jax.ShapeDtypeStruct((size.ch, size.queries), F32),
        ],
        scratch_shapes=[
            pltpu.VMEM((size.keys, size.q_block), F32),
            pltpu.VMEM((size.keys, HEAD_DIM), BF16),
            pltpu.VMEM((size.keys, HEAD_DIM), BF16),
            pltpu.VMEM((size.queries, HEAD_DIM), BF16),
        ],
        compiler_params=size.params,
        name="attention_forward",
    )(guidance, *blocks, readout)


def surrogate_gain(ratio, advantage):
    clipped = jnp.clip(ratio, 0.8, 1.2)
    keep = ratio * advantage <= clipped * advantage
    return jnp.where(keep, -ratio * advantage, jnp.zeros_like(ratio))


def relative_reward(every, own):
    count = len(every)
    mean = sum(every[1:], every[0]) / count
    square = sum([x * x for x in every[1:]], every[0] * every[0]) / count
    spread = jnp.sqrt(jnp.maximum(square - mean * mean, 0.0))
    return (own - mean) / jnp.maximum(spread, 1.0)


def combine_kernel(size, rate, part, other, noise, old, out):
    out[:, : size.queries] = (part[...] + other[...]).astype(BF16)
    own = part[:, : size.sub] + other[:, : size.sub]
    own = own - (old[...] + noise[...] * (1.0 / rate[0]))
    high = own.astype(BF16)
    low = own - high.astype(F32)
    squares = jnp.sum(noise[...] * noise[...], axis=(0, 1), keepdims=True)
    near = squares.astype(BF16).astype(F32)
    far = (squares - near).astype(BF16).astype(F32)
    for index, value in enumerate((near, far, squares - near - far)):
        low = jnp.where(is_place(low.shape, index), value, low)
    out[:, : size.sub] = high
    out[:, size.queries :] = low.astype(BF16)


def is_place(shape, index):
    row = lax.broadcasted_iota(jnp.int32, shape, 0)
    lane = lax.broadcasted_iota(jnp.int32, shape, 1)
    return (row == 0) & (lane == index)


def combine(size, rate, part, other, noise, old):
    arrays = (part, other, noise, old)
    shape = (size.ch, size.queries + size.sub)
    return pl.pallas_call(
        functools.partial(combine_kernel, size),
        grid=(1,),
        in_specs=[SMEM] + [whole(x.shape) for x in arrays],
        out_specs=whole(shape),
        out_shape=jax.ShapeDtypeStruct(shape, BF16),
        compiler_params=size.params,
        name="combine_branches",
    )(rate, *arrays)


def velocity_grad(size, rate, guidance, stats, gathered, grad, ratio_out):
    rest, squares = [], []
    for slot in range(size.parts):
        parts = []
        for apart in range(size.parts):
            other = slot ^ apart
            part = gathered[apart][:, other * size.sub : (other + 1) * size.sub].astype(F32)
            if apart == slot:
                low = gathered[apart][:, size.queries :].astype(F32)
                squares.append(low[:1, :1] + low[:1, 1:2] + low[:1, 2:3])
                for index in range(3):
                    low = jnp.where(is_place(low.shape, index), 0.0, low)
                part = part + low
            parts.append(part)
        rest.append(tree_sum(parts) * -rate[0])
    norm = tree_sum([jnp.sum(x * x, axis=(0, 1), keepdims=True) for x in rest])
    own = lax.axis_index("img")
    every = [jnp.full((1, 1), stats[k], F32) for k in range(size.images)]
    advantage = relative_reward(every, jnp.full((1, 1), stats[own], F32))
    ratio = jnp.exp((tree_sum(squares) - norm) * (0.5 / (size.queries * size.ch)))
    gain = surrogate_gain(ratio, advantage)
    factor = gain * (rate[0] * branch_weight(guidance[0]))
    for slot in range(size.parts):
        grad[:, slot * size.sub : (slot + 1) * size.sub] = rest[slot] * factor
    ratio_out[...] = ratio


def backward_kernel(size, *refs):
    if size.mirrored:
        rate, guidance, stats = refs[:3]
        gathered = refs[3 : 3 + size.parts]
        refs = refs[3 + size.parts :]
    else:
        given, refs = refs[0], refs[1:]
    blocks = refs[: size.lists]
    readout, raised, each, inverse, ratio_out, readout_out = refs[size.lists : size.lists + 6]
    refs = refs[size.lists + 6 :]
    outs, refs = refs[: size.lists], refs[size.lists :]
    if size.late:
        late_outs, refs = refs[: size.lists], refs[size.lists :]
    grad_ref, scores, keys, values, queries, grad_keys, grad_queries, small = refs
    head, step = pl.program_id(0), pl.program_id(1)

    @pl.when((head == 0) & (step == 0))
    def _():
        if size.mirrored:
            velocity_grad(size, rate, guidance, stats, gathered, grad_ref, ratio_out)
        else:
            grad_ref[...] = given[...]
            ratio_out[...] = jnp.zeros(ratio_out.shape, F32)

    @pl.when(step == 0)
    def _():
        gather_queries(size, blocks, queries)
        gather_keys(size, blocks, size.at_keys, False, keys)
        gather_keys(size, blocks, size.at_values, True, values)

    first = pl.multiple_of(step * size.q_block, 128)
    held = readout[:, cols(size.group() * size.width + head * HEAD_DIM, HEAD_DIM)]
    projected = dot_nt(values[...], held).astype(BF16)
    grad = (grad_ref[:, pl.ds(first, size.q_block)] * inverse[0]).astype(BF16)
    delta = jnp.sum(grad.astype(F32) * each[0], axis=0, keepdims=True)
    for lo, hi in size.tiles():
        tile = dot(projected[lo:hi], grad) - delta
        scores[lo:hi] = (raised[0, lo:hi].astype(F32) * tile).astype(BF16)
    key_part = dot(scores[...], queries[pl.ds(first, size.q_block), :]) * SCALE
    query_part = dot_tn(keys[...], scores[...]) * SCALE
    grad_queries[pl.ds(first, size.q_block), :] = query_part.T.astype(BF16)
    small_part = dot_nt(grad, raised[0])
    if size.q_blocks == 1:
        grad_keys[...] = key_part
        small[...] = small_part
    else:

        @pl.when(step == 0)
        def _():
            grad_keys[...] = key_part
            small[...] = small_part

        @pl.when(step > 0)
        def _():
            grad_keys[...] += key_part
            small[...] += small_part

    @pl.when(step == size.q_blocks - 1)
    def _():
        little = small[...].astype(BF16)
        readout_out[...] = dot(little, values[...])
        value_text = dot_tn(little[:, size.img_keys :], held)

        def write(targets):
            for slot in range(size.parts):
                out = at(targets, slot)
                near = slice(slot * size.rows, (slot + 1) * size.rows)
                out[: size.sub] = grad_queries[slot * size.sub : (slot + 1) * size.sub]
                out[size.sub : size.sub + size.rows] = grad_keys[near].astype(BF16)
                start = size.img_keys + slot * size.txt
                pair = [
                    grad_keys[start : start + size.txt],
                    value_text[slot * size.txt : (slot + 1) * size.txt],
                ]
                out[size.at_pair : size.at_small] = jnp.concatenate(pair, axis=0).astype(BF16)
                out[size.at_small :] = little[:, near]

        if size.late:
            early = size.heads - size.late

            @pl.when(head < early)
            def _():
                write(outs)

            @pl.when(head >= early)
            def _():
                write(late_outs)

        else:
            write(outs)


def backward(size, given, blocks, readout, saved):
    if size.mirrored:
        rate, guidance, stats, gathered = given
        first = [rate, guidance, stats] + gathered
        specs = [SMEM] * 3 + [whole(x.shape) for x in gathered]
    else:
        first, specs = [given], [whole(given.shape)]
    raised, each, inverse = saved
    early = size.heads - size.late
    home_specs = size.head_specs(size.home_rows, lambda h, b: jnp.minimum(h, early - 1))
    if size.late:
        home_specs += size.head_specs(size.home_rows, lambda h, b: jnp.maximum(h - early, 0))
    outs = pl.pallas_call(
        functools.partial(backward_kernel, size),
        grid=(size.heads, size.q_blocks),
        in_specs=specs
        + size.head_specs(size.sent_rows, lambda h, b: h)
        + [
            whole(readout.shape),
            pl.BlockSpec((1, size.keys, size.q_block), lambda h, b: (h, 0, b)),
            pl.BlockSpec((1, size.ch, size.q_block), lambda h, b: (h, 0, b)),
            pl.BlockSpec((1, 1, size.q_block), lambda h, b: (h, 0, b)),
        ],
        out_specs=[whole((1, 1)), pl.BlockSpec((size.ch, HEAD_DIM), lambda h, b: (0, h))]
        + home_specs,
        out_shape=[
            jax.ShapeDtypeStruct((1, 1), F32),
            jax.ShapeDtypeStruct((size.ch, size.width), F32),
        ]
        + [x for width in size.home_widths() for x in size.shapes(size.home_rows, width)],
        scratch_shapes=[
            pltpu.VMEM((size.ch, size.queries), F32),
            pltpu.VMEM((size.keys, size.q_block), BF16),
            pltpu.VMEM((size.keys, HEAD_DIM), BF16),
            pltpu.VMEM((size.keys, HEAD_DIM), BF16),
            pltpu.VMEM((size.queries, HEAD_DIM), BF16),
            pltpu.VMEM((size.keys, HEAD_DIM), F32),
            pltpu.VMEM((size.queries, HEAD_DIM), BF16),
            pltpu.VMEM((size.ch, size.keys), F32),
        ],
        compiler_params=size.params,
        name="attention_backward",
    )(*first, *blocks, readout, raised, each, inverse)
    sent = outs[2:]
    return outs[0], outs[1], [sent[k : k + size.lists] for k in range(0, len(sent), size.lists)]


def home_kernel(size, readout, *refs):
    out, text_out = refs[-2:]
    offset = 0
    for index, width in enumerate(size.home_widths()):
        blocks = refs[index * size.lists : (index + 1) * size.lists]
        for group in range(size.groups):
            start = (size.base() ^ group) * size.width + offset
            place = cols(start, width)
            held = [at(blocks, group * size.copies + copy) for copy in range(size.copies)]
            for copy in range(size.copies):
                out[0, copy * size.sub : (copy + 1) * size.sub, place] = held[copy][: size.sub]
            if size.copies == 1:
                rest = held[0][size.sub :]
            else:
                rest = sum([x[size.sub :].astype(F32) for x in held]).astype(BF16)
            out[1, :, place] = rest[: size.rows]
            pair = rest[size.rows : size.rows + 2 * size.txt].astype(F32)
            pair = jnp.stack([pair[: size.txt], pair[size.txt :]], axis=1)
            text_out[:, :, place] = pair.astype(BF16)
            for head in range(width // HEAD_DIM):
                near = cols(start + head * HEAD_DIM, HEAD_DIM)
                lanes = slice(head * size.rows, (head + 1) * size.rows)
                little = rest[size.rows + 2 * size.txt :, lanes]
                out[2, :, near] = dot_tn(little, readout[:, near]).astype(BF16)
        offset += width


def home(size, readout, homes):
    shapes = ((3, size.rows, size.features), (size.txt, 2, size.features))
    specs = [x for width in size.home_widths() for x in size.specs(size.home_rows, width)]
    return pl.pallas_call(
        functools.partial(home_kernel, size),
        grid=(1,),
        in_specs=[whole(readout.shape)] + specs,
        out_specs=[whole(x) for x in shapes],
        out_shape=[jax.ShapeDtypeStruct(x, BF16) for x in shapes],
        compiler_params=size.params,
        name="home_tokens",
    )(readout, *[x for blocks in homes for x in blocks])


def place_kernel(size, *refs):
    found, out = refs[:-1], refs[-1]
    for slot in range(size.parts):
        place = cols((size.base() ^ slot) * size.width, size.width)
        out[:, place] = found[slot][...].astype(F32)


def sum_readout(size, part):
    sent = (part + mirror(part, "cfg", 1)).astype(BF16)
    held = lax.all_gather(sent, "img", axis=0)
    return tree_sum([held[k].astype(F32) for k in range(size.images)]).astype(BF16)


def place_readout(size, found):
    return pl.pallas_call(
        functools.partial(place_kernel, size),
        grid=(1,),
        in_specs=[whole(x.shape) for x in found],
        out_specs=whole((size.ch, size.features)),
        out_shape=jax.ShapeDtypeStruct((size.ch, size.features), F32),
        compiler_params=size.params,
        name="place_readout_grad",
    )(*found)


def on_device(img_qkv, txt_kv, readout, old_velocity, noise, step_ratio, rewards, guidance):
    features, channels = readout.shape
    size = Sizes(img_qkv.shape[2], txt_kv.shape[2], features, channels)
    place = lax.axis_index("seq")
    own = lax.axis_index("img")
    slots = img_qkv[0, 0].transpose(1, 0, 2)
    wide = readout.T
    strength = guidance.reshape(1)
    noise_wide, old_wide = noise[0].T, old_velocity[0].T
    blocks = exchange(size, pack(size, slots, txt_kv[0, 0]))

    mine = jnp.arange(size.images) == own
    stats = lax.psum(jnp.where(mine, rewards[0], 0.0), "img")
    stats, blocks = lax.optimization_barrier((stats, blocks))

    *saved, part = forward(size, strength, blocks, wide)
    other = mirror(part, "cfg", 1)
    if size.mirrored:
        sent = combine(size, step_ratio, part, other, noise_wide, old_wide)
        gathered = spread(size, [sent] * size.parts)
        given = (step_ratio, strength, stats, gathered)
    else:
        copy = place % size.copies
        rate = step_ratio[0]
        chosen = jnp.arange(size.copies).reshape(-1, 1, 1) == copy
        guided = lax.psum(jnp.where(chosen, (part + other)[None], 0.0), "seq")
        guided = lax.dynamic_index_in_dim(guided, copy, 0, False)
        mixed = lax.all_gather(noise_wide + rate * old_wide, "seq", axis=0)
        near = lax.dynamic_slice_in_dim(mixed, copy * size.sub, size.sub, 2)
        near = near.transpose(1, 0, 2).reshape(channels, size.queries)
        left = near - rate * guided
        norm = lax.psum(jnp.sum(left * left), "seq") / size.groups
        squares = lax.psum(jnp.sum(noise * noise), "seq")
        every = [stats[k] for k in range(size.images)]
        advantage = relative_reward(every, rewards[0])
        count = size.parts * size.rows * channels
        ratio = jnp.exp((squares - norm) * (0.5 / count))
        gain = surrogate_gain(ratio, advantage)
        given = left * (gain * (rate * branch_weight(guidance)))
    found, readout_part, sent = backward(size, given, blocks, wide, saved)
    if size.mirrored:
        ratio = found
    if size.mirrored and lax.axis_size("cfg") == 2 and size.images in (1, 2, 4, 8):
        homes = [exchange(size, sent[0])]
        total = sum_readout(size, readout_part)
        if size.late:
            total, late = lax.optimization_barrier((total, sent[1]))
        every = spread(size, [total] * size.parts)
        if size.late:
            homes.append(exchange(size, late))
        token_grads, text_grads = home(size, wide, homes)
        token_grads, every = lax.optimization_barrier((token_grads, every))
        readout_grad = place_readout(size, every).T
    else:
        homes = [exchange(size, x) for x in sent]
        token_grads, text_grads = home(size, wide, homes)
        full = jnp.zeros((channels, features), F32)
        start = size.group() * size.width
        full = lax.dynamic_update_slice_in_dim(full, readout_part, start, 1)
        readout_grad = lax.psum(full, ("cfg", "img", "seq")).T
    img_grad = token_grads.transpose(1, 0, 2)[None, None]
    return (img_grad, text_grads[None, None], readout_grad, ratio.reshape(1))


def solution(mesh):
    return jax.shard_map(
        on_device,
        mesh=mesh,
        in_specs=(
            P("cfg", "img", "seq", None, None),
            P("cfg", "img", "seq", None, None),
            P(),
            P("img", "seq", None),
            P("img", "seq", None),
            P("img"),
            P("img"),
            P(),
        ),
        out_specs=(
            P("cfg", "img", "seq", None, None),
            P("cfg", "img", "seq", None, None),
            P(),
            P("img"),
        ),
        check_vma=False,
    )
```

```python
import functools
import math

import jax
import jax.numpy as jnp
from jax import lax
from jax.experimental import pallas as pl
from jax.experimental.pallas import tpu as pltpu
from jax.sharding import PartitionSpec as P

HEADS = 16
HEAD_DIM = 128
SCALE = HEAD_DIM ** (-0.5)
EXP2_SCALE = SCALE * math.log2(math.e)
F32 = jnp.float32
BF16 = jnp.bfloat16
MIB = 1024 * 1024
SMEM = pl.BlockSpec(memory_space=pltpu.SMEM)
ANY = pl.BlockSpec(memory_space=pl.ANY)


def dot(a, b):
    return jnp.dot(a, b, preferred_element_type=F32)


def dot_nt(a, b):
    return lax.dot_general(a, b, (((1,), (1,)), ((), ())), preferred_element_type=F32)


def dot_tn(a, b):
    return lax.dot_general(a, b, (((0,), (0,)), ((), ())), preferred_element_type=F32)


def whole(shape):
    return pl.BlockSpec(shape, lambda *_: (0,) * len(shape))


def at(refs, slot):
    return refs[slot].at[0] if len(refs) > 1 else refs[0].at[slot]


def cols(start, size):
    return pl.ds(pl.multiple_of(start, 128), size)


def tree_sum(terms):
    while len(terms) > 1:
        terms = [terms[k] + terms[k + 1] for k in range(0, len(terms), 2)]
    return terms[0]


def mirror(x, axis, apart):
    count = lax.axis_size(axis)
    return lax.ppermute(x, axis, [(i, i ^ apart) for i in range(count)])


class Sizes:
    def __init__(self, img_rows, txt_rows, features, channels):
        self.parts = lax.axis_size("seq")
        self.images = lax.axis_size("img")
        self.copies = max(1, self.parts // HEADS)
        self.groups = self.parts // self.copies
        self.features = features
        self.ch = channels
        self.width = features // self.groups
        self.heads = self.width // HEAD_DIM
        self.rows = img_rows
        self.txt = txt_rows
        self.sub = img_rows // self.copies
        self.img_keys = self.parts * img_rows
        self.keys = self.img_keys + self.parts * txt_rows
        self.queries = self.parts * self.sub
        power = self.images & (self.images - 1) == 0
        self.mirrored = self.parts in (2, 4, 8) and self.copies == 1
        self.mirrored = self.mirrored and self.heads > 1 and power and lax.axis_size("cfg") == 2
        self.lists = self.parts if self.mirrored else 1
        self.each = self.parts // self.lists
        self.at_keys = self.sub
        self.at_values = self.sub + self.rows
        self.at_text = self.sub + 2 * self.rows
        self.sent_rows = self.at_text + 2 * self.txt
        self.at_pair = self.sub + self.rows
        self.at_small = self.at_pair + 2 * self.txt
        self.home_rows = self.at_small + self.ch
        block = self.queries
        while block % 256 == 0 and self.keys * block > 600_000:
            block //= 2
        self.q_block = block
        self.q_blocks = self.queries // block
        limit = (16 if self.mirrored else 48) * MIB
        self.halves = 2 if self.mirrored else 1
        self.late = 1 if self.mirrored else 0
        self.params = pltpu.CompilerParams(vmem_limit_bytes=limit)

    def tiles(self):
        edges = list(range(0, self.img_keys, self.rows)) + [self.img_keys, self.keys]
        return list(zip(edges[:-1], edges[1:]))

    def shapes(self, rows, width):
        shape = (self.each, rows, width)
        return [jax.ShapeDtypeStruct(shape, BF16) for _ in range(self.lists)]

    def specs(self, rows, width):
        return [whole((self.each, rows, width)) for _ in range(self.lists)]

    def home_widths(self):
        widths = [(self.heads - self.late) * HEAD_DIM]
        return widths + [self.late * HEAD_DIM] * (self.late > 0)

    def head_specs(self, rows, index):
        return [
            pl.BlockSpec((self.each, rows, HEAD_DIM), lambda *g: (0, 0, index(*g)))
            for _ in range(self.lists)
        ]

    def base(self):
        place = lax.axis_index("seq")
        return place if self.mirrored else jnp.zeros_like(place)

    def group(self):
        return lax.axis_index("seq") // self.copies


def spread(size, blocks):
    found = [mirror(blocks[k], "seq", k) for k in reversed(range(1, size.parts))]
    return [blocks[0]] + found[::-1]


def exchange(size, blocks):
    if size.mirrored:
        return spread(size, blocks)
    return [lax.all_to_all(blocks[0], "seq", split_axis=0, concat_axis=0, tiled=True)]


def branch_weight(guidance):
    return jnp.where(lax.axis_index("cfg") == 0, guidance, 1.0 - guidance)


def pack_kernel(size, which, slots, text, *refs):
    count = len(which) if size.mirrored else 1
    outs = refs[:count]
    words, block, arrived, left, read = refs[count:]
    incoming = []
    places = []
    for spot, slot in enumerate(which):
        dest = size.base() ^ slot
        place = cols((dest // size.copies) * size.width, size.width)
        places.append(place)
        if size.copies == 1:
            queries = slots.at[0, :, place]
        else:
            first = pl.multiple_of((dest % size.copies) * size.sub, 16)
            queries = slots.at[0, pl.ds(first, size.sub), place]
        ends = (
            (queries, block.at[spot, pl.ds(0, size.sub)]),
            (slots.at[1, :, place], block.at[spot, pl.ds(size.at_keys, size.rows)]),
            (slots.at[2, :, place], block.at[spot, pl.ds(size.at_values, size.rows)]),
        )
        copies = [
            pltpu.make_async_copy(source, target, arrived.at[spot, index])
            for index, (source, target) in enumerate(ends)
        ]
        if not incoming:
            fetch = pltpu.make_async_copy(text, words, read)
            fetch.start()
        for copy in copies:
            copy.start()
        incoming.append(copies)
    fetch.wait()
    outgoing = []
    for spot, (place, copies) in enumerate(zip(places, incoming)):
        pair = words[:, :, place].astype(F32)
        pair = jnp.concatenate([pair[:, 0], pair[:, 1]], axis=0)
        block[spot, size.at_text :] = pair.astype(BF16)
        for copy in copies:
            copy.wait()
        out = outs[spot].at[0] if size.mirrored else outs[0].at[spot]
        outgoing.append(pltpu.make_async_copy(block.at[spot], out, left.at[spot]))
        outgoing[-1].start()
    for copy in outgoing:
        copy.wait()


def pack(size, slots, text, which, limit):
    count = len(which)
    shapes = size.shapes(size.sent_rows, size.width)[: count if size.mirrored else 1]
    return pl.pallas_call(
        functools.partial(pack_kernel, size, which),
        in_specs=[ANY, ANY],
        out_specs=[ANY] * len(shapes),
        out_shape=shapes,
        scratch_shapes=[
            pltpu.VMEM(text.shape, BF16),
            pltpu.VMEM((count, size.sent_rows, size.width), BF16),
            pltpu.SemaphoreType.DMA((count, 3)),
            pltpu.SemaphoreType.DMA((count,)),
            pltpu.SemaphoreType.DMA,
        ],
        compiler_params=pltpu.CompilerParams(vmem_limit_bytes=limit),
        name="pack_tokens",
    )(slots, text)


def text_rows(size, blocks, second):
    found = []
    for slot in range(size.parts):
        pair = at(blocks, slot)[size.at_text : size.at_text + 2 * size.txt].astype(F32)
        found.append(pair[size.txt :] if second else pair[: size.txt])
    return jnp.concatenate(found, axis=0).astype(BF16)


def gather_queries(size, blocks, queries):
    for slot in range(size.parts):
        queries[slot * size.sub : (slot + 1) * size.sub] = at(blocks, slot)[: size.sub]


def gather_keys(size, blocks, first, second, keys):
    for slot in range(size.parts):
        part = at(blocks, slot)[first : first + size.rows]
        keys[slot * size.rows : (slot + 1) * size.rows] = part
    keys[size.img_keys :] = text_rows(size, blocks, second)


def folded(x, combine):
    return combine(x.reshape(x.shape[0] // 8, 8, x.shape[1]), axis=0)


def forward_kernel(size, guidance, *refs):
    blocks = refs[: size.lists]
    readout, raised, each, inverse = refs[size.lists : size.lists + 4]
    outs = refs[size.lists + 4 : size.lists + 4 + size.halves]
    total, scores, keys, values, queries = refs[size.lists + 4 + size.halves :]
    step, head = pl.program_id(0), pl.program_id(1)
    gather_queries(size, blocks, queries)
    gather_keys(size, blocks, size.at_keys, False, keys)
    gather_keys(size, blocks, size.at_values, True, values)
    query = queries[pl.ds(pl.multiple_of(step * size.q_block, 128), size.q_block), :]
    peaks = []
    for lo, hi in size.tiles():
        tile = dot_nt(keys[lo:hi], query)
        scores[lo:hi] = tile
        peaks.append(folded(tile, jnp.max))
    top = jnp.max(functools.reduce(jnp.maximum, peaks), axis=0, keepdims=True)
    sums = []
    for lo, hi in size.tiles():
        tile = jnp.exp2((scores[lo:hi] - top) * EXP2_SCALE)
        sums.append(folded(tile, jnp.sum))
        raised[0, lo:hi] = tile.astype(BF16)
    inverted = 1.0 / jnp.sum(sum(sums[1:], sums[0]), axis=0, keepdims=True)
    held = readout[:, cols(size.group() * size.width + head * HEAD_DIM, HEAD_DIM)]
    projected = dot_nt(held, values[...]).astype(BF16)
    velocity = dot(projected, raised[0]) * inverted
    each[0] = velocity
    inverse[0] = inverted
    part = velocity * branch_weight(guidance[0])

    @pl.when(head == 0)
    def _():
        total[...] = part

    @pl.when(head > 0)
    def _():
        total[...] += part

    @pl.when(head == size.heads - 1)
    def _():
        for half, out in enumerate(outs):
            out[...] = total[half_rows(size, half)]


def half_rows(size, half):
    per = size.ch // size.halves
    if size.halves == 1:
        return pl.ds(0, per)
    return pl.ds(pl.multiple_of((lax.axis_index("cfg") ^ half) * per, per), per)


def forward(size, guidance, blocks, readout):
    return pl.pallas_call(
        functools.partial(forward_kernel, size),
        grid=(size.q_blocks, size.heads),
        in_specs=[SMEM]
        + size.head_specs(size.sent_rows, lambda b, h: h)
        + [whole(readout.shape)],
        out_specs=[
            pl.BlockSpec((1, size.keys, size.q_block), lambda b, h: (h, 0, b)),
            pl.BlockSpec((1, size.ch, size.q_block), lambda b, h: (h, 0, b)),
            pl.BlockSpec((1, 1, size.q_block), lambda b, h: (h, 0, b)),
        ]
        + [pl.BlockSpec((size.ch // size.halves, size.q_block), lambda b, h: (0, b))]
        * size.halves,
        out_shape=[
            jax.ShapeDtypeStruct((size.heads, size.keys, size.queries), BF16),
            jax.ShapeDtypeStruct((size.heads, size.ch, size.queries), F32),
            jax.ShapeDtypeStruct((size.heads, 1, size.queries), F32),
        ]
        + [jax.ShapeDtypeStruct((size.ch // size.halves, size.queries), F32)] * size.halves,
        scratch_shapes=[
            pltpu.VMEM((size.ch, size.q_block), F32),
            pltpu.VMEM((size.keys, size.q_block), F32),
            pltpu.VMEM((size.keys, HEAD_DIM), BF16),
            pltpu.VMEM((size.keys, HEAD_DIM), BF16),
            pltpu.VMEM((size.queries, HEAD_DIM), BF16),
        ],
        compiler_params=size.params,
        name="attention_forward",
    )(guidance, *blocks, readout)


def surrogate_gain(ratio, advantage):
    clipped = jnp.clip(ratio, 0.8, 1.2)
    keep = ratio * advantage <= clipped * advantage
    return jnp.where(keep, -ratio * advantage, jnp.zeros_like(ratio))


def relative_reward(every, own):
    count = len(every)
    mean = sum(every[1:], every[0]) / count
    square = sum([x * x for x in every[1:]], every[0] * every[0]) / count
    spread = jnp.sqrt(jnp.maximum(square - mean * mean, 0.0))
    return (own - mean) / jnp.maximum(spread, 1.0)


def combine_kernel(size, rate, part, other, noise, old, out):
    rows = half_rows(size, 0)
    out[:, : size.queries] = (part[...] + other[...]).astype(BF16)
    own = part[:, : size.sub] + other[:, : size.sub]
    own = own - (old[rows] + noise[rows] * (1.0 / rate[0]))
    high = own.astype(BF16)
    low = own - high.astype(F32)
    squares = jnp.sum(noise[rows] * noise[rows], axis=(0, 1), keepdims=True)
    near = squares.astype(BF16).astype(F32)
    far = (squares - near).astype(BF16).astype(F32)
    for index, value in enumerate((near, far, squares - near - far)):
        low = jnp.where(is_place(low.shape, index), value, low)
    out[:, : size.sub] = high
    out[:, size.queries :] = low.astype(BF16)


def is_place(shape, index):
    row = lax.broadcasted_iota(jnp.int32, shape, 0)
    lane = lax.broadcasted_iota(jnp.int32, shape, 1)
    return (row == 0) & (lane == index)


def combine(size, rate, part, other, noise, old):
    arrays = (part, other, noise, old)
    shape = (size.ch // size.halves, size.queries + size.sub)
    return pl.pallas_call(
        functools.partial(combine_kernel, size),
        grid=(1,),
        in_specs=[SMEM] + [whole(x.shape) for x in arrays],
        out_specs=whole(shape),
        out_shape=jax.ShapeDtypeStruct(shape, BF16),
        compiler_params=size.params,
        name="combine_branches",
    )(rate, *arrays)


def gather_guided_kernel(size, *refs):
    gathered, out = refs[:-1], refs[-1]
    per = size.ch // size.halves
    squares, norms = [], []
    for slot in range(size.parts):
        parts = []
        for apart in range(size.parts):
            other = slot ^ apart
            part = gathered[apart][:, other * size.sub : (other + 1) * size.sub].astype(F32)
            if apart == slot:
                low = gathered[apart][:, size.queries :].astype(F32)
                squares.append(low[:1, :1] + low[:1, 1:2] + low[:1, 2:3])
                for index in range(3):
                    low = jnp.where(is_place(low.shape, index), 0.0, low)
                part = part + low
            parts.append(part)
        left = tree_sum(parts)
        norms.append(jnp.sum(left * left, axis=(0, 1), keepdims=True))
        out[:per, slot * size.sub : (slot + 1) * size.sub] = left
    row = lax.broadcasted_iota(jnp.int32, (8, size.queries), 0)
    out[per:] = jnp.where(row == 0, tree_sum(squares), tree_sum(norms))


def gather_guided(size, gathered):
    shape = (size.ch // size.halves + 8, size.queries)
    return pl.pallas_call(
        functools.partial(gather_guided_kernel, size),
        grid=(1,),
        in_specs=[whole(x.shape) for x in gathered],
        out_specs=whole(shape),
        out_shape=jax.ShapeDtypeStruct(shape, F32),
        compiler_params=size.params,
        name="gather_guided",
    )(*gathered)


def velocity_grad(size, rate, guidance, stats, moved, grad, ratio_out):
    per = size.ch // size.halves
    norm = tree_sum([x[per + 1 : per + 2, :1] for x in moved])
    squares = tree_sum([x[per : per + 1, :1] for x in moved])
    own = lax.axis_index("img")
    every = [jnp.full((1, 1), stats[k], F32) for k in range(size.images)]
    advantage = relative_reward(every, jnp.full((1, 1), stats[own], F32))
    exponent = (squares - norm * (rate[0] * rate[0])) * (0.5 / (size.queries * size.ch))
    ratio = jnp.exp(exponent)
    gain = surrogate_gain(ratio, advantage)
    factor = gain * (-rate[0] * rate[0] * branch_weight(guidance[0]))
    for half, x in enumerate(moved):
        grad[half_rows(size, half)] = x[:per] * factor
    ratio_out[...] = ratio


def backward_kernel(size, *refs):
    if size.mirrored:
        rate, guidance, stats = refs[:3]
        moved = refs[3 : 3 + size.halves]
        refs = refs[3 + size.halves :]
    else:
        given, refs = refs[0], refs[1:]
    blocks = refs[: size.lists]
    readout, raised, each, inverse, ratio_out, readout_out = refs[size.lists : size.lists + 6]
    refs = refs[size.lists + 6 :]
    outs, refs = refs[: size.lists], refs[size.lists :]
    if size.late:
        late_outs, refs = refs[: size.lists], refs[size.lists :]
    grad_ref, scores, keys, values, queries, grad_keys, grad_queries, small = refs
    head, step = pl.program_id(0), pl.program_id(1)

    @pl.when((head == 0) & (step == 0))
    def _():
        if size.mirrored:
            velocity_grad(size, rate, guidance, stats, moved, grad_ref, ratio_out)
        else:
            grad_ref[...] = given[...]
            ratio_out[...] = jnp.zeros(ratio_out.shape, F32)

    @pl.when(step == 0)
    def _():
        gather_queries(size, blocks, queries)
        gather_keys(size, blocks, size.at_keys, False, keys)
        gather_keys(size, blocks, size.at_values, True, values)

    first = pl.multiple_of(step * size.q_block, 128)
    held = readout[:, cols(size.group() * size.width + head * HEAD_DIM, HEAD_DIM)]
    projected = dot_nt(values[...], held).astype(BF16)
    grad = (grad_ref[:, pl.ds(first, size.q_block)] * inverse[0]).astype(BF16)
    delta = jnp.sum(grad.astype(F32) * each[0], axis=0, keepdims=True)
    for lo, hi in size.tiles():
        tile = dot(projected[lo:hi], grad) - delta
        scores[lo:hi] = (raised[0, lo:hi].astype(F32) * tile).astype(BF16)
    key_part = dot(scores[...], queries[pl.ds(first, size.q_block), :]) * SCALE
    query_part = dot_tn(keys[...], scores[...]) * SCALE
    grad_queries[pl.ds(first, size.q_block), :] = query_part.T.astype(BF16)
    small_part = dot_nt(grad, raised[0])
    if size.q_blocks == 1:
        grad_keys[...] = key_part
        small[...] = small_part
    else:

        @pl.when(step == 0)
        def _():
            grad_keys[...] = key_part
            small[...] = small_part

        @pl.when(step > 0)
        def _():
            grad_keys[...] += key_part
            small[...] += small_part

    @pl.when(step == size.q_blocks - 1)
    def _():
        little = small[...].astype(BF16)
        readout_out[...] = dot(little, values[...])
        value_text = dot_tn(little[:, size.img_keys :], held)

        def write(targets):
            for slot in range(size.parts):
                out = at(targets, slot)
                near = slice(slot * size.rows, (slot + 1) * size.rows)
                out[: size.sub] = grad_queries[slot * size.sub : (slot + 1) * size.sub]
                out[size.sub : size.sub + size.rows] = grad_keys[near].astype(BF16)
                start = size.img_keys + slot * size.txt
                pair = [
                    grad_keys[start : start + size.txt],
                    value_text[slot * size.txt : (slot + 1) * size.txt],
                ]
                out[size.at_pair : size.at_small] = jnp.concatenate(pair, axis=0).astype(BF16)
                out[size.at_small :] = little[:, near]

        if size.late:
            early = size.heads - size.late

            @pl.when(head < early)
            def _():
                write(outs)

            @pl.when(head >= early)
            def _():
                write(late_outs)

        else:
            write(outs)


def backward(size, given, blocks, readout, saved):
    if size.mirrored:
        rate, guidance, stats, moved = given
        first = [rate, guidance, stats] + moved
        specs = [SMEM] * 3 + [whole(x.shape) for x in moved]
    else:
        first, specs = [given], [whole(given.shape)]
    raised, each, inverse = saved
    early = size.heads - size.late
    home_specs = size.head_specs(size.home_rows, lambda h, b: jnp.minimum(h, early - 1))
    if size.late:
        home_specs += size.head_specs(size.home_rows, lambda h, b: jnp.maximum(h - early, 0))
    outs = pl.pallas_call(
        functools.partial(backward_kernel, size),
        grid=(size.heads, size.q_blocks),
        in_specs=specs
        + size.head_specs(size.sent_rows, lambda h, b: h)
        + [
            whole(readout.shape),
            pl.BlockSpec((1, size.keys, size.q_block), lambda h, b: (h, 0, b)),
            pl.BlockSpec((1, size.ch, size.q_block), lambda h, b: (h, 0, b)),
            pl.BlockSpec((1, 1, size.q_block), lambda h, b: (h, 0, b)),
        ],
        out_specs=[whole((1, 1)), pl.BlockSpec((size.ch, HEAD_DIM), lambda h, b: (0, h))]
        + home_specs,
        out_shape=[
            jax.ShapeDtypeStruct((1, 1), F32),
            jax.ShapeDtypeStruct((size.ch, size.width), F32),
        ]
        + [x for width in size.home_widths() for x in size.shapes(size.home_rows, width)],
        scratch_shapes=[
            pltpu.VMEM((size.ch, size.queries), F32),
            pltpu.VMEM((size.keys, size.q_block), BF16),
            pltpu.VMEM((size.keys, HEAD_DIM), BF16),
            pltpu.VMEM((size.keys, HEAD_DIM), BF16),
            pltpu.VMEM((size.queries, HEAD_DIM), BF16),
            pltpu.VMEM((size.keys, HEAD_DIM), F32),
            pltpu.VMEM((size.queries, HEAD_DIM), BF16),
            pltpu.VMEM((size.ch, size.keys), F32),
        ],
        compiler_params=size.params,
        name="attention_backward",
    )(*first, *blocks, readout, raised, each, inverse)
    sent = outs[2:]
    return outs[0], outs[1], [sent[k : k + size.lists] for k in range(0, len(sent), size.lists)]


def home_kernel(size, readout, *refs):
    out, text_out = refs[-2:]
    offset = 0
    for index, width in enumerate(size.home_widths()):
        blocks = refs[index * size.lists : (index + 1) * size.lists]
        for group in range(size.groups):
            start = (size.base() ^ group) * size.width + offset
            place = cols(start, width)
            held = [at(blocks, group * size.copies + copy) for copy in range(size.copies)]
            for copy in range(size.copies):
                out[0, copy * size.sub : (copy + 1) * size.sub, place] = held[copy][: size.sub]
            if size.copies == 1:
                rest = held[0][size.sub : size.home_rows]
            else:
                rest = sum([x[size.sub :].astype(F32) for x in held]).astype(BF16)
            out[1, :, place] = rest[: size.rows]
            pair = rest[size.rows : size.rows + 2 * size.txt].astype(F32)
            pair = jnp.stack([pair[: size.txt], pair[size.txt :]], axis=1)
            text_out[:, :, place] = pair.astype(BF16)
            for head in range(width // HEAD_DIM):
                near = cols(start + head * HEAD_DIM, HEAD_DIM)
                lanes = slice(head * size.rows, (head + 1) * size.rows)
                little = rest[size.rows + 2 * size.txt :, lanes]
                out[2, :, near] = dot_tn(little, readout[:, near]).astype(BF16)
        offset += width


def home(size, readout, homes):
    shapes = [(3, size.rows, size.features), (size.txt, 2, size.features)]
    outs = [jax.ShapeDtypeStruct(x, BF16) for x in shapes]
    specs = [whole(x.shape) for blocks in homes for x in blocks]
    return pl.pallas_call(
        functools.partial(home_kernel, size),
        grid=(1,),
        in_specs=[whole(readout.shape)] + specs,
        out_specs=[whole(x.shape) for x in outs],
        out_shape=outs,
        compiler_params=size.params,
        name="home_tokens",
    )(readout, *[x for blocks in homes for x in blocks])


def join_readout_kernel(size, held, *refs):
    blocks, outs = refs[: size.parts], refs[size.parts :]
    rows = half_rows(size, 0)
    per = size.ch // size.halves
    total = tree_sum([held[k, rows].astype(F32) for k in range(size.images)]).astype(BF16)
    for block, out in zip(blocks, outs):
        out[0, : size.home_rows] = block[0]
        for head in range(size.heads):
            first = size.home_rows + head * per
            out[0, first : first + per] = total[:, head * HEAD_DIM : (head + 1) * HEAD_DIM]


def join_readout(size, part, blocks):
    sent = (part + mirror(part, "cfg", 1)).astype(BF16)
    held = lax.all_gather(sent, "img", axis=0)
    shape = (1, size.home_rows + size.heads * size.ch // size.halves, HEAD_DIM)
    return pl.pallas_call(
        functools.partial(join_readout_kernel, size),
        grid=(1,),
        in_specs=[whole(held.shape)] + [whole(x.shape) for x in blocks],
        out_specs=[whole(shape)] * size.parts,
        out_shape=[jax.ShapeDtypeStruct(shape, BF16)] * size.parts,
        compiler_params=size.params,
        name="join_readout_grad",
    )(held, *blocks)


def place_kernel(size, *refs):
    out = refs[-1]
    per = size.ch // size.halves
    for half in range(size.halves):
        for slot in range(size.parts):
            found = refs[half * size.parts + slot]
            for head in range(size.heads):
                lanes = cols((size.base() ^ slot) * size.width + head * HEAD_DIM, HEAD_DIM)
                first = size.home_rows + head * per
                out[half_rows(size, half), lanes] = found[0, first : first + per].astype(F32)


def place_readout(size, found):
    return pl.pallas_call(
        functools.partial(place_kernel, size),
        grid=(1,),
        in_specs=[whole(x.shape) for x in found],
        out_specs=whole((size.ch, size.features)),
        out_shape=jax.ShapeDtypeStruct((size.ch, size.features), F32),
        compiler_params=size.params,
        name="place_readout_grad",
    )(*found)


def on_device(img_qkv, txt_kv, readout, old_velocity, noise, step_ratio, rewards, guidance):
    features, channels = readout.shape
    size = Sizes(img_qkv.shape[2], txt_kv.shape[2], features, channels)
    place = lax.axis_index("seq")
    own = lax.axis_index("img")
    slots = img_qkv[0, 0].transpose(1, 0, 2)
    wide = readout.T
    strength = guidance.reshape(1)
    noise_wide, old_wide = noise[0].T, old_velocity[0].T
    text = txt_kv[0, 0]
    if size.mirrored:
        away = list(range(1, size.parts))
        sent = pack(size, slots, text, away, 60 * MIB)
        blocks = [mirror(block, "seq", k) for k, block in zip(away, sent)]
    else:
        blocks = exchange(size, pack(size, slots, text, list(range(size.parts)), 48 * MIB))

    mine = jnp.arange(size.images) == own
    stats = lax.psum(jnp.where(mine, rewards[0], 0.0), "img")
    if size.mirrored:
        stats, near, words = lax.optimization_barrier((stats, slots, text))
        blocks = list(pack(size, near, words, [0], 16 * MIB)) + blocks
        blocks = lax.optimization_barrier(blocks)

    *saved, part = forward(size, strength, blocks, wide)
    if size.mirrored:
        saved, kept, part = saved[:3], saved[3], part
        other = mirror(part, "cfg", 1)
        sent = combine(size, step_ratio, kept, other, noise_wide, old_wide)
        guided = gather_guided(size, spread(size, [sent] * size.parts))
        given = (step_ratio, strength, stats, [guided, mirror(guided, "cfg", 1)])
    else:
        other = mirror(part, "cfg", 1)
        copy = place % size.copies
        rate = step_ratio[0]
        chosen = jnp.arange(size.copies).reshape(-1, 1, 1) == copy
        guided = lax.psum(jnp.where(chosen, (part + other)[None], 0.0), "seq")
        guided = lax.dynamic_index_in_dim(guided, copy, 0, False)
        mixed = lax.all_gather(noise_wide + rate * old_wide, "seq", axis=0)
        near = lax.dynamic_slice_in_dim(mixed, copy * size.sub, size.sub, 2)
        near = near.transpose(1, 0, 2).reshape(channels, size.queries)
        left = near - rate * guided
        norm = lax.psum(jnp.sum(left * left), "seq") / size.groups
        squares = lax.psum(jnp.sum(noise * noise), "seq")
        every = [stats[k] for k in range(size.images)]
        advantage = relative_reward(every, rewards[0])
        count = size.parts * size.rows * channels
        ratio = jnp.exp((squares - norm) * (0.5 / count))
        gain = surrogate_gain(ratio, advantage)
        given = left * (gain * (rate * branch_weight(guidance)))
    found, readout_part, sent = backward(size, given, blocks, wide, saved)
    if size.mirrored:
        ratio = found
    if size.late:
        homes = [exchange(size, sent[0])]
        homes.append(exchange(size, join_readout(size, readout_part, sent[1])))
        joined = homes[1]
        found = joined + [mirror(x, "cfg", 1) for x in joined]
        token_grads, text_grads = home(size, wide, homes)
        token_grads, found = lax.optimization_barrier((token_grads, found))
        readout_grad = place_readout(size, found).T
    else:
        homes = [exchange(size, x) for x in sent]
        token_grads, text_grads = home(size, wide, homes)
        full = jnp.zeros((channels, features), F32)
        start = size.group() * size.width
        full = lax.dynamic_update_slice_in_dim(full, readout_part, start, 1)
        readout_grad = lax.psum(full, ("cfg", "img", "seq")).T
    img_grad = token_grads.transpose(1, 0, 2)[None, None]
    return (img_grad, text_grads[None, None], readout_grad, ratio.reshape(1))


def solution(mesh):
    return jax.shard_map(
        on_device,
        mesh=mesh,
        in_specs=(
            P("cfg", "img", "seq", None, None),
            P("cfg", "img", "seq", None, None),
            P(),
            P("img", "seq", None),
            P("img", "seq", None),
            P("img"),
            P("img"),
            P(),
        ),
        out_specs=(
            P("cfg", "img", "seq", None, None),
            P("cfg", "img", "seq", None, None),
            P(),
            P("img"),
        ),
        check_vma=False,
    )
```

```python
import functools
import math

import jax
import jax.numpy as jnp
from jax import lax
from jax.experimental import pallas as pl
from jax.experimental.pallas import tpu as pltpu
from jax.sharding import PartitionSpec as P

HEADS = 16
HEAD_DIM = 128
SCALE = HEAD_DIM ** (-0.5)
EXP2_SCALE = SCALE * math.log2(math.e)
F32 = jnp.float32
BF16 = jnp.bfloat16
MIB = 1024 * 1024
SMEM = pl.BlockSpec(memory_space=pltpu.SMEM)
ANY = pl.BlockSpec(memory_space=pl.ANY)


def dot(a, b):
    return jnp.dot(a, b, preferred_element_type=F32)


def dot_nt(a, b):
    return lax.dot_general(a, b, (((1,), (1,)), ((), ())), preferred_element_type=F32)


def dot_tn(a, b):
    return lax.dot_general(a, b, (((0,), (0,)), ((), ())), preferred_element_type=F32)


def whole(shape):
    return pl.BlockSpec(shape, lambda *_: (0,) * len(shape))


def at(refs, slot):
    return refs[slot].at[0] if len(refs) > 1 else refs[0].at[slot]


def cols(start, size):
    return pl.ds(pl.multiple_of(start, 128), size)


def tree_sum(terms):
    while len(terms) > 1:
        terms = [terms[k] + terms[k + 1] for k in range(0, len(terms), 2)]
    return terms[0]


def mirror(x, axis, apart):
    count = lax.axis_size(axis)
    return lax.ppermute(x, axis, [(i, i ^ apart) for i in range(count)])


class Sizes:
    def __init__(self, img_rows, txt_rows, features, channels):
        self.parts = lax.axis_size("seq")
        self.images = lax.axis_size("img")
        self.copies = max(1, self.parts // HEADS)
        self.groups = self.parts // self.copies
        self.features = features
        self.ch = channels
        self.width = features // self.groups
        self.heads = self.width // HEAD_DIM
        self.rows = img_rows
        self.txt = txt_rows
        self.sub = img_rows // self.copies
        self.img_keys = self.parts * img_rows
        self.keys = self.img_keys + self.parts * txt_rows
        self.queries = self.parts * self.sub
        power = self.images & (self.images - 1) == 0
        self.mirrored = self.parts in (2, 4, 8) and self.copies == 1
        self.mirrored = self.mirrored and self.heads > 1 and power and lax.axis_size("cfg") == 2
        self.lists = self.parts if self.mirrored else 1
        self.each = self.parts // self.lists
        self.at_keys = self.sub
        self.at_values = self.sub + self.rows
        self.at_text = self.sub + 2 * self.rows
        self.sent_rows = self.at_text + 2 * self.txt
        self.at_pair = self.sub + self.rows
        self.at_small = self.at_pair + 2 * self.txt
        self.home_rows = self.at_small + self.ch
        block = self.queries
        while block % 256 == 0 and self.keys * block > 600_000:
            block //= 2
        self.q_block = block
        self.q_blocks = self.queries // block
        limit = (16 if self.mirrored else 48) * MIB
        self.halves = 2 if self.mirrored else 1
        self.late = 1 if self.mirrored else 0
        self.params = pltpu.CompilerParams(vmem_limit_bytes=limit)

    def tiles(self):
        edges = list(range(0, self.img_keys, self.rows)) + [self.img_keys, self.keys]
        return list(zip(edges[:-1], edges[1:]))

    def shapes(self, rows, width):
        shape = (self.each, rows, width)
        return [jax.ShapeDtypeStruct(shape, BF16) for _ in range(self.lists)]

    def specs(self, rows, width):
        return [whole((self.each, rows, width)) for _ in range(self.lists)]

    def home_widths(self):
        widths = [(self.heads - self.late) * HEAD_DIM]
        return widths + [self.late * HEAD_DIM] * (self.late > 0)

    def grid(self):
        return {} if self.mirrored else {"grid": (self.q_blocks,)}

    def full(self, shape):
        return pl.BlockSpec(memory_space=pltpu.VMEM) if self.mirrored else whole(shape)

    def by_queries(self, *lead):
        if self.mirrored:
            return pl.BlockSpec(memory_space=pltpu.VMEM)
        return pl.BlockSpec(lead + (self.q_block,), lambda b: (0,) * len(lead) + (b,))

    def base(self):
        place = lax.axis_index("seq")
        return place if self.mirrored else jnp.zeros_like(place)

    def group(self):
        return lax.axis_index("seq") // self.copies


def spread(size, blocks):
    found = [mirror(blocks[k], "seq", k) for k in reversed(range(1, size.parts))]
    return [blocks[0]] + found[::-1]


def exchange(size, blocks):
    if size.mirrored:
        return spread(size, blocks)
    return [lax.all_to_all(blocks[0], "seq", split_axis=0, concat_axis=0, tiled=True)]


def branch_weight(guidance):
    return jnp.where(lax.axis_index("cfg") == 0, guidance, 1.0 - guidance)


def pack_kernel(size, which, slots, text, *refs):
    count = len(which) if size.mirrored else 1
    outs = refs[:count]
    words, block, arrived, left, read = refs[count:]
    incoming = []
    places = []
    for spot, slot in enumerate(which):
        dest = size.base() ^ slot
        place = cols((dest // size.copies) * size.width, size.width)
        places.append(place)
        if size.copies == 1:
            queries = slots.at[0, :, place]
        else:
            first = pl.multiple_of((dest % size.copies) * size.sub, 16)
            queries = slots.at[0, pl.ds(first, size.sub), place]
        ends = (
            (queries, block.at[spot, pl.ds(0, size.sub)]),
            (slots.at[1, :, place], block.at[spot, pl.ds(size.at_keys, size.rows)]),
            (slots.at[2, :, place], block.at[spot, pl.ds(size.at_values, size.rows)]),
        )
        copies = [
            pltpu.make_async_copy(source, target, arrived.at[spot, index])
            for index, (source, target) in enumerate(ends)
        ]
        if not incoming:
            fetch = pltpu.make_async_copy(text, words, read)
            fetch.start()
        for copy in copies:
            copy.start()
        incoming.append(copies)
    fetch.wait()
    outgoing = []
    for spot, (place, copies) in enumerate(zip(places, incoming)):
        pair = words[:, :, place].astype(F32)
        pair = jnp.concatenate([pair[:, 0], pair[:, 1]], axis=0)
        block[spot, size.at_text :] = pair.astype(BF16)
        for copy in copies:
            copy.wait()
        out = outs[spot].at[0] if size.mirrored else outs[0].at[spot]
        outgoing.append(pltpu.make_async_copy(block.at[spot], out, left.at[spot]))
        outgoing[-1].start()
    for copy in outgoing:
        copy.wait()


def pack(size, slots, text, which, limit):
    count = len(which)
    shapes = size.shapes(size.sent_rows, size.width)[: count if size.mirrored else 1]
    return pl.pallas_call(
        functools.partial(pack_kernel, size, which),
        in_specs=[ANY, ANY],
        out_specs=[ANY] * len(shapes),
        out_shape=shapes,
        scratch_shapes=[
            pltpu.VMEM(text.shape, BF16),
            pltpu.VMEM((count, size.sent_rows, size.width), BF16),
            pltpu.SemaphoreType.DMA((count, 3)),
            pltpu.SemaphoreType.DMA((count,)),
            pltpu.SemaphoreType.DMA,
        ],
        compiler_params=pltpu.CompilerParams(vmem_limit_bytes=limit),
        name="pack_tokens",
    )(slots, text)


def lanes_of(head):
    return slice(head * HEAD_DIM, (head + 1) * HEAD_DIM)


def text_rows(size, blocks, head, second):
    found = []
    for slot in range(size.parts):
        block = at(blocks, slot)
        pair = block[size.at_text : size.at_text + 2 * size.txt, lanes_of(head)].astype(F32)
        found.append(pair[size.txt :] if second else pair[: size.txt])
    return jnp.concatenate(found, axis=0).astype(BF16)


def rows_of(size, blocks, head, first, count):
    return [at(blocks, slot)[first : first + count, lanes_of(head)] for slot in range(size.parts)]


def keys_of(size, blocks, head):
    found = rows_of(size, blocks, head, size.at_keys, size.rows)
    return found + [text_rows(size, blocks, head, False)]


def values_of(size, blocks, head):
    found = rows_of(size, blocks, head, size.at_values, size.rows)
    return found + [text_rows(size, blocks, head, True)]


def queries_of(size, blocks, head, step):
    if size.q_blocks == 1:
        return jnp.concatenate(rows_of(size, blocks, head, 0, size.sub), axis=0)
    count = size.q_block // size.sub
    found = [
        blocks[0][step * count + k, : size.sub, lanes_of(head)] for k in range(count)
    ]
    return jnp.concatenate(found, axis=0)


def folded(x, combine):
    return combine(x.reshape(x.shape[0] // 8, 8, x.shape[1]), axis=0)


def forward_kernel(size, guidance, *refs):
    blocks = refs[: size.lists]
    readout, raised, each, inverse = refs[size.lists : size.lists + 4]
    outs = refs[size.lists + 4 : size.lists + 4 + size.halves]
    total, scores = refs[size.lists + 4 + size.halves :]
    step = 0 if size.mirrored else pl.program_id(0)
    weight = branch_weight(guidance[0])
    velocities = []
    for head in range(size.heads):
        query = queries_of(size, blocks, head, step)
        peaks = []
        for (lo, hi), key in zip(size.tiles(), keys_of(size, blocks, head)):
            tile = dot_nt(key, query)
            scores[head, lo:hi] = tile
            peaks.append(folded(tile, jnp.max))
        top = jnp.max(functools.reduce(jnp.maximum, peaks), axis=0, keepdims=True)
        sums = []
        for lo, hi in size.tiles():
            tile = jnp.exp2((scores[head, lo:hi] - top) * EXP2_SCALE)
            sums.append(folded(tile, jnp.sum))
            raised[head, lo:hi] = tile.astype(BF16)
        inverted = 1.0 / jnp.sum(sum(sums[1:], sums[0]), axis=0, keepdims=True)
        held = readout[:, cols(size.group() * size.width + head * HEAD_DIM, HEAD_DIM)]
        projected = [dot_nt(held, value) for value in values_of(size, blocks, head)]
        projected = jnp.concatenate(projected, axis=1).astype(BF16)
        velocity = dot(projected, raised[head]) * inverted
        each[head] = velocity
        inverse[head] = inverted
        velocities.append(velocity)
    total[...] = sum(velocities[1:], velocities[0]) * weight
    for half, out in enumerate(outs):
        out[...] = total[half_rows(size, half)]


def half_rows(size, half):
    per = size.ch // size.halves
    if size.halves == 1:
        return pl.ds(0, per)
    return pl.ds(pl.multiple_of((lax.axis_index("cfg") ^ half) * per, per), per)


def forward(size, guidance, blocks, readout):
    per = size.ch // size.halves
    return pl.pallas_call(
        functools.partial(forward_kernel, size),
        in_specs=[SMEM] + [size.full(x.shape) for x in blocks] + [size.full(readout.shape)],
        out_specs=[
            size.by_queries(size.heads, size.keys),
            size.by_queries(size.heads, size.ch),
            size.by_queries(size.heads, 1),
        ]
        + [size.by_queries(per)] * size.halves,
        out_shape=[
            jax.ShapeDtypeStruct((size.heads, size.keys, size.queries), BF16),
            jax.ShapeDtypeStruct((size.heads, size.ch, size.queries), F32),
            jax.ShapeDtypeStruct((size.heads, 1, size.queries), F32),
        ]
        + [jax.ShapeDtypeStruct((per, size.queries), F32)] * size.halves,
        scratch_shapes=[
            pltpu.VMEM((size.ch, size.q_block), F32),
            pltpu.VMEM((size.heads, size.keys, size.q_block), F32),
        ],
        compiler_params=size.params,
        name="attention_forward",
        **size.grid(),
    )(guidance, *blocks, readout)


def surrogate_gain(ratio, advantage):
    clipped = jnp.clip(ratio, 0.8, 1.2)
    keep = ratio * advantage <= clipped * advantage
    return jnp.where(keep, -ratio * advantage, jnp.zeros_like(ratio))


def relative_reward(every, own):
    count = len(every)
    mean = sum(every[1:], every[0]) / count
    square = sum([x * x for x in every[1:]], every[0] * every[0]) / count
    spread = jnp.sqrt(jnp.maximum(square - mean * mean, 0.0))
    return (own - mean) / jnp.maximum(spread, 1.0)


def combine_kernel(size, rate, part, other, noise, old, out):
    rows = half_rows(size, 0)
    out[:, : size.queries] = (part[...] + other[...]).astype(BF16)
    own = part[:, : size.sub] + other[:, : size.sub]
    own = own - (old[rows] + noise[rows] * (1.0 / rate[0]))
    high = own.astype(BF16)
    low = own - high.astype(F32)
    squares = jnp.sum(noise[rows] * noise[rows], axis=(0, 1), keepdims=True)
    near = squares.astype(BF16).astype(F32)
    far = (squares - near).astype(BF16).astype(F32)
    for index, value in enumerate((near, far, squares - near - far)):
        low = jnp.where(is_place(low.shape, index), value, low)
    out[:, : size.sub] = high
    out[:, size.queries :] = low.astype(BF16)


def is_place(shape, index):
    row = lax.broadcasted_iota(jnp.int32, shape, 0)
    lane = lax.broadcasted_iota(jnp.int32, shape, 1)
    return (row == 0) & (lane == index)


def combine(size, rate, part, other, noise, old):
    arrays = (part, other, noise, old)
    shape = (size.ch // size.halves, size.queries + size.sub)
    return pl.pallas_call(
        functools.partial(combine_kernel, size),
        grid=(1,),
        in_specs=[SMEM] + [whole(x.shape) for x in arrays],
        out_specs=whole(shape),
        out_shape=jax.ShapeDtypeStruct(shape, BF16),
        compiler_params=size.params,
        name="combine_branches",
    )(rate, *arrays)


def gather_guided_kernel(size, *refs):
    gathered, out = refs[:-1], refs[-1]
    per = size.ch // size.halves
    squares, norms = [], []
    for slot in range(size.parts):
        parts = []
        for apart in range(size.parts):
            other = slot ^ apart
            part = gathered[apart][:, other * size.sub : (other + 1) * size.sub].astype(F32)
            if apart == slot:
                low = gathered[apart][:, size.queries :].astype(F32)
                squares.append(low[:1, :1] + low[:1, 1:2] + low[:1, 2:3])
                for index in range(3):
                    low = jnp.where(is_place(low.shape, index), 0.0, low)
                part = part + low
            parts.append(part)
        left = tree_sum(parts)
        norms.append(jnp.sum(left * left, axis=(0, 1), keepdims=True))
        out[:per, slot * size.sub : (slot + 1) * size.sub] = left
    row = lax.broadcasted_iota(jnp.int32, (8, size.queries), 0)
    out[per:] = jnp.where(row == 0, tree_sum(squares), tree_sum(norms))


def gather_guided(size, gathered):
    shape = (size.ch // size.halves + 8, size.queries)
    return pl.pallas_call(
        functools.partial(gather_guided_kernel, size),
        grid=(1,),
        in_specs=[whole(x.shape) for x in gathered],
        out_specs=whole(shape),
        out_shape=jax.ShapeDtypeStruct(shape, F32),
        compiler_params=size.params,
        name="gather_guided",
    )(*gathered)


def velocity_grad(size, rate, guidance, stats, moved, grad, ratio_out):
    per = size.ch // size.halves
    norm = tree_sum([x[per + 1 : per + 2, :1] for x in moved])
    squares = tree_sum([x[per : per + 1, :1] for x in moved])
    own = lax.axis_index("img")
    every = [jnp.full((1, 1), stats[k], F32) for k in range(size.images)]
    advantage = relative_reward(every, jnp.full((1, 1), stats[own], F32))
    exponent = (squares - norm * (rate[0] * rate[0])) * (0.5 / (size.queries * size.ch))
    ratio = jnp.exp(exponent)
    gain = surrogate_gain(ratio, advantage)
    factor = gain * (-rate[0] * rate[0] * branch_weight(guidance[0]))
    for half, x in enumerate(moved):
        grad[half_rows(size, half)] = x[:per] * factor
    ratio_out[...] = ratio


def backward_kernel(size, *refs):
    if size.mirrored:
        rate, guidance, stats = refs[:3]
        moved = refs[3 : 3 + size.halves]
        refs = refs[3 + size.halves :]
    else:
        given, refs = refs[0], refs[1:]
    blocks = refs[: size.lists]
    readout, raised, each, inverse, ratio_out, readout_out = refs[size.lists : size.lists + 6]
    refs = refs[size.lists + 6 :]
    outs, refs = refs[: size.lists], refs[size.lists :]
    if size.late:
        late_outs, refs = refs[: size.lists], refs[size.lists :]
    grad_ref, scores, grad_keys, grad_queries, small = refs
    step = 0 if size.mirrored else pl.program_id(0)
    if size.mirrored:
        velocity_grad(size, rate, guidance, stats, moved, grad_ref, ratio_out)
    else:
        grad_ref[...] = given[...]
        ratio_out[...] = jnp.zeros(ratio_out.shape, F32)

    def add(ref, value):
        if size.q_blocks == 1:
            ref[...] = value
            return

        @pl.when(step == 0)
        def _():
            ref[...] = value

        @pl.when(step > 0)
        def _():
            ref[...] += value

    early = size.heads - size.late
    for head in range(size.heads):
        targets, lanes = (outs, lanes_of(head)) if head < early else (late_outs, lanes_of(head - early))
        query = queries_of(size, blocks, head, step)
        keys = keys_of(size, blocks, head)
        values = values_of(size, blocks, head)
        held = readout[:, cols(size.group() * size.width + head * HEAD_DIM, HEAD_DIM)]
        grad = (grad_ref[...] * inverse[head]).astype(BF16)
        delta = jnp.sum(grad.astype(F32) * each[head], axis=0, keepdims=True)
        little = dot_nt(raised[head], grad).T
        add(small.at[head], little)
        projected = dot_nt(jnp.concatenate(values, axis=0), held).astype(BF16)
        tile = dot(projected, grad) - delta
        scores[head] = (raised[head].astype(F32) * tile).astype(BF16)
        add(grad_keys.at[head], dot(scores[head], query) * SCALE)
        found = dot_tn(jnp.concatenate(keys, axis=0), scores[head]) * SCALE
        if size.mirrored:
            grad_queries[head] = found.astype(BF16).T
        else:
            first = pl.multiple_of(step * size.q_block, 128)
            grad_queries[head, pl.ds(first, size.q_block)] = found.astype(BF16).T

        def write():
            little = small[head].astype(BF16)
            readout_out[:, lanes_of(head)] = dot(little, jnp.concatenate(values, axis=0))
            value_text = dot_tn(little[:, size.img_keys :], held)
            for slot in range(size.parts):
                out = at(targets, slot)
                near = slice(slot * size.rows, (slot + 1) * size.rows)
                out[: size.sub, lanes] = grad_queries[head, slot * size.sub : (slot + 1) * size.sub]
                out[size.sub : size.sub + size.rows, lanes] = grad_keys[head, near].astype(BF16)
                start = size.img_keys + slot * size.txt
                pair = [
                    grad_keys[head, start : start + size.txt],
                    value_text[slot * size.txt : (slot + 1) * size.txt],
                ]
                pair = jnp.concatenate(pair, axis=0).astype(BF16)
                out[size.at_pair : size.at_small, lanes] = pair
                out[size.at_small :, lanes] = little[:, near]

        if size.mirrored:
            write()
        else:
            pl.when(step == size.q_blocks - 1)(write)


def backward(size, given, blocks, readout, saved):
    if size.mirrored:
        rate, guidance, stats, moved = given
        first = [rate, guidance, stats] + moved
        specs = [SMEM] * 3 + [size.full(x.shape) for x in moved]
    else:
        first, specs = [given], [size.by_queries(size.ch)]
    raised, each, inverse = saved
    shapes = [x for width in size.home_widths() for x in size.shapes(size.home_rows, width)]
    shapes = [
        jax.ShapeDtypeStruct((1, 1), F32),
        jax.ShapeDtypeStruct((size.ch, size.width), F32),
    ] + shapes
    outs = pl.pallas_call(
        functools.partial(backward_kernel, size),
        in_specs=specs
        + [size.full(x.shape) for x in blocks]
        + [
            size.full(readout.shape),
            size.by_queries(size.heads, size.keys),
            size.by_queries(size.heads, size.ch),
            size.by_queries(size.heads, 1),
        ],
        out_specs=[size.full(x.shape) for x in shapes],
        out_shape=shapes,
        scratch_shapes=[
            pltpu.VMEM((size.ch, size.q_block), F32),
            pltpu.VMEM((size.heads, size.keys, size.q_block), BF16),
            pltpu.VMEM((size.heads, size.keys, HEAD_DIM), F32),
            pltpu.VMEM((size.heads, size.queries, HEAD_DIM), BF16),
            pltpu.VMEM((size.heads, size.ch, size.keys), F32),
        ],
        compiler_params=size.params,
        name="attention_backward",
        **size.grid(),
    )(*first, *blocks, readout, raised, each, inverse)
    sent = outs[2:]
    return outs[0], outs[1], [sent[k : k + size.lists] for k in range(0, len(sent), size.lists)]


def home_kernel(size, readout, *refs):
    out, text_out = refs[-2:]
    offset = 0
    for index, width in enumerate(size.home_widths()):
        blocks = refs[index * size.lists : (index + 1) * size.lists]
        for group in range(size.groups):
            start = (size.base() ^ group) * size.width + offset
            place = cols(start, width)
            held = [at(blocks, group * size.copies + copy) for copy in range(size.copies)]
            for copy in range(size.copies):
                out[0, copy * size.sub : (copy + 1) * size.sub, place] = held[copy][: size.sub]
            if size.copies == 1:
                rest = held[0][size.sub : size.home_rows]
            else:
                rest = sum([x[size.sub :].astype(F32) for x in held]).astype(BF16)
            out[1, :, place] = rest[: size.rows]
            pair = rest[size.rows : size.rows + 2 * size.txt].astype(F32)
            pair = jnp.stack([pair[: size.txt], pair[size.txt :]], axis=1)
            text_out[:, :, place] = pair.astype(BF16)
            for head in range(width // HEAD_DIM):
                near = cols(start + head * HEAD_DIM, HEAD_DIM)
                lanes = slice(head * size.rows, (head + 1) * size.rows)
                little = rest[size.rows + 2 * size.txt :, lanes]
                out[2, :, near] = dot_tn(little, readout[:, near]).astype(BF16)
        offset += width


def home(size, readout, homes):
    shapes = [(3, size.rows, size.features), (size.txt, 2, size.features)]
    outs = [jax.ShapeDtypeStruct(x, BF16) for x in shapes]
    specs = [whole(x.shape) for blocks in homes for x in blocks]
    return pl.pallas_call(
        functools.partial(home_kernel, size),
        grid=(1,),
        in_specs=[whole(readout.shape)] + specs,
        out_specs=[whole(x.shape) for x in outs],
        out_shape=outs,
        compiler_params=size.params,
        name="home_tokens",
    )(readout, *[x for blocks in homes for x in blocks])


def join_readout_kernel(size, held, *refs):
    blocks, outs = refs[: size.parts], refs[size.parts :]
    rows = half_rows(size, 0)
    per = size.ch // size.halves
    total = tree_sum([held[k, rows].astype(F32) for k in range(size.images)]).astype(BF16)
    for block, out in zip(blocks, outs):
        out[0, : size.home_rows] = block[0]
        for head in range(size.heads):
            first = size.home_rows + head * per
            out[0, first : first + per] = total[:, head * HEAD_DIM : (head + 1) * HEAD_DIM]


def join_readout(size, part, blocks):
    sent = (part + mirror(part, "cfg", 1)).astype(BF16)
    held = lax.all_gather(sent, "img", axis=0)
    shape = (1, size.home_rows + size.heads * size.ch // size.halves, HEAD_DIM)
    return pl.pallas_call(
        functools.partial(join_readout_kernel, size),
        grid=(1,),
        in_specs=[whole(held.shape)] + [whole(x.shape) for x in blocks],
        out_specs=[whole(shape)] * size.parts,
        out_shape=[jax.ShapeDtypeStruct(shape, BF16)] * size.parts,
        compiler_params=size.params,
        name="join_readout_grad",
    )(held, *blocks)


def place_kernel(size, *refs):
    out = refs[-1]
    per = size.ch // size.halves
    for half in range(size.halves):
        for slot in range(size.parts):
            found = refs[half * size.parts + slot]
            for head in range(size.heads):
                lanes = cols((size.base() ^ slot) * size.width + head * HEAD_DIM, HEAD_DIM)
                first = size.home_rows + head * per
                out[half_rows(size, half), lanes] = found[0, first : first + per].astype(F32)


def place_readout(size, found):
    return pl.pallas_call(
        functools.partial(place_kernel, size),
        grid=(1,),
        in_specs=[whole(x.shape) for x in found],
        out_specs=whole((size.ch, size.features)),
        out_shape=jax.ShapeDtypeStruct((size.ch, size.features), F32),
        compiler_params=size.params,
        name="place_readout_grad",
    )(*found)


def on_device(img_qkv, txt_kv, readout, old_velocity, noise, step_ratio, rewards, guidance):
    features, channels = readout.shape
    size = Sizes(img_qkv.shape[2], txt_kv.shape[2], features, channels)
    place = lax.axis_index("seq")
    own = lax.axis_index("img")
    slots = img_qkv[0, 0].transpose(1, 0, 2)
    wide = readout.T
    strength = guidance.reshape(1)
    noise_wide, old_wide = noise[0].T, old_velocity[0].T
    text = txt_kv[0, 0]
    if size.mirrored:
        away = list(range(1, size.parts))
        sent = pack(size, slots, text, away, 60 * MIB)
        blocks = [mirror(block, "seq", k) for k, block in zip(away, sent)]
    else:
        blocks = exchange(size, pack(size, slots, text, list(range(size.parts)), 48 * MIB))

    mine = jnp.arange(size.images) == own
    stats = lax.psum(jnp.where(mine, rewards[0], 0.0), "img")
    if size.mirrored:
        stats, near, words = lax.optimization_barrier((stats, slots, text))
        blocks = list(pack(size, near, words, [0], 16 * MIB)) + blocks
        blocks = lax.optimization_barrier(blocks)

    *saved, part = forward(size, strength, blocks, wide)
    if size.mirrored:
        saved, kept, part = saved[:3], saved[3], part
        other = mirror(part, "cfg", 1)
        sent = combine(size, step_ratio, kept, other, noise_wide, old_wide)
        guided = gather_guided(size, spread(size, [sent] * size.parts))
        given = (step_ratio, strength, stats, [guided, mirror(guided, "cfg", 1)])
    else:
        other = mirror(part, "cfg", 1)
        copy = place % size.copies
        rate = step_ratio[0]
        chosen = jnp.arange(size.copies).reshape(-1, 1, 1) == copy
        guided = lax.psum(jnp.where(chosen, (part + other)[None], 0.0), "seq")
        guided = lax.dynamic_index_in_dim(guided, copy, 0, False)
        mixed = lax.all_gather(noise_wide + rate * old_wide, "seq", axis=0)
        near = lax.dynamic_slice_in_dim(mixed, copy * size.sub, size.sub, 2)
        near = near.transpose(1, 0, 2).reshape(channels, size.queries)
        left = near - rate * guided
        norm = lax.psum(jnp.sum(left * left), "seq") / size.groups
        squares = lax.psum(jnp.sum(noise * noise), "seq")
        every = [stats[k] for k in range(size.images)]
        advantage = relative_reward(every, rewards[0])
        count = size.parts * size.rows * channels
        ratio = jnp.exp((squares - norm) * (0.5 / count))
        gain = surrogate_gain(ratio, advantage)
        given = left * (gain * (rate * branch_weight(guidance)))
    found, readout_part, sent = backward(size, given, blocks, wide, saved)
    if size.mirrored:
        ratio = found
    if size.late:
        homes = [exchange(size, sent[0])]
        homes.append(exchange(size, join_readout(size, readout_part, sent[1])))
        joined = homes[1]
        found = joined + [mirror(x, "cfg", 1) for x in joined]
        token_grads, text_grads = home(size, wide, homes)
        token_grads, found = lax.optimization_barrier((token_grads, found))
        readout_grad = place_readout(size, found).T
    else:
        homes = [exchange(size, x) for x in sent]
        token_grads, text_grads = home(size, wide, homes)
        full = jnp.zeros((channels, features), F32)
        start = size.group() * size.width
        full = lax.dynamic_update_slice_in_dim(full, readout_part, start, 1)
        readout_grad = lax.psum(full, ("cfg", "img", "seq")).T
    img_grad = token_grads.transpose(1, 0, 2)[None, None]
    return (img_grad, text_grads[None, None], readout_grad, ratio.reshape(1))


def solution(mesh):
    return jax.shard_map(
        on_device,
        mesh=mesh,
        in_specs=(
            P("cfg", "img", "seq", None, None),
            P("cfg", "img", "seq", None, None),
            P(),
            P("img", "seq", None),
            P("img", "seq", None),
            P("img"),
            P("img"),
            P(),
        ),
        out_specs=(
            P("cfg", "img", "seq", None, None),
            P("cfg", "img", "seq", None, None),
            P(),
            P("img"),
        ),
        check_vma=False,
    )
```

```python
import functools
import math

import jax
import jax.numpy as jnp
from jax import lax
from jax.experimental import pallas as pl
from jax.experimental.pallas import tpu as pltpu
from jax.sharding import PartitionSpec as P

HEADS = 16
HEAD_DIM = 128
SCALE = HEAD_DIM ** (-0.5)
EXP2_SCALE = SCALE * math.log2(math.e)
F32 = jnp.float32
BF16 = jnp.bfloat16
MIB = 1024 * 1024
SMEM = pl.BlockSpec(memory_space=pltpu.SMEM)
ANY = pl.BlockSpec(memory_space=pl.ANY)


def dot(a, b):
    return jnp.dot(a, b, preferred_element_type=F32)


def dot_nt(a, b):
    return lax.dot_general(a, b, (((1,), (1,)), ((), ())), preferred_element_type=F32)


def dot_tn(a, b):
    return lax.dot_general(a, b, (((0,), (0,)), ((), ())), preferred_element_type=F32)


def whole(shape):
    return pl.BlockSpec(shape, lambda *_: (0,) * len(shape))


def at(refs, slot):
    return refs[slot].at[0] if len(refs) > 1 else refs[0].at[slot]


def cols(start, size):
    return pl.ds(pl.multiple_of(start, 128), size)


def tree_sum(terms):
    while len(terms) > 1:
        terms = [terms[k] + terms[k + 1] for k in range(0, len(terms), 2)]
    return terms[0]


def mirror(x, axis, apart):
    count = lax.axis_size(axis)
    return lax.ppermute(x, axis, [(i, i ^ apart) for i in range(count)])


class Sizes:
    def __init__(self, img_rows, txt_rows, features, channels):
        self.parts = lax.axis_size("seq")
        self.images = lax.axis_size("img")
        self.copies = max(1, self.parts // HEADS)
        self.groups = self.parts // self.copies
        self.features = features
        self.ch = channels
        self.width = features // self.groups
        self.heads = self.width // HEAD_DIM
        self.rows = img_rows
        self.txt = txt_rows
        self.sub = img_rows // self.copies
        self.img_keys = self.parts * img_rows
        self.keys = self.img_keys + self.parts * txt_rows
        self.queries = self.parts * self.sub
        power = self.images & (self.images - 1) == 0
        self.mirrored = self.parts in (2, 4, 8) and self.copies == 1
        self.mirrored = self.mirrored and self.heads > 1 and power and lax.axis_size("cfg") == 2
        self.lists = self.parts if self.mirrored else 1
        self.each = self.parts // self.lists
        self.at_keys = self.sub
        self.at_values = self.sub + self.rows
        self.at_text = self.sub + 2 * self.rows
        self.sent_rows = self.at_text + 2 * self.txt
        self.at_pair = self.sub + self.rows
        self.at_small = self.at_pair + 2 * self.txt
        self.home_rows = self.at_small + self.ch
        block = self.queries
        while block % 256 == 0 and self.keys * block > 600_000:
            block //= 2
        self.q_block = block
        self.q_blocks = self.queries // block
        limit = (16 if self.mirrored else 48) * MIB
        self.halves = 2 if self.mirrored else 1
        self.late = 1 if self.mirrored else 0
        self.params = pltpu.CompilerParams(vmem_limit_bytes=limit)

    def tiles(self):
        edges = list(range(0, self.img_keys, self.rows)) + [self.img_keys, self.keys]
        return list(zip(edges[:-1], edges[1:]))

    def shapes(self, rows, width):
        shape = (self.each, rows, width)
        return [jax.ShapeDtypeStruct(shape, BF16) for _ in range(self.lists)]

    def specs(self, rows, width):
        return [whole((self.each, rows, width)) for _ in range(self.lists)]

    def home_widths(self):
        widths = [(self.heads - self.late) * HEAD_DIM]
        return widths + [self.late * HEAD_DIM] * (self.late > 0)

    def grid(self):
        return {} if self.mirrored else {"grid": (self.q_blocks,)}

    def full(self, shape):
        return pl.BlockSpec(memory_space=pltpu.VMEM) if self.mirrored else whole(shape)

    def by_queries(self, *lead):
        if self.mirrored:
            return pl.BlockSpec(memory_space=pltpu.VMEM)
        return pl.BlockSpec(lead + (self.q_block,), lambda b: (0,) * len(lead) + (b,))

    def base(self):
        place = lax.axis_index("seq")
        return place if self.mirrored else jnp.zeros_like(place)

    def group(self):
        return lax.axis_index("seq") // self.copies


def far_first(blocks):
    own, near, *far = blocks
    far, near = lax.optimization_barrier((far, near))
    return [own, near] + list(far)


def spread(size, blocks):
    return [blocks[0]] + [mirror(blocks[k], "seq", k) for k in range(1, size.parts)]


def exchange(size, blocks):
    if size.mirrored:
        return far_first(spread(size, blocks))
    return [lax.all_to_all(blocks[0], "seq", split_axis=0, concat_axis=0, tiled=True)]


def branch_weight(guidance):
    return jnp.where(lax.axis_index("cfg") == 0, guidance, 1.0 - guidance)


def pack_kernel(size, which, slots, text, *refs):
    count = len(which) if size.mirrored else 1
    outs = refs[:count]
    words, block, arrived, left, read = refs[count:]
    incoming = []
    places = []
    for spot, slot in enumerate(which):
        dest = size.base() ^ slot
        place = cols((dest // size.copies) * size.width, size.width)
        places.append(place)
        if size.copies == 1:
            queries = slots.at[0, :, place]
        else:
            first = pl.multiple_of((dest % size.copies) * size.sub, 16)
            queries = slots.at[0, pl.ds(first, size.sub), place]
        ends = (
            (queries, block.at[spot, pl.ds(0, size.sub)]),
            (slots.at[1, :, place], block.at[spot, pl.ds(size.at_keys, size.rows)]),
            (slots.at[2, :, place], block.at[spot, pl.ds(size.at_values, size.rows)]),
        )
        copies = [
            pltpu.make_async_copy(source, target, arrived.at[spot, index])
            for index, (source, target) in enumerate(ends)
        ]
        if not incoming:
            fetch = pltpu.make_async_copy(text, words, read)
            fetch.start()
        for copy in copies:
            copy.start()
        incoming.append(copies)
    fetch.wait()
    outgoing = []
    for spot, (place, copies) in enumerate(zip(places, incoming)):
        pair = words[:, :, place].astype(F32)
        pair = jnp.concatenate([pair[:, 0], pair[:, 1]], axis=0)
        block[spot, size.at_text :] = pair.astype(BF16)
        for copy in copies:
            copy.wait()
        out = outs[spot].at[0] if size.mirrored else outs[0].at[spot]
        outgoing.append(pltpu.make_async_copy(block.at[spot], out, left.at[spot]))
        outgoing[-1].start()
    for copy in outgoing:
        copy.wait()


def pack(size, slots, text, which, limit):
    count = len(which)
    shapes = size.shapes(size.sent_rows, size.width)[: count if size.mirrored else 1]
    return pl.pallas_call(
        functools.partial(pack_kernel, size, which),
        in_specs=[ANY, ANY],
        out_specs=[ANY] * len(shapes),
        out_shape=shapes,
        scratch_shapes=[
            pltpu.VMEM(text.shape, BF16),
            pltpu.VMEM((count, size.sent_rows, size.width), BF16),
            pltpu.SemaphoreType.DMA((count, 3)),
            pltpu.SemaphoreType.DMA((count,)),
            pltpu.SemaphoreType.DMA,
        ],
        compiler_params=pltpu.CompilerParams(vmem_limit_bytes=limit),
        name="pack_tokens",
    )(slots, text)


def lanes_of(head):
    return slice(head * HEAD_DIM, (head + 1) * HEAD_DIM)


def text_rows(size, blocks, head, second):
    found = []
    for slot in range(size.parts):
        block = at(blocks, slot)
        pair = block[size.at_text : size.at_text + 2 * size.txt, lanes_of(head)].astype(F32)
        found.append(pair[size.txt :] if second else pair[: size.txt])
    return jnp.concatenate(found, axis=0).astype(BF16)


def rows_of(size, blocks, head, first, count):
    return [at(blocks, slot)[first : first + count, lanes_of(head)] for slot in range(size.parts)]


def keys_of(size, blocks, head):
    found = rows_of(size, blocks, head, size.at_keys, size.rows)
    return found + [text_rows(size, blocks, head, False)]


def values_of(size, blocks, head):
    found = rows_of(size, blocks, head, size.at_values, size.rows)
    return found + [text_rows(size, blocks, head, True)]


def queries_of(size, blocks, head, step):
    if size.q_blocks == 1:
        return jnp.concatenate(rows_of(size, blocks, head, 0, size.sub), axis=0)
    count = size.q_block // size.sub
    found = [
        blocks[0][step * count + k, : size.sub, lanes_of(head)] for k in range(count)
    ]
    return jnp.concatenate(found, axis=0)


def folded(x, combine):
    return combine(x.reshape(x.shape[0] // 8, 8, x.shape[1]), axis=0)


def forward_kernel(size, guidance, *refs):
    blocks = refs[: size.lists]
    readout, raised, each, inverse = refs[size.lists : size.lists + 4]
    outs = refs[size.lists + 4 : size.lists + 4 + size.halves]
    total, scores = refs[size.lists + 4 + size.halves :]
    step = 0 if size.mirrored else pl.program_id(0)
    weight = branch_weight(guidance[0])
    velocities = []
    for head in range(size.heads):
        query = queries_of(size, blocks, head, step)
        peaks = []
        for (lo, hi), key in zip(size.tiles(), keys_of(size, blocks, head)):
            tile = dot_nt(key, query)
            scores[head, lo:hi] = tile
            peaks.append(folded(tile, jnp.max))
        top = jnp.max(functools.reduce(jnp.maximum, peaks), axis=0, keepdims=True)
        sums = []
        for lo, hi in size.tiles():
            tile = jnp.exp2((scores[head, lo:hi] - top) * EXP2_SCALE)
            sums.append(folded(tile, jnp.sum))
            raised[head, lo:hi] = tile.astype(BF16)
        inverted = 1.0 / jnp.sum(sum(sums[1:], sums[0]), axis=0, keepdims=True)
        held = readout[:, cols(size.group() * size.width + head * HEAD_DIM, HEAD_DIM)]
        projected = [dot_nt(held, value) for value in values_of(size, blocks, head)]
        projected = jnp.concatenate(projected, axis=1).astype(BF16)
        velocity = dot(projected, raised[head]) * inverted
        each[head] = velocity
        inverse[head] = inverted
        velocities.append(velocity)
    total[...] = sum(velocities[1:], velocities[0]) * weight
    for half, out in enumerate(outs):
        out[...] = total[half_rows(size, half)]


def half_rows(size, half):
    per = size.ch // size.halves
    if size.halves == 1:
        return pl.ds(0, per)
    return pl.ds(pl.multiple_of((lax.axis_index("cfg") ^ half) * per, per), per)


def forward(size, guidance, blocks, readout):
    per = size.ch // size.halves
    return pl.pallas_call(
        functools.partial(forward_kernel, size),
        in_specs=[SMEM] + [size.full(x.shape) for x in blocks] + [size.full(readout.shape)],
        out_specs=[
            size.by_queries(size.heads, size.keys),
            size.by_queries(size.heads, size.ch),
            size.by_queries(size.heads, 1),
        ]
        + [size.by_queries(per)] * size.halves,
        out_shape=[
            jax.ShapeDtypeStruct((size.heads, size.keys, size.queries), BF16),
            jax.ShapeDtypeStruct((size.heads, size.ch, size.queries), F32),
            jax.ShapeDtypeStruct((size.heads, 1, size.queries), F32),
        ]
        + [jax.ShapeDtypeStruct((per, size.queries), F32)] * size.halves,
        scratch_shapes=[
            pltpu.VMEM((size.ch, size.q_block), F32),
            pltpu.VMEM((size.heads, size.keys, size.q_block), F32),
        ],
        compiler_params=size.params,
        name="attention_forward",
        **size.grid(),
    )(guidance, *blocks, readout)


def surrogate_gain(ratio, advantage):
    clipped = jnp.clip(ratio, 0.8, 1.2)
    keep = ratio * advantage <= clipped * advantage
    return jnp.where(keep, -ratio * advantage, jnp.zeros_like(ratio))


def relative_reward(every, own):
    count = len(every)
    mean = sum(every[1:], every[0]) / count
    square = sum([x * x for x in every[1:]], every[0] * every[0]) / count
    spread = jnp.sqrt(jnp.maximum(square - mean * mean, 0.0))
    return (own - mean) / jnp.maximum(spread, 1.0)


def combine_kernel(size, rate, part, other, noise, old, out):
    rows = half_rows(size, 0)
    out[:, : size.queries] = (part[...] + other[...]).astype(BF16)
    own = part[:, : size.sub] + other[:, : size.sub]
    own = own - (old[rows] + noise[rows] * (1.0 / rate[0]))
    high = own.astype(BF16)
    low = own - high.astype(F32)
    squares = jnp.sum(noise[rows] * noise[rows], axis=(0, 1), keepdims=True)
    near = squares.astype(BF16).astype(F32)
    far = (squares - near).astype(BF16).astype(F32)
    for index, value in enumerate((near, far, squares - near - far)):
        low = jnp.where(is_place(low.shape, index), value, low)
    out[:, : size.sub] = high
    out[:, size.queries :] = low.astype(BF16)


def is_place(shape, index):
    row = lax.broadcasted_iota(jnp.int32, shape, 0)
    lane = lax.broadcasted_iota(jnp.int32, shape, 1)
    return (row == 0) & (lane == index)


def combine(size, rate, part, other, noise, old):
    arrays = (part, other, noise, old)
    shape = (size.ch // size.halves, size.queries + size.sub)
    return pl.pallas_call(
        functools.partial(combine_kernel, size),
        grid=(1,),
        in_specs=[SMEM] + [whole(x.shape) for x in arrays],
        out_specs=whole(shape),
        out_shape=jax.ShapeDtypeStruct(shape, BF16),
        compiler_params=size.params,
        name="combine_branches",
    )(rate, *arrays)


def gather_guided_kernel(size, *refs):
    gathered, out = refs[:-1], refs[-1]
    per = size.ch // size.halves
    squares, norms = [], []
    for slot in range(size.parts):
        parts = []
        for apart in range(size.parts):
            other = slot ^ apart
            part = gathered[apart][:, other * size.sub : (other + 1) * size.sub].astype(F32)
            if apart == slot:
                low = gathered[apart][:, size.queries :].astype(F32)
                squares.append(low[:1, :1] + low[:1, 1:2] + low[:1, 2:3])
                for index in range(3):
                    low = jnp.where(is_place(low.shape, index), 0.0, low)
                part = part + low
            parts.append(part)
        left = tree_sum(parts)
        norms.append(jnp.sum(left * left, axis=(0, 1), keepdims=True))
        out[:per, slot * size.sub : (slot + 1) * size.sub] = left
    row = lax.broadcasted_iota(jnp.int32, (8, size.queries), 0)
    out[per:] = jnp.where(row == 0, tree_sum(squares), tree_sum(norms))


def gather_guided(size, gathered):
    shape = (size.ch // size.halves + 8, size.queries)
    return pl.pallas_call(
        functools.partial(gather_guided_kernel, size),
        grid=(1,),
        in_specs=[whole(x.shape) for x in gathered],
        out_specs=whole(shape),
        out_shape=jax.ShapeDtypeStruct(shape, F32),
        compiler_params=size.params,
        name="gather_guided",
    )(*gathered)


def velocity_grad(size, rate, guidance, stats, moved, grad, ratio_out):
    per = size.ch // size.halves
    norm = tree_sum([x[per + 1 : per + 2, :1] for x in moved])
    squares = tree_sum([x[per : per + 1, :1] for x in moved])
    own = lax.axis_index("img")
    every = [jnp.full((1, 1), stats[k], F32) for k in range(size.images)]
    advantage = relative_reward(every, jnp.full((1, 1), stats[own], F32))
    exponent = (squares - norm * (rate[0] * rate[0])) * (0.5 / (size.queries * size.ch))
    ratio = jnp.exp(exponent)
    gain = surrogate_gain(ratio, advantage)
    factor = gain * (-rate[0] * rate[0] * branch_weight(guidance[0]))
    for half, x in enumerate(moved):
        grad[half_rows(size, half)] = x[:per] * factor
    ratio_out[...] = ratio


def backward_kernel(size, *refs):
    if size.mirrored:
        rate, guidance, stats = refs[:3]
        moved = refs[3 : 3 + size.halves]
        refs = refs[3 + size.halves :]
    else:
        given, refs = refs[0], refs[1:]
    blocks = refs[: size.lists]
    readout, raised, each, inverse, ratio_out, readout_out = refs[size.lists : size.lists + 6]
    refs = refs[size.lists + 6 :]
    outs, refs = refs[: size.lists], refs[size.lists :]
    if size.late:
        late_outs, refs = refs[: size.lists], refs[size.lists :]
    grad_ref, scores, grad_keys, grad_queries, small = refs
    step = 0 if size.mirrored else pl.program_id(0)
    if size.mirrored:
        velocity_grad(size, rate, guidance, stats, moved, grad_ref, ratio_out)
    else:
        grad_ref[...] = given[...]
        ratio_out[...] = jnp.zeros(ratio_out.shape, F32)

    def add(ref, value):
        if size.q_blocks == 1:
            ref[...] = value
            return

        @pl.when(step == 0)
        def _():
            ref[...] = value

        @pl.when(step > 0)
        def _():
            ref[...] += value

    early = size.heads - size.late
    for head in range(size.heads):
        targets, lanes = (outs, lanes_of(head)) if head < early else (late_outs, lanes_of(head - early))
        query = queries_of(size, blocks, head, step)
        keys = keys_of(size, blocks, head)
        values = values_of(size, blocks, head)
        held = readout[:, cols(size.group() * size.width + head * HEAD_DIM, HEAD_DIM)]
        grad = (grad_ref[...] * inverse[head]).astype(BF16)
        delta = jnp.sum(grad.astype(F32) * each[head], axis=0, keepdims=True)
        little = dot_nt(raised[head], grad).T
        add(small.at[head], little)
        projected = dot_nt(jnp.concatenate(values, axis=0), held).astype(BF16)
        tile = dot(projected, grad) - delta
        scores[head] = (raised[head].astype(F32) * tile).astype(BF16)
        add(grad_keys.at[head], dot(scores[head], query) * SCALE)
        found = dot_tn(jnp.concatenate(keys, axis=0), scores[head]) * SCALE
        if size.mirrored:
            grad_queries[head] = found.astype(BF16).T
        else:
            first = pl.multiple_of(step * size.q_block, 128)
            grad_queries[head, pl.ds(first, size.q_block)] = found.astype(BF16).T

        def write():
            little = small[head].astype(BF16)
            readout_out[:, lanes_of(head)] = dot(little, jnp.concatenate(values, axis=0))
            value_text = dot_tn(little[:, size.img_keys :], held)
            for slot in range(size.parts):
                out = at(targets, slot)
                near = slice(slot * size.rows, (slot + 1) * size.rows)
                out[: size.sub, lanes] = grad_queries[head, slot * size.sub : (slot + 1) * size.sub]
                out[size.sub : size.sub + size.rows, lanes] = grad_keys[head, near].astype(BF16)
                start = size.img_keys + slot * size.txt
                pair = [
                    grad_keys[head, start : start + size.txt],
                    value_text[slot * size.txt : (slot + 1) * size.txt],
                ]
                pair = jnp.concatenate(pair, axis=0).astype(BF16)
                out[size.at_pair : size.at_small, lanes] = pair
                out[size.at_small :, lanes] = little[:, near]

        if size.mirrored:
            write()
        else:
            pl.when(step == size.q_blocks - 1)(write)


def backward(size, given, blocks, readout, saved):
    if size.mirrored:
        rate, guidance, stats, moved = given
        first = [rate, guidance, stats] + moved
        specs = [SMEM] * 3 + [size.full(x.shape) for x in moved]
    else:
        first, specs = [given], [size.by_queries(size.ch)]
    raised, each, inverse = saved
    shapes = [x for width in size.home_widths() for x in size.shapes(size.home_rows, width)]
    shapes = [
        jax.ShapeDtypeStruct((1, 1), F32),
        jax.ShapeDtypeStruct((size.ch, size.width), F32),
    ] + shapes
    outs = pl.pallas_call(
        functools.partial(backward_kernel, size),
        in_specs=specs
        + [size.full(x.shape) for x in blocks]
        + [
            size.full(readout.shape),
            size.by_queries(size.heads, size.keys),
            size.by_queries(size.heads, size.ch),
            size.by_queries(size.heads, 1),
        ],
        out_specs=[size.full(x.shape) for x in shapes],
        out_shape=shapes,
        scratch_shapes=[
            pltpu.VMEM((size.ch, size.q_block), F32),
            pltpu.VMEM((size.heads, size.keys, size.q_block), BF16),
            pltpu.VMEM((size.heads, size.keys, HEAD_DIM), F32),
            pltpu.VMEM((size.heads, size.queries, HEAD_DIM), BF16),
            pltpu.VMEM((size.heads, size.ch, size.keys), F32),
        ],
        compiler_params=size.params,
        name="attention_backward",
        **size.grid(),
    )(*first, *blocks, readout, raised, each, inverse)
    sent = outs[2:]
    return outs[0], outs[1], [sent[k : k + size.lists] for k in range(0, len(sent), size.lists)]


def home_kernel(size, readout, *refs):
    out, text_out = refs[-2:]
    offset = 0
    for index, width in enumerate(size.home_widths()):
        blocks = refs[index * size.lists : (index + 1) * size.lists]
        for group in range(size.groups):
            start = (size.base() ^ group) * size.width + offset
            place = cols(start, width)
            held = [at(blocks, group * size.copies + copy) for copy in range(size.copies)]
            for copy in range(size.copies):
                out[0, copy * size.sub : (copy + 1) * size.sub, place] = held[copy][: size.sub]
            if size.copies == 1:
                rest = held[0][size.sub : size.home_rows]
            else:
                rest = sum([x[size.sub :].astype(F32) for x in held]).astype(BF16)
            out[1, :, place] = rest[: size.rows]
            pair = rest[size.rows : size.rows + 2 * size.txt].astype(F32)
            pair = jnp.stack([pair[: size.txt], pair[size.txt :]], axis=1)
            text_out[:, :, place] = pair.astype(BF16)
            for head in range(width // HEAD_DIM):
                near = cols(start + head * HEAD_DIM, HEAD_DIM)
                lanes = slice(head * size.rows, (head + 1) * size.rows)
                little = rest[size.rows + 2 * size.txt :, lanes]
                out[2, :, near] = dot_tn(little, readout[:, near]).astype(BF16)
        offset += width


def home(size, readout, homes):
    shapes = [(3, size.rows, size.features), (size.txt, 2, size.features)]
    outs = [jax.ShapeDtypeStruct(x, BF16) for x in shapes]
    specs = [whole(x.shape) for blocks in homes for x in blocks]
    return pl.pallas_call(
        functools.partial(home_kernel, size),
        grid=(1,),
        in_specs=[whole(readout.shape)] + specs,
        out_specs=[whole(x.shape) for x in outs],
        out_shape=outs,
        compiler_params=size.params,
        name="home_tokens",
    )(readout, *[x for blocks in homes for x in blocks])


def join_readout_kernel(size, held, *refs):
    blocks, outs = refs[: size.parts], refs[size.parts :]
    rows = half_rows(size, 0)
    per = size.ch // size.halves
    total = tree_sum([held[k, rows].astype(F32) for k in range(size.images)]).astype(BF16)
    for block, out in zip(blocks, outs):
        out[0, : size.home_rows] = block[0]
        for head in range(size.heads):
            first = size.home_rows + head * per
            out[0, first : first + per] = total[:, head * HEAD_DIM : (head + 1) * HEAD_DIM]


def join_readout(size, part, blocks):
    sent = (part + mirror(part, "cfg", 1)).astype(BF16)
    held = lax.all_gather(sent, "img", axis=0)
    shape = (1, size.home_rows + size.heads * size.ch // size.halves, HEAD_DIM)
    return pl.pallas_call(
        functools.partial(join_readout_kernel, size),
        grid=(1,),
        in_specs=[whole(held.shape)] + [whole(x.shape) for x in blocks],
        out_specs=[whole(shape)] * size.parts,
        out_shape=[jax.ShapeDtypeStruct(shape, BF16)] * size.parts,
        compiler_params=size.params,
        name="join_readout_grad",
    )(held, *blocks)


def place_kernel(size, *refs):
    out = refs[-1]
    per = size.ch // size.halves
    for half in range(size.halves):
        for slot in range(size.parts):
            found = refs[half * size.parts + slot]
            for head in range(size.heads):
                lanes = cols((size.base() ^ slot) * size.width + head * HEAD_DIM, HEAD_DIM)
                first = size.home_rows + head * per
                out[half_rows(size, half), lanes] = found[0, first : first + per].astype(F32)


def place_readout(size, found):
    return pl.pallas_call(
        functools.partial(place_kernel, size),
        grid=(1,),
        in_specs=[whole(x.shape) for x in found],
        out_specs=whole((size.ch, size.features)),
        out_shape=jax.ShapeDtypeStruct((size.ch, size.features), F32),
        compiler_params=size.params,
        name="place_readout_grad",
    )(*found)


def on_device(img_qkv, txt_kv, readout, old_velocity, noise, step_ratio, rewards, guidance):
    features, channels = readout.shape
    size = Sizes(img_qkv.shape[2], txt_kv.shape[2], features, channels)
    place = lax.axis_index("seq")
    own = lax.axis_index("img")
    slots = img_qkv[0, 0].transpose(1, 0, 2)
    wide = readout.T
    strength = guidance.reshape(1)
    noise_wide, old_wide = noise[0].T, old_velocity[0].T
    text = txt_kv[0, 0]
    if size.mirrored:
        first = min(2, size.parts - 1)
        rest = [k for k in range(1, size.parts) if k != first]
        packed = dict(zip([first], pack(size, slots, text, [first], 60 * MIB)))
        packed.update(zip(rest, pack(size, slots, text, rest, 60 * MIB) if rest else []))
        blocks = [mirror(packed[k], "seq", k) for k in range(1, size.parts)]
    else:
        blocks = exchange(size, pack(size, slots, text, list(range(size.parts)), 48 * MIB))

    mine = jnp.arange(size.images) == own
    stats = lax.psum(jnp.where(mine, rewards[0], 0.0), "img")
    if size.mirrored:
        stats, near, words = lax.optimization_barrier((stats, slots, text))
        blocks = list(pack(size, near, words, [0], 16 * MIB)) + blocks
        blocks = far_first(blocks)

    *saved, part = forward(size, strength, blocks, wide)
    if size.mirrored:
        saved, kept, part = saved[:3], saved[3], part
        other = mirror(part, "cfg", 1)
        sent = combine(size, step_ratio, kept, other, noise_wide, old_wide)
        guided = gather_guided(size, spread(size, [sent] * size.parts))
        given = (step_ratio, strength, stats, [guided, mirror(guided, "cfg", 1)])
    else:
        other = mirror(part, "cfg", 1)
        copy = place % size.copies
        rate = step_ratio[0]
        chosen = jnp.arange(size.copies).reshape(-1, 1, 1) == copy
        guided = lax.psum(jnp.where(chosen, (part + other)[None], 0.0), "seq")
        guided = lax.dynamic_index_in_dim(guided, copy, 0, False)
        mixed = lax.all_gather(noise_wide + rate * old_wide, "seq", axis=0)
        near = lax.dynamic_slice_in_dim(mixed, copy * size.sub, size.sub, 2)
        near = near.transpose(1, 0, 2).reshape(channels, size.queries)
        left = near - rate * guided
        norm = lax.psum(jnp.sum(left * left), "seq") / size.groups
        squares = lax.psum(jnp.sum(noise * noise), "seq")
        every = [stats[k] for k in range(size.images)]
        advantage = relative_reward(every, rewards[0])
        count = size.parts * size.rows * channels
        ratio = jnp.exp((squares - norm) * (0.5 / count))
        gain = surrogate_gain(ratio, advantage)
        given = left * (gain * (rate * branch_weight(guidance)))
    found, readout_part, sent = backward(size, given, blocks, wide, saved)
    if size.mirrored:
        ratio = found
    if size.late:
        homes = [exchange(size, sent[0])]
        homes.append(spread(size, join_readout(size, readout_part, sent[1])))
        joined = homes[1]
        found = joined + [mirror(x, "cfg", 1) for x in joined]
        token_grads, text_grads = home(size, wide, homes)
        token_grads, found = lax.optimization_barrier((token_grads, found))
        readout_grad = place_readout(size, found).T
    else:
        homes = [exchange(size, x) for x in sent]
        token_grads, text_grads = home(size, wide, homes)
        full = jnp.zeros((channels, features), F32)
        start = size.group() * size.width
        full = lax.dynamic_update_slice_in_dim(full, readout_part, start, 1)
        readout_grad = lax.psum(full, ("cfg", "img", "seq")).T
    img_grad = token_grads.transpose(1, 0, 2)[None, None]
    return (img_grad, text_grads[None, None], readout_grad, ratio.reshape(1))


def solution(mesh):
    return jax.shard_map(
        on_device,
        mesh=mesh,
        in_specs=(
            P("cfg", "img", "seq", None, None),
            P("cfg", "img", "seq", None, None),
            P(),
            P("img", "seq", None),
            P("img", "seq", None),
            P("img"),
            P("img"),
            P(),
        ),
        out_specs=(
            P("cfg", "img", "seq", None, None),
            P("cfg", "img", "seq", None, None),
            P(),
            P("img"),
        ),
        check_vma=False,
    )
```

```python
import functools
import math

import jax
import jax.numpy as jnp
from jax import lax
from jax.experimental import pallas as pl
from jax.experimental.pallas import tpu as pltpu
from jax.sharding import PartitionSpec as P

HEADS = 16
HEAD_DIM = 128
SCALE = HEAD_DIM ** (-0.5)
EXP2_SCALE = SCALE * math.log2(math.e)
F32 = jnp.float32
BF16 = jnp.bfloat16
MIB = 1024 * 1024
SMEM = pl.BlockSpec(memory_space=pltpu.SMEM)
ANY = pl.BlockSpec(memory_space=pl.ANY)


def dot(a, b):
    return jnp.dot(a, b, preferred_element_type=F32)


def dot_nt(a, b):
    return lax.dot_general(a, b, (((1,), (1,)), ((), ())), preferred_element_type=F32)


def dot_tn(a, b):
    return lax.dot_general(a, b, (((0,), (0,)), ((), ())), preferred_element_type=F32)


def whole(shape):
    return pl.BlockSpec(shape, lambda *_: (0,) * len(shape))


def at(refs, slot):
    return refs[slot].at[0] if len(refs) > 1 else refs[0].at[slot]


def cols(start, size):
    return pl.ds(pl.multiple_of(start, 128), size)


def tree_sum(terms):
    while len(terms) > 1:
        terms = [terms[k] + terms[k + 1] for k in range(0, len(terms), 2)]
    return terms[0]


def mirror(x, axis, apart):
    count = lax.axis_size(axis)
    return lax.ppermute(x, axis, [(i, i ^ apart) for i in range(count)])


class Sizes:
    def __init__(self, img_rows, txt_rows, features, channels):
        self.parts = lax.axis_size("seq")
        self.images = lax.axis_size("img")
        self.copies = max(1, self.parts // HEADS)
        self.groups = self.parts // self.copies
        self.features = features
        self.ch = channels
        self.width = features // self.groups
        self.heads = self.width // HEAD_DIM
        self.rows = img_rows
        self.txt = txt_rows
        self.sub = img_rows // self.copies
        self.img_keys = self.parts * img_rows
        self.keys = self.img_keys + self.parts * txt_rows
        self.queries = self.parts * self.sub
        power = self.images & (self.images - 1) == 0
        self.mirrored = self.parts in (2, 4, 8) and self.copies == 1
        self.mirrored = self.mirrored and self.heads > 1 and power and lax.axis_size("cfg") == 2
        self.lists = self.parts if self.mirrored else 1
        self.each = self.parts // self.lists
        self.at_keys = self.sub
        self.at_values = self.sub + self.rows
        self.at_text = self.sub + 2 * self.rows
        self.sent_rows = self.at_text + 2 * self.txt
        self.at_pair = self.sub + self.rows
        self.at_small = self.at_pair + 2 * self.txt
        self.home_rows = self.at_small + self.ch
        block = self.queries
        while block % 256 == 0 and self.keys * block > 600_000:
            block //= 2
        self.q_block = block
        self.q_blocks = self.queries // block
        limit = (16 if self.mirrored else 48) * MIB
        self.halves = 2 if self.mirrored else 1
        self.late = 1 if self.mirrored else 0
        self.params = pltpu.CompilerParams(vmem_limit_bytes=limit)

    def tiles(self):
        edges = list(range(0, self.img_keys, self.rows)) + [self.img_keys, self.keys]
        return list(zip(edges[:-1], edges[1:]))

    def shapes(self, rows, width):
        shape = (self.each, rows, width)
        return [jax.ShapeDtypeStruct(shape, BF16) for _ in range(self.lists)]

    def specs(self, rows, width):
        return [whole((self.each, rows, width)) for _ in range(self.lists)]

    def home_widths(self):
        widths = [(self.heads - self.late) * HEAD_DIM]
        return widths + [self.late * HEAD_DIM] * (self.late > 0)

    def grid(self):
        return {} if self.mirrored else {"grid": (self.q_blocks,)}

    def full(self, shape):
        return pl.BlockSpec(memory_space=pltpu.VMEM) if self.mirrored else whole(shape)

    def by_queries(self, *lead):
        if self.mirrored:
            return pl.BlockSpec(memory_space=pltpu.VMEM)
        return pl.BlockSpec(lead + (self.q_block,), lambda b: (0,) * len(lead) + (b,))

    def base(self):
        place = lax.axis_index("seq")
        return place if self.mirrored else jnp.zeros_like(place)

    def group(self):
        return lax.axis_index("seq") // self.copies


def far_first(blocks):
    own, near, *far = blocks
    far, near = lax.optimization_barrier((far, near))
    return [own, near] + list(far)


def spread(size, blocks):
    return [blocks[0]] + [mirror(blocks[k], "seq", k) for k in range(1, size.parts)]


def exchange(size, blocks):
    if size.mirrored:
        return far_first(spread(size, blocks))
    return [lax.all_to_all(blocks[0], "seq", split_axis=0, concat_axis=0, tiled=True)]


def branch_weight(guidance):
    return jnp.where(lax.axis_index("cfg") == 0, guidance, 1.0 - guidance)


def pack_kernel(size, which, slots, text, *refs):
    count = len(which) if size.mirrored else 1
    outs = refs[:count]
    words, block, arrived, left, read = refs[count:]
    incoming = []
    places = []
    for spot, slot in enumerate(which):
        dest = size.base() ^ slot
        place = cols((dest // size.copies) * size.width, size.width)
        places.append(place)
        if size.copies == 1:
            queries = slots.at[0, :, place]
        else:
            first = pl.multiple_of((dest % size.copies) * size.sub, 16)
            queries = slots.at[0, pl.ds(first, size.sub), place]
        ends = (
            (queries, block.at[spot, pl.ds(0, size.sub)]),
            (slots.at[1, :, place], block.at[spot, pl.ds(size.at_keys, size.rows)]),
            (slots.at[2, :, place], block.at[spot, pl.ds(size.at_values, size.rows)]),
        )
        copies = [
            pltpu.make_async_copy(source, target, arrived.at[spot, index])
            for index, (source, target) in enumerate(ends)
        ]
        if not incoming:
            fetch = pltpu.make_async_copy(text, words, read)
            fetch.start()
        for copy in copies:
            copy.start()
        incoming.append(copies)
    fetch.wait()
    outgoing = []
    for spot, (place, copies) in enumerate(zip(places, incoming)):
        pair = words[:, :, place].astype(F32)
        pair = jnp.concatenate([pair[:, 0], pair[:, 1]], axis=0)
        block[spot, size.at_text :] = pair.astype(BF16)
        for copy in copies:
            copy.wait()
        out = outs[spot].at[0] if size.mirrored else outs[0].at[spot]
        outgoing.append(pltpu.make_async_copy(block.at[spot], out, left.at[spot]))
        outgoing[-1].start()
    for copy in outgoing:
        copy.wait()


def pack(size, slots, text, which, limit):
    count = len(which)
    shapes = size.shapes(size.sent_rows, size.width)[: count if size.mirrored else 1]
    return pl.pallas_call(
        functools.partial(pack_kernel, size, which),
        in_specs=[ANY, ANY],
        out_specs=[ANY] * len(shapes),
        out_shape=shapes,
        scratch_shapes=[
            pltpu.VMEM(text.shape, BF16),
            pltpu.VMEM((count, size.sent_rows, size.width), BF16),
            pltpu.SemaphoreType.DMA((count, 3)),
            pltpu.SemaphoreType.DMA((count,)),
            pltpu.SemaphoreType.DMA,
        ],
        compiler_params=pltpu.CompilerParams(vmem_limit_bytes=limit),
        name="pack_tokens",
    )(slots, text)


def slice_tokens(size, slots, text, slot):
    start = (size.base() ^ slot) * size.width
    tokens = lax.dynamic_slice_in_dim(slots, start, size.width, 2)
    words = lax.dynamic_slice_in_dim(text, start, size.width, 2).transpose(1, 0, 2)
    parts = [tokens.reshape(3 * size.rows, size.width), words.reshape(2 * size.txt, size.width)]
    return jnp.concatenate(parts, axis=0)[None]


def lanes_of(head):
    return slice(head * HEAD_DIM, (head + 1) * HEAD_DIM)


def text_rows(size, blocks, head, second):
    found = []
    for slot in range(size.parts):
        block = at(blocks, slot)
        pair = block[size.at_text : size.at_text + 2 * size.txt, lanes_of(head)].astype(F32)
        found.append(pair[size.txt :] if second else pair[: size.txt])
    return jnp.concatenate(found, axis=0).astype(BF16)


def rows_of(size, blocks, head, first, count):
    return [at(blocks, slot)[first : first + count, lanes_of(head)] for slot in range(size.parts)]


def keys_of(size, blocks, head):
    found = rows_of(size, blocks, head, size.at_keys, size.rows)
    return found + [text_rows(size, blocks, head, False)]


def values_of(size, blocks, head):
    found = rows_of(size, blocks, head, size.at_values, size.rows)
    return found + [text_rows(size, blocks, head, True)]


def queries_of(size, blocks, head, step):
    if size.q_blocks == 1:
        return jnp.concatenate(rows_of(size, blocks, head, 0, size.sub), axis=0)
    count = size.q_block // size.sub
    found = [
        blocks[0][step * count + k, : size.sub, lanes_of(head)] for k in range(count)
    ]
    return jnp.concatenate(found, axis=0)


def folded(x, combine):
    return combine(x.reshape(x.shape[0] // 8, 8, x.shape[1]), axis=0)


def forward_kernel(size, guidance, *refs):
    blocks = refs[: size.lists]
    readout, raised, each, inverse = refs[size.lists : size.lists + 4]
    outs = refs[size.lists + 4 : size.lists + 4 + size.halves]
    total, scores = refs[size.lists + 4 + size.halves :]
    step = 0 if size.mirrored else pl.program_id(0)
    weight = branch_weight(guidance[0])
    velocities = []
    for head in range(size.heads):
        query = queries_of(size, blocks, head, step)
        peaks = []
        for (lo, hi), key in zip(size.tiles(), keys_of(size, blocks, head)):
            tile = dot_nt(key, query)
            scores[head, lo:hi] = tile
            peaks.append(folded(tile, jnp.max))
        top = jnp.max(functools.reduce(jnp.maximum, peaks), axis=0, keepdims=True)
        sums = []
        for lo, hi in size.tiles():
            tile = jnp.exp2((scores[head, lo:hi] - top) * EXP2_SCALE)
            sums.append(folded(tile, jnp.sum))
            raised[head, lo:hi] = tile.astype(BF16)
        inverted = 1.0 / jnp.sum(sum(sums[1:], sums[0]), axis=0, keepdims=True)
        held = readout[:, cols(size.group() * size.width + head * HEAD_DIM, HEAD_DIM)]
        projected = [dot_nt(held, value) for value in values_of(size, blocks, head)]
        projected = jnp.concatenate(projected, axis=1).astype(BF16)
        velocity = dot(projected, raised[head]) * inverted
        each[head] = velocity
        inverse[head] = inverted
        velocities.append(velocity)
    total[...] = sum(velocities[1:], velocities[0]) * weight
    for half, out in enumerate(outs):
        out[...] = total[half_rows(size, half)]


def half_rows(size, half):
    per = size.ch // size.halves
    if size.halves == 1:
        return pl.ds(0, per)
    return pl.ds(pl.multiple_of((lax.axis_index("cfg") ^ half) * per, per), per)


def forward(size, guidance, blocks, readout):
    per = size.ch // size.halves
    return pl.pallas_call(
        functools.partial(forward_kernel, size),
        in_specs=[SMEM] + [size.full(x.shape) for x in blocks] + [size.full(readout.shape)],
        out_specs=[
            size.by_queries(size.heads, size.keys),
            size.by_queries(size.heads, size.ch),
            size.by_queries(size.heads, 1),
        ]
        + [size.by_queries(per)] * size.halves,
        out_shape=[
            jax.ShapeDtypeStruct((size.heads, size.keys, size.queries), BF16),
            jax.ShapeDtypeStruct((size.heads, size.ch, size.queries), F32),
            jax.ShapeDtypeStruct((size.heads, 1, size.queries), F32),
        ]
        + [jax.ShapeDtypeStruct((per, size.queries), F32)] * size.halves,
        scratch_shapes=[
            pltpu.VMEM((size.ch, size.q_block), F32),
            pltpu.VMEM((size.heads, size.keys, size.q_block), F32),
        ],
        compiler_params=size.params,
        name="attention_forward",
        **size.grid(),
    )(guidance, *blocks, readout)


def surrogate_gain(ratio, advantage):
    clipped = jnp.clip(ratio, 0.8, 1.2)
    keep = ratio * advantage <= clipped * advantage
    return jnp.where(keep, -ratio * advantage, jnp.zeros_like(ratio))


def relative_reward(every, own):
    count = len(every)
    mean = sum(every[1:], every[0]) / count
    square = sum([x * x for x in every[1:]], every[0] * every[0]) / count
    spread = jnp.sqrt(jnp.maximum(square - mean * mean, 0.0))
    return (own - mean) / jnp.maximum(spread, 1.0)


def combine_kernel(size, rate, part, other, noise, old, out):
    rows = half_rows(size, 0)
    out[:, : size.queries] = (part[...] + other[...]).astype(BF16)
    own = part[:, : size.sub] + other[:, : size.sub]
    own = own - (old[rows] + noise[rows] * (1.0 / rate[0]))
    high = own.astype(BF16)
    low = own - high.astype(F32)
    squares = jnp.sum(noise[rows] * noise[rows], axis=(0, 1), keepdims=True)
    near = squares.astype(BF16).astype(F32)
    far = (squares - near).astype(BF16).astype(F32)
    for index, value in enumerate((near, far, squares - near - far)):
        low = jnp.where(is_place(low.shape, index), value, low)
    out[:, : size.sub] = high
    out[:, size.queries :] = low.astype(BF16)


def is_place(shape, index):
    row = lax.broadcasted_iota(jnp.int32, shape, 0)
    lane = lax.broadcasted_iota(jnp.int32, shape, 1)
    return (row == 0) & (lane == index)


def combine(size, rate, part, other, noise, old):
    arrays = (part, other, noise, old)
    shape = (size.ch // size.halves, size.queries + size.sub)
    return pl.pallas_call(
        functools.partial(combine_kernel, size),
        grid=(1,),
        in_specs=[SMEM] + [whole(x.shape) for x in arrays],
        out_specs=whole(shape),
        out_shape=jax.ShapeDtypeStruct(shape, BF16),
        compiler_params=size.params,
        name="combine_branches",
    )(rate, *arrays)


def gather_guided_kernel(size, *refs):
    gathered, out = refs[:-1], refs[-1]
    per = size.ch // size.halves
    squares, norms = [], []
    for slot in range(size.parts):
        parts = []
        for apart in range(size.parts):
            other = slot ^ apart
            part = gathered[apart][:, other * size.sub : (other + 1) * size.sub].astype(F32)
            if apart == slot:
                low = gathered[apart][:, size.queries :].astype(F32)
                squares.append(low[:1, :1] + low[:1, 1:2] + low[:1, 2:3])
                for index in range(3):
                    low = jnp.where(is_place(low.shape, index), 0.0, low)
                part = part + low
            parts.append(part)
        left = tree_sum(parts)
        norms.append(jnp.sum(left * left, axis=(0, 1), keepdims=True))
        out[:per, slot * size.sub : (slot + 1) * size.sub] = left
    row = lax.broadcasted_iota(jnp.int32, (8, size.queries), 0)
    out[per:] = jnp.where(row == 0, tree_sum(squares), tree_sum(norms))


def gather_guided(size, gathered):
    shape = (size.ch // size.halves + 8, size.queries)
    return pl.pallas_call(
        functools.partial(gather_guided_kernel, size),
        grid=(1,),
        in_specs=[whole(x.shape) for x in gathered],
        out_specs=whole(shape),
        out_shape=jax.ShapeDtypeStruct(shape, F32),
        compiler_params=size.params,
        name="gather_guided",
    )(*gathered)


def velocity_grad(size, rate, guidance, stats, moved, grad, ratio_out):
    per = size.ch // size.halves
    norm = tree_sum([x[per + 1 : per + 2, :1] for x in moved])
    squares = tree_sum([x[per : per + 1, :1] for x in moved])
    own = lax.axis_index("img")
    every = [jnp.full((1, 1), stats[k], F32) for k in range(size.images)]
    advantage = relative_reward(every, jnp.full((1, 1), stats[own], F32))
    exponent = (squares - norm * (rate[0] * rate[0])) * (0.5 / (size.queries * size.ch))
    ratio = jnp.exp(exponent)
    gain = surrogate_gain(ratio, advantage)
    factor = gain * (-rate[0] * rate[0] * branch_weight(guidance[0]))
    for half, x in enumerate(moved):
        grad[half_rows(size, half)] = x[:per] * factor
    ratio_out[...] = ratio


def backward_kernel(size, *refs):
    if size.mirrored:
        rate, guidance, stats = refs[:3]
        moved = refs[3 : 3 + size.halves]
        refs = refs[3 + size.halves :]
    else:
        given, refs = refs[0], refs[1:]
    blocks = refs[: size.lists]
    readout, raised, each, inverse, ratio_out, readout_out = refs[size.lists : size.lists + 6]
    refs = refs[size.lists + 6 :]
    outs, refs = refs[: size.lists], refs[size.lists :]
    if size.late:
        late_outs, refs = refs[: size.lists], refs[size.lists :]
    grad_ref, scores, grad_keys, grad_queries, small = refs
    step = 0 if size.mirrored else pl.program_id(0)
    if size.mirrored:
        velocity_grad(size, rate, guidance, stats, moved, grad_ref, ratio_out)
    else:
        grad_ref[...] = given[...]
        ratio_out[...] = jnp.zeros(ratio_out.shape, F32)

    def add(ref, value):
        if size.q_blocks == 1:
            ref[...] = value
            return

        @pl.when(step == 0)
        def _():
            ref[...] = value

        @pl.when(step > 0)
        def _():
            ref[...] += value

    early = size.heads - size.late
    for head in range(size.heads):
        targets, lanes = (outs, lanes_of(head)) if head < early else (late_outs, lanes_of(head - early))
        query = queries_of(size, blocks, head, step)
        keys = keys_of(size, blocks, head)
        values = values_of(size, blocks, head)
        held = readout[:, cols(size.group() * size.width + head * HEAD_DIM, HEAD_DIM)]
        grad = (grad_ref[...] * inverse[head]).astype(BF16)
        delta = jnp.sum(grad.astype(F32) * each[head], axis=0, keepdims=True)
        little = dot_nt(raised[head], grad).T
        add(small.at[head], little)
        projected = dot_nt(jnp.concatenate(values, axis=0), held).astype(BF16)
        tile = dot(projected, grad) - delta
        scores[head] = (raised[head].astype(F32) * tile).astype(BF16)
        add(grad_keys.at[head], dot(scores[head], query) * SCALE)
        found = dot_tn(jnp.concatenate(keys, axis=0), scores[head]) * SCALE
        if size.mirrored:
            grad_queries[head] = found.astype(BF16).T
        else:
            first = pl.multiple_of(step * size.q_block, 128)
            grad_queries[head, pl.ds(first, size.q_block)] = found.astype(BF16).T

        def write():
            little = small[head].astype(BF16)
            readout_out[:, lanes_of(head)] = dot(little, jnp.concatenate(values, axis=0))
            value_text = dot_tn(little[:, size.img_keys :], held)
            for slot in range(size.parts):
                out = at(targets, slot)
                near = slice(slot * size.rows, (slot + 1) * size.rows)
                out[: size.sub, lanes] = grad_queries[head, slot * size.sub : (slot + 1) * size.sub]
                out[size.sub : size.sub + size.rows, lanes] = grad_keys[head, near].astype(BF16)
                start = size.img_keys + slot * size.txt
                pair = [
                    grad_keys[head, start : start + size.txt],
                    value_text[slot * size.txt : (slot + 1) * size.txt],
                ]
                pair = jnp.concatenate(pair, axis=0).astype(BF16)
                out[size.at_pair : size.at_small, lanes] = pair
                out[size.at_small :, lanes] = little[:, near]

        if size.mirrored:
            write()
        else:
            pl.when(step == size.q_blocks - 1)(write)


def backward(size, given, blocks, readout, saved):
    if size.mirrored:
        rate, guidance, stats, moved = given
        first = [rate, guidance, stats] + moved
        specs = [SMEM] * 3 + [size.full(x.shape) for x in moved]
    else:
        first, specs = [given], [size.by_queries(size.ch)]
    raised, each, inverse = saved
    shapes = [x for width in size.home_widths() for x in size.shapes(size.home_rows, width)]
    shapes = [
        jax.ShapeDtypeStruct((1, 1), F32),
        jax.ShapeDtypeStruct((size.ch, size.width), F32),
    ] + shapes
    outs = pl.pallas_call(
        functools.partial(backward_kernel, size),
        in_specs=specs
        + [size.full(x.shape) for x in blocks]
        + [
            size.full(readout.shape),
            size.by_queries(size.heads, size.keys),
            size.by_queries(size.heads, size.ch),
            size.by_queries(size.heads, 1),
        ],
        out_specs=[size.full(x.shape) for x in shapes],
        out_shape=shapes,
        scratch_shapes=[
            pltpu.VMEM((size.ch, size.q_block), F32),
            pltpu.VMEM((size.heads, size.keys, size.q_block), BF16),
            pltpu.VMEM((size.heads, size.keys, HEAD_DIM), F32),
            pltpu.VMEM((size.heads, size.queries, HEAD_DIM), BF16),
            pltpu.VMEM((size.heads, size.ch, size.keys), F32),
        ],
        compiler_params=size.params,
        name="attention_backward",
        **size.grid(),
    )(*first, *blocks, readout, raised, each, inverse)
    sent = outs[2:]
    return outs[0], outs[1], [sent[k : k + size.lists] for k in range(0, len(sent), size.lists)]


def home_kernel(size, readout, *refs):
    out, text_out = refs[-2:]
    offset = 0
    for index, width in enumerate(size.home_widths()):
        blocks = refs[index * size.lists : (index + 1) * size.lists]
        for group in range(size.groups):
            start = (size.base() ^ group) * size.width + offset
            place = cols(start, width)
            held = [at(blocks, group * size.copies + copy) for copy in range(size.copies)]
            for copy in range(size.copies):
                out[0, copy * size.sub : (copy + 1) * size.sub, place] = held[copy][: size.sub]
            if size.copies == 1:
                rest = held[0][size.sub : size.home_rows]
            else:
                rest = sum([x[size.sub :].astype(F32) for x in held]).astype(BF16)
            out[1, :, place] = rest[: size.rows]
            pair = rest[size.rows : size.rows + 2 * size.txt].astype(F32)
            pair = jnp.stack([pair[: size.txt], pair[size.txt :]], axis=1)
            text_out[:, :, place] = pair.astype(BF16)
            for head in range(width // HEAD_DIM):
                near = cols(start + head * HEAD_DIM, HEAD_DIM)
                lanes = slice(head * size.rows, (head + 1) * size.rows)
                little = rest[size.rows + 2 * size.txt :, lanes]
                out[2, :, near] = dot_tn(little, readout[:, near]).astype(BF16)
        offset += width


def home(size, readout, homes):
    shapes = [(3, size.rows, size.features), (size.txt, 2, size.features)]
    outs = [jax.ShapeDtypeStruct(x, BF16) for x in shapes]
    specs = [whole(x.shape) for blocks in homes for x in blocks]
    return pl.pallas_call(
        functools.partial(home_kernel, size),
        grid=(1,),
        in_specs=[whole(readout.shape)] + specs,
        out_specs=[whole(x.shape) for x in outs],
        out_shape=outs,
        compiler_params=size.params,
        name="home_tokens",
    )(readout, *[x for blocks in homes for x in blocks])


def join_readout_kernel(size, held, *refs):
    blocks, outs = refs[: size.parts], refs[size.parts :]
    rows = half_rows(size, 0)
    per = size.ch // size.halves
    total = tree_sum([held[k, rows].astype(F32) for k in range(size.images)]).astype(BF16)
    for block, out in zip(blocks, outs):
        out[0, : size.home_rows] = block[0]
        for head in range(size.heads):
            first = size.home_rows + head * per
            out[0, first : first + per] = total[:, head * HEAD_DIM : (head + 1) * HEAD_DIM]


def join_readout(size, part, blocks):
    sent = (part + mirror(part, "cfg", 1)).astype(BF16)
    held = lax.all_gather(sent, "img", axis=0)
    shape = (1, size.home_rows + size.heads * size.ch // size.halves, HEAD_DIM)
    return pl.pallas_call(
        functools.partial(join_readout_kernel, size),
        grid=(1,),
        in_specs=[whole(held.shape)] + [whole(x.shape) for x in blocks],
        out_specs=[whole(shape)] * size.parts,
        out_shape=[jax.ShapeDtypeStruct(shape, BF16)] * size.parts,
        compiler_params=size.params,
        name="join_readout_grad",
    )(held, *blocks)


def place_kernel(size, *refs):
    out = refs[-1]
    per = size.ch // size.halves
    for half in range(size.halves):
        for slot in range(size.parts):
            found = refs[half * size.parts + slot]
            for head in range(size.heads):
                lanes = cols((size.base() ^ slot) * size.width + head * HEAD_DIM, HEAD_DIM)
                first = size.home_rows + head * per
                out[half_rows(size, half), lanes] = found[0, first : first + per].astype(F32)


def place_readout(size, found):
    return pl.pallas_call(
        functools.partial(place_kernel, size),
        grid=(1,),
        in_specs=[whole(x.shape) for x in found],
        out_specs=whole((size.ch, size.features)),
        out_shape=jax.ShapeDtypeStruct((size.ch, size.features), F32),
        compiler_params=size.params,
        name="place_readout_grad",
    )(*found)


def on_device(img_qkv, txt_kv, readout, old_velocity, noise, step_ratio, rewards, guidance):
    features, channels = readout.shape
    size = Sizes(img_qkv.shape[2], txt_kv.shape[2], features, channels)
    place = lax.axis_index("seq")
    own = lax.axis_index("img")
    slots = img_qkv[0, 0].transpose(1, 0, 2)
    wide = readout.T
    strength = guidance.reshape(1)
    noise_wide, old_wide = noise[0].T, old_velocity[0].T
    text = txt_kv[0, 0]
    if size.mirrored:
        first = min(2, size.parts - 1)
        rest = [k for k in range(1, size.parts) if k != first]
        packed = {first: slice_tokens(size, slots, text, first)}
        packed.update(zip(rest, pack(size, slots, text, rest, 60 * MIB) if rest else []))
        blocks = [mirror(packed[k], "seq", k) for k in range(1, size.parts)]
    else:
        blocks = exchange(size, pack(size, slots, text, list(range(size.parts)), 48 * MIB))

    mine = jnp.arange(size.images) == own
    stats = lax.psum(jnp.where(mine, rewards[0], 0.0), "img")
    if size.mirrored:
        stats, near, words = lax.optimization_barrier((stats, slots, text))
        blocks = list(pack(size, near, words, [0], 16 * MIB)) + blocks
        blocks = far_first(blocks)

    *saved, part = forward(size, strength, blocks, wide)
    if size.mirrored:
        saved, kept, part = saved[:3], saved[3], part
        other = mirror(part, "cfg", 1)
        sent = combine(size, step_ratio, kept, other, noise_wide, old_wide)
        guided = gather_guided(size, spread(size, [sent] * size.parts))
        given = (step_ratio, strength, stats, [guided, mirror(guided, "cfg", 1)])
    else:
        other = mirror(part, "cfg", 1)
        copy = place % size.copies
        rate = step_ratio[0]
        chosen = jnp.arange(size.copies).reshape(-1, 1, 1) == copy
        guided = lax.psum(jnp.where(chosen, (part + other)[None], 0.0), "seq")
        guided = lax.dynamic_index_in_dim(guided, copy, 0, False)
        mixed = lax.all_gather(noise_wide + rate * old_wide, "seq", axis=0)
        near = lax.dynamic_slice_in_dim(mixed, copy * size.sub, size.sub, 2)
        near = near.transpose(1, 0, 2).reshape(channels, size.queries)
        left = near - rate * guided
        norm = lax.psum(jnp.sum(left * left), "seq") / size.groups
        squares = lax.psum(jnp.sum(noise * noise), "seq")
        every = [stats[k] for k in range(size.images)]
        advantage = relative_reward(every, rewards[0])
        count = size.parts * size.rows * channels
        ratio = jnp.exp((squares - norm) * (0.5 / count))
        gain = surrogate_gain(ratio, advantage)
        given = left * (gain * (rate * branch_weight(guidance)))
    found, readout_part, sent = backward(size, given, blocks, wide, saved)
    if size.mirrored:
        ratio = found
    if size.late:
        homes = [exchange(size, sent[0])]
        homes.append(spread(size, join_readout(size, readout_part, sent[1])))
        joined = homes[1]
        found = joined + [mirror(x, "cfg", 1) for x in joined]
        token_grads, text_grads = home(size, wide, homes)
        token_grads, found = lax.optimization_barrier((token_grads, found))
        readout_grad = place_readout(size, found).T
    else:
        homes = [exchange(size, x) for x in sent]
        token_grads, text_grads = home(size, wide, homes)
        full = jnp.zeros((channels, features), F32)
        start = size.group() * size.width
        full = lax.dynamic_update_slice_in_dim(full, readout_part, start, 1)
        readout_grad = lax.psum(full, ("cfg", "img", "seq")).T
    img_grad = token_grads.transpose(1, 0, 2)[None, None]
    return (img_grad, text_grads[None, None], readout_grad, ratio.reshape(1))


def solution(mesh):
    return jax.shard_map(
        on_device,
        mesh=mesh,
        in_specs=(
            P("cfg", "img", "seq", None, None),
            P("cfg", "img", "seq", None, None),
            P(),
            P("img", "seq", None),
            P("img", "seq", None),
            P("img"),
            P("img"),
            P(),
        ),
        out_specs=(
            P("cfg", "img", "seq", None, None),
            P("cfg", "img", "seq", None, None),
            P(),
            P("img"),
        ),
        check_vma=False,
    )
```

```python
import functools
import math

import jax
import jax.numpy as jnp
from jax import lax
from jax.experimental import pallas as pl
from jax.experimental.pallas import tpu as pltpu
from jax.sharding import PartitionSpec as P

HEADS = 16
HEAD_DIM = 128
SCALE = HEAD_DIM ** (-0.5)
EXP2_SCALE = SCALE * math.log2(math.e)
F32 = jnp.float32
BF16 = jnp.bfloat16
MIB = 1024 * 1024
SMEM = pl.BlockSpec(memory_space=pltpu.SMEM)
ANY = pl.BlockSpec(memory_space=pl.ANY)


def dot(a, b):
    return jnp.dot(a, b, preferred_element_type=F32)


def dot_nt(a, b):
    return lax.dot_general(a, b, (((1,), (1,)), ((), ())), preferred_element_type=F32)


def dot_tn(a, b):
    return lax.dot_general(a, b, (((0,), (0,)), ((), ())), preferred_element_type=F32)


def whole(shape):
    return pl.BlockSpec(shape, lambda *_: (0,) * len(shape))


def at(refs, slot):
    return refs[slot].at[0] if len(refs) > 1 else refs[0].at[slot]


def cols(start, size):
    return pl.ds(pl.multiple_of(start, 128), size)


def tree_sum(terms):
    while len(terms) > 1:
        terms = [terms[k] + terms[k + 1] for k in range(0, len(terms), 2)]
    return terms[0]


def mirror(x, axis, apart):
    count = lax.axis_size(axis)
    return lax.ppermute(x, axis, [(i, i ^ apart) for i in range(count)])


class Sizes:
    def __init__(self, img_rows, txt_rows, features, channels):
        self.parts = lax.axis_size("seq")
        self.images = lax.axis_size("img")
        self.copies = max(1, self.parts // HEADS)
        self.groups = self.parts // self.copies
        self.features = features
        self.ch = channels
        self.width = features // self.groups
        self.heads = self.width // HEAD_DIM
        self.rows = img_rows
        self.txt = txt_rows
        self.sub = img_rows // self.copies
        self.img_keys = self.parts * img_rows
        self.keys = self.img_keys + self.parts * txt_rows
        self.queries = self.parts * self.sub
        power = self.images & (self.images - 1) == 0
        self.mirrored = self.parts in (2, 4, 8) and self.copies == 1
        self.mirrored = self.mirrored and self.heads > 1 and power and lax.axis_size("cfg") == 2
        self.lists = self.parts if self.mirrored else 1
        self.each = self.parts // self.lists
        self.at_keys = self.sub
        self.at_values = self.sub + self.rows
        self.at_text = self.sub + 2 * self.rows
        self.sent_rows = self.at_text + 2 * self.txt
        self.at_pair = self.sub + self.rows
        self.at_small = self.at_pair + 2 * self.txt
        self.home_rows = self.at_small + self.ch
        block = self.queries
        while block % 256 == 0 and self.keys * block > 600_000:
            block //= 2
        self.q_block = block
        self.q_blocks = self.queries // block
        limit = (16 if self.mirrored else 48) * MIB
        self.halves = 2 if self.mirrored else 1
        self.late = 1 if self.mirrored else 0
        self.params = pltpu.CompilerParams(vmem_limit_bytes=limit)

    def tiles(self):
        edges = list(range(0, self.img_keys, self.rows)) + [self.img_keys, self.keys]
        return list(zip(edges[:-1], edges[1:]))

    def shapes(self, rows, width):
        shape = (self.each, rows, width)
        return [jax.ShapeDtypeStruct(shape, BF16) for _ in range(self.lists)]

    def specs(self, rows, width):
        return [whole((self.each, rows, width)) for _ in range(self.lists)]

    def home_widths(self):
        widths = [(self.heads - self.late) * HEAD_DIM]
        return widths + [self.late * HEAD_DIM] * (self.late > 0)

    def grid(self):
        return {} if self.mirrored else {"grid": (self.q_blocks,)}

    def full(self, shape):
        return pl.BlockSpec(memory_space=pltpu.VMEM) if self.mirrored else whole(shape)

    def by_queries(self, *lead):
        if self.mirrored:
            return pl.BlockSpec(memory_space=pltpu.VMEM)
        return pl.BlockSpec(lead + (self.q_block,), lambda b: (0,) * len(lead) + (b,))

    def base(self):
        place = lax.axis_index("seq")
        return place if self.mirrored else jnp.zeros_like(place)

    def group(self):
        return lax.axis_index("seq") // self.copies


def far_first(blocks):
    own, near, *far = blocks
    far, near = lax.optimization_barrier((far, near))
    return [own, near] + list(far)


def spread(size, blocks):
    return [blocks[0]] + [mirror(blocks[k], "seq", k) for k in range(1, size.parts)]


def exchange(size, blocks):
    if size.mirrored:
        own, near, *far = spread(size, blocks)
        far, near = lax.optimization_barrier((far[::-1], near))
        return [own, near] + list(far)[::-1]
    return [lax.all_to_all(blocks[0], "seq", split_axis=0, concat_axis=0, tiled=True)]


def branch_weight(guidance):
    return jnp.where(lax.axis_index("cfg") == 0, guidance, 1.0 - guidance)


def pack_kernel(size, which, slots, text, *refs):
    count = len(which) if size.mirrored else 1
    outs = refs[:count]
    words, block, arrived, left, read = refs[count:]
    incoming = []
    places = []
    for spot, slot in enumerate(which):
        dest = size.base() ^ slot
        place = cols((dest // size.copies) * size.width, size.width)
        places.append(place)
        if size.copies == 1:
            queries = slots.at[0, :, place]
        else:
            first = pl.multiple_of((dest % size.copies) * size.sub, 16)
            queries = slots.at[0, pl.ds(first, size.sub), place]
        ends = (
            (queries, block.at[spot, pl.ds(0, size.sub)]),
            (slots.at[1, :, place], block.at[spot, pl.ds(size.at_keys, size.rows)]),
            (slots.at[2, :, place], block.at[spot, pl.ds(size.at_values, size.rows)]),
        )
        copies = [
            pltpu.make_async_copy(source, target, arrived.at[spot, index])
            for index, (source, target) in enumerate(ends)
        ]
        if not incoming:
            fetch = pltpu.make_async_copy(text, words, read)
            fetch.start()
        for copy in copies:
            copy.start()
        incoming.append(copies)
    fetch.wait()
    outgoing = []
    for spot, (place, copies) in enumerate(zip(places, incoming)):
        pair = words[:, :, place].astype(F32)
        pair = jnp.concatenate([pair[:, 0], pair[:, 1]], axis=0)
        block[spot, size.at_text :] = pair.astype(BF16)
        for copy in copies:
            copy.wait()
        out = outs[spot].at[0] if size.mirrored else outs[0].at[spot]
        outgoing.append(pltpu.make_async_copy(block.at[spot], out, left.at[spot]))
        outgoing[-1].start()
    for copy in outgoing:
        copy.wait()


def pack(size, slots, text, which, limit):
    count = len(which)
    shapes = size.shapes(size.sent_rows, size.width)[: count if size.mirrored else 1]
    return pl.pallas_call(
        functools.partial(pack_kernel, size, which),
        in_specs=[ANY, ANY],
        out_specs=[ANY] * len(shapes),
        out_shape=shapes,
        scratch_shapes=[
            pltpu.VMEM(text.shape, BF16),
            pltpu.VMEM((count, size.sent_rows, size.width), BF16),
            pltpu.SemaphoreType.DMA((count, 3)),
            pltpu.SemaphoreType.DMA((count,)),
            pltpu.SemaphoreType.DMA,
        ],
        compiler_params=pltpu.CompilerParams(vmem_limit_bytes=limit),
        name="pack_tokens",
    )(slots, text)


def slice_tokens(size, slots, text, slot):
    start = (size.base() ^ slot) * size.width
    tokens = lax.dynamic_slice_in_dim(slots, start, size.width, 2)
    words = lax.dynamic_slice_in_dim(text, start, size.width, 2).transpose(1, 0, 2)
    parts = [tokens.reshape(3 * size.rows, size.width), words.reshape(2 * size.txt, size.width)]
    return jnp.concatenate(parts, axis=0)[None]


def lanes_of(head):
    return slice(head * HEAD_DIM, (head + 1) * HEAD_DIM)


def text_rows(size, blocks, head, second):
    found = []
    for slot in range(size.parts):
        block = at(blocks, slot)
        pair = block[size.at_text : size.at_text + 2 * size.txt, lanes_of(head)].astype(F32)
        found.append(pair[size.txt :] if second else pair[: size.txt])
    return jnp.concatenate(found, axis=0).astype(BF16)


def rows_of(size, blocks, head, first, count):
    return [at(blocks, slot)[first : first + count, lanes_of(head)] for slot in range(size.parts)]


def keys_of(size, blocks, head):
    found = rows_of(size, blocks, head, size.at_keys, size.rows)
    return found + [text_rows(size, blocks, head, False)]


def values_of(size, blocks, head):
    found = rows_of(size, blocks, head, size.at_values, size.rows)
    return found + [text_rows(size, blocks, head, True)]


def queries_of(size, blocks, head, step):
    if size.q_blocks == 1:
        return jnp.concatenate(rows_of(size, blocks, head, 0, size.sub), axis=0)
    count = size.q_block // size.sub
    found = [
        blocks[0][step * count + k, : size.sub, lanes_of(head)] for k in range(count)
    ]
    return jnp.concatenate(found, axis=0)


def folded(x, combine):
    return combine(x.reshape(x.shape[0] // 8, 8, x.shape[1]), axis=0)


def forward_kernel(size, guidance, *refs):
    blocks = refs[: size.lists]
    readout, raised, each, inverse = refs[size.lists : size.lists + 4]
    outs = refs[size.lists + 4 : size.lists + 4 + size.halves]
    total, scores = refs[size.lists + 4 + size.halves :]
    step = 0 if size.mirrored else pl.program_id(0)
    weight = branch_weight(guidance[0])
    velocities = []
    for head in range(size.heads):
        query = queries_of(size, blocks, head, step)
        peaks = []
        for (lo, hi), key in zip(size.tiles(), keys_of(size, blocks, head)):
            tile = dot_nt(key, query)
            scores[head, lo:hi] = tile
            peaks.append(folded(tile, jnp.max))
        top = jnp.max(functools.reduce(jnp.maximum, peaks), axis=0, keepdims=True)
        sums = []
        for lo, hi in size.tiles():
            tile = jnp.exp2((scores[head, lo:hi] - top) * EXP2_SCALE)
            sums.append(folded(tile, jnp.sum))
            raised[head, lo:hi] = tile.astype(BF16)
        inverted = 1.0 / jnp.sum(sum(sums[1:], sums[0]), axis=0, keepdims=True)
        held = readout[:, cols(size.group() * size.width + head * HEAD_DIM, HEAD_DIM)]
        projected = [dot_nt(held, value) for value in values_of(size, blocks, head)]
        projected = jnp.concatenate(projected, axis=1).astype(BF16)
        velocity = dot(projected, raised[head]) * inverted
        each[head] = velocity
        inverse[head] = inverted
        velocities.append(velocity)
    total[...] = sum(velocities[1:], velocities[0]) * weight
    for half, out in enumerate(outs):
        out[...] = total[half_rows(size, half)]


def half_rows(size, half):
    per = size.ch // size.halves
    if size.halves == 1:
        return pl.ds(0, per)
    return pl.ds(pl.multiple_of((lax.axis_index("cfg") ^ half) * per, per), per)


def forward(size, guidance, blocks, readout):
    per = size.ch // size.halves
    return pl.pallas_call(
        functools.partial(forward_kernel, size),
        in_specs=[SMEM] + [size.full(x.shape) for x in blocks] + [size.full(readout.shape)],
        out_specs=[
            size.by_queries(size.heads, size.keys),
            size.by_queries(size.heads, size.ch),
            size.by_queries(size.heads, 1),
        ]
        + [size.by_queries(per)] * size.halves,
        out_shape=[
            jax.ShapeDtypeStruct((size.heads, size.keys, size.queries), BF16),
            jax.ShapeDtypeStruct((size.heads, size.ch, size.queries), F32),
            jax.ShapeDtypeStruct((size.heads, 1, size.queries), F32),
        ]
        + [jax.ShapeDtypeStruct((per, size.queries), F32)] * size.halves,
        scratch_shapes=[
            pltpu.VMEM((size.ch, size.q_block), F32),
            pltpu.VMEM((size.heads, size.keys, size.q_block), F32),
        ],
        compiler_params=size.params,
        name="attention_forward",
        **size.grid(),
    )(guidance, *blocks, readout)


def surrogate_gain(ratio, advantage):
    clipped = jnp.clip(ratio, 0.8, 1.2)
    keep = ratio * advantage <= clipped * advantage
    return jnp.where(keep, -ratio * advantage, jnp.zeros_like(ratio))


def relative_reward(every, own):
    count = len(every)
    mean = sum(every[1:], every[0]) / count
    square = sum([x * x for x in every[1:]], every[0] * every[0]) / count
    spread = jnp.sqrt(jnp.maximum(square - mean * mean, 0.0))
    return (own - mean) / jnp.maximum(spread, 1.0)


def combine_kernel(size, rate, part, other, noise, old, out):
    rows = half_rows(size, 0)
    out[:, : size.queries] = (part[...] + other[...]).astype(BF16)
    own = part[:, : size.sub] + other[:, : size.sub]
    own = own - (old[rows] + noise[rows] * (1.0 / rate[0]))
    high = own.astype(BF16)
    low = own - high.astype(F32)
    squares = jnp.sum(noise[rows] * noise[rows], axis=(0, 1), keepdims=True)
    near = squares.astype(BF16).astype(F32)
    far = (squares - near).astype(BF16).astype(F32)
    for index, value in enumerate((near, far, squares - near - far)):
        low = jnp.where(is_place(low.shape, index), value, low)
    out[:, : size.sub] = high
    out[:, size.queries :] = low.astype(BF16)


def is_place(shape, index):
    row = lax.broadcasted_iota(jnp.int32, shape, 0)
    lane = lax.broadcasted_iota(jnp.int32, shape, 1)
    return (row == 0) & (lane == index)


def combine(size, rate, part, other, noise, old):
    arrays = (part, other, noise, old)
    shape = (size.ch // size.halves, size.queries + size.sub)
    return pl.pallas_call(
        functools.partial(combine_kernel, size),
        grid=(1,),
        in_specs=[SMEM] + [whole(x.shape) for x in arrays],
        out_specs=whole(shape),
        out_shape=jax.ShapeDtypeStruct(shape, BF16),
        compiler_params=size.params,
        name="combine_branches",
    )(rate, *arrays)


def gather_guided_kernel(size, *refs):
    gathered, out = refs[:-1], refs[-1]
    per = size.ch // size.halves
    squares, norms = [], []
    for slot in range(size.parts):
        parts = []
        for apart in range(size.parts):
            other = slot ^ apart
            part = gathered[apart][:, other * size.sub : (other + 1) * size.sub].astype(F32)
            if apart == slot:
                low = gathered[apart][:, size.queries :].astype(F32)
                squares.append(low[:1, :1] + low[:1, 1:2] + low[:1, 2:3])
                for index in range(3):
                    low = jnp.where(is_place(low.shape, index), 0.0, low)
                part = part + low
            parts.append(part)
        left = tree_sum(parts)
        norms.append(jnp.sum(left * left, axis=(0, 1), keepdims=True))
        out[:per, slot * size.sub : (slot + 1) * size.sub] = left
    row = lax.broadcasted_iota(jnp.int32, (8, size.queries), 0)
    out[per:] = jnp.where(row == 0, tree_sum(squares), tree_sum(norms))


def gather_guided(size, gathered):
    shape = (size.ch // size.halves + 8, size.queries)
    return pl.pallas_call(
        functools.partial(gather_guided_kernel, size),
        grid=(1,),
        in_specs=[whole(x.shape) for x in gathered],
        out_specs=whole(shape),
        out_shape=jax.ShapeDtypeStruct(shape, F32),
        compiler_params=size.params,
        name="gather_guided",
    )(*gathered)


def velocity_grad(size, rate, guidance, stats, moved, grad, ratio_out):
    per = size.ch // size.halves
    norm = tree_sum([x[per + 1 : per + 2, :1] for x in moved])
    squares = tree_sum([x[per : per + 1, :1] for x in moved])
    own = lax.axis_index("img")
    every = [jnp.full((1, 1), stats[k], F32) for k in range(size.images)]
    advantage = relative_reward(every, jnp.full((1, 1), stats[own], F32))
    exponent = (squares - norm * (rate[0] * rate[0])) * (0.5 / (size.queries * size.ch))
    ratio = jnp.exp(exponent)
    gain = surrogate_gain(ratio, advantage)
    factor = gain * (-rate[0] * rate[0] * branch_weight(guidance[0]))
    for half, x in enumerate(moved):
        grad[half_rows(size, half)] = x[:per] * factor
    ratio_out[...] = ratio


def backward_kernel(size, *refs):
    if size.mirrored:
        rate, guidance, stats = refs[:3]
        moved = refs[3 : 3 + size.halves]
        refs = refs[3 + size.halves :]
    else:
        given, refs = refs[0], refs[1:]
    blocks = refs[: size.lists]
    readout, raised, each, inverse, ratio_out, readout_out = refs[size.lists : size.lists + 6]
    refs = refs[size.lists + 6 :]
    outs, refs = refs[: size.lists], refs[size.lists :]
    if size.late:
        late_outs, refs = refs[: size.lists], refs[size.lists :]
    grad_ref, scores, grad_keys, grad_queries, small = refs
    step = 0 if size.mirrored else pl.program_id(0)
    if size.mirrored:
        velocity_grad(size, rate, guidance, stats, moved, grad_ref, ratio_out)
    else:
        grad_ref[...] = given[...]
        ratio_out[...] = jnp.zeros(ratio_out.shape, F32)

    def add(ref, value):
        if size.q_blocks == 1:
            ref[...] = value
            return

        @pl.when(step == 0)
        def _():
            ref[...] = value

        @pl.when(step > 0)
        def _():
            ref[...] += value

    early = size.heads - size.late
    for head in range(size.heads):
        targets, lanes = (outs, lanes_of(head)) if head < early else (late_outs, lanes_of(head - early))
        query = queries_of(size, blocks, head, step)
        keys = keys_of(size, blocks, head)
        values = values_of(size, blocks, head)
        held = readout[:, cols(size.group() * size.width + head * HEAD_DIM, HEAD_DIM)]
        grad = (grad_ref[...] * inverse[head]).astype(BF16)
        delta = jnp.sum(grad.astype(F32) * each[head], axis=0, keepdims=True)
        little = dot_nt(raised[head], grad).T
        add(small.at[head], little)
        projected = dot_nt(jnp.concatenate(values, axis=0), held).astype(BF16)
        tile = dot(projected, grad) - delta
        scores[head] = (raised[head].astype(F32) * tile).astype(BF16)
        add(grad_keys.at[head], dot(scores[head], query) * SCALE)
        found = dot_tn(jnp.concatenate(keys, axis=0), scores[head]) * SCALE
        if size.mirrored:
            grad_queries[head] = found.astype(BF16).T
        else:
            first = pl.multiple_of(step * size.q_block, 128)
            grad_queries[head, pl.ds(first, size.q_block)] = found.astype(BF16).T

        def write():
            little = small[head].astype(BF16)
            readout_out[:, lanes_of(head)] = dot(little, jnp.concatenate(values, axis=0))
            value_text = dot_tn(little[:, size.img_keys :], held)
            for slot in range(size.parts):
                out = at(targets, slot)
                near = slice(slot * size.rows, (slot + 1) * size.rows)
                out[: size.sub, lanes] = grad_queries[head, slot * size.sub : (slot + 1) * size.sub]
                out[size.sub : size.sub + size.rows, lanes] = grad_keys[head, near].astype(BF16)
                start = size.img_keys + slot * size.txt
                pair = [
                    grad_keys[head, start : start + size.txt],
                    value_text[slot * size.txt : (slot + 1) * size.txt],
                ]
                pair = jnp.concatenate(pair, axis=0).astype(BF16)
                out[size.at_pair : size.at_small, lanes] = pair
                out[size.at_small :, lanes] = little[:, near]

        if size.mirrored:
            write()
        else:
            pl.when(step == size.q_blocks - 1)(write)


def backward(size, given, blocks, readout, saved):
    if size.mirrored:
        rate, guidance, stats, moved = given
        first = [rate, guidance, stats] + moved
        specs = [SMEM] * 3 + [size.full(x.shape) for x in moved]
    else:
        first, specs = [given], [size.by_queries(size.ch)]
    raised, each, inverse = saved
    shapes = [x for width in size.home_widths() for x in size.shapes(size.home_rows, width)]
    shapes = [
        jax.ShapeDtypeStruct((1, 1), F32),
        jax.ShapeDtypeStruct((size.ch, size.width), F32),
    ] + shapes
    outs = pl.pallas_call(
        functools.partial(backward_kernel, size),
        in_specs=specs
        + [size.full(x.shape) for x in blocks]
        + [
            size.full(readout.shape),
            size.by_queries(size.heads, size.keys),
            size.by_queries(size.heads, size.ch),
            size.by_queries(size.heads, 1),
        ],
        out_specs=[size.full(x.shape) for x in shapes],
        out_shape=shapes,
        scratch_shapes=[
            pltpu.VMEM((size.ch, size.q_block), F32),
            pltpu.VMEM((size.heads, size.keys, size.q_block), BF16),
            pltpu.VMEM((size.heads, size.keys, HEAD_DIM), F32),
            pltpu.VMEM((size.heads, size.queries, HEAD_DIM), BF16),
            pltpu.VMEM((size.heads, size.ch, size.keys), F32),
        ],
        compiler_params=size.params,
        name="attention_backward",
        **size.grid(),
    )(*first, *blocks, readout, raised, each, inverse)
    sent = outs[2:]
    return outs[0], outs[1], [sent[k : k + size.lists] for k in range(0, len(sent), size.lists)]


def home_kernel(size, readout, *refs):
    out, text_out = refs[-2:]
    offset = 0
    for index, width in enumerate(size.home_widths()):
        blocks = refs[index * size.lists : (index + 1) * size.lists]
        for group in range(size.groups):
            start = (size.base() ^ group) * size.width + offset
            place = cols(start, width)
            held = [at(blocks, group * size.copies + copy) for copy in range(size.copies)]
            for copy in range(size.copies):
                out[0, copy * size.sub : (copy + 1) * size.sub, place] = held[copy][: size.sub]
            if size.copies == 1:
                rest = held[0][size.sub : size.home_rows]
            else:
                rest = sum([x[size.sub :].astype(F32) for x in held]).astype(BF16)
            out[1, :, place] = rest[: size.rows]
            pair = rest[size.rows : size.rows + 2 * size.txt].astype(F32)
            pair = jnp.stack([pair[: size.txt], pair[size.txt :]], axis=1)
            text_out[:, :, place] = pair.astype(BF16)
            for head in range(width // HEAD_DIM):
                near = cols(start + head * HEAD_DIM, HEAD_DIM)
                lanes = slice(head * size.rows, (head + 1) * size.rows)
                little = rest[size.rows + 2 * size.txt :, lanes]
                out[2, :, near] = dot_tn(little, readout[:, near]).astype(BF16)
        offset += width


def home(size, readout, homes):
    shapes = [(3, size.rows, size.features), (size.txt, 2, size.features)]
    outs = [jax.ShapeDtypeStruct(x, BF16) for x in shapes]
    specs = [whole(x.shape) for blocks in homes for x in blocks]
    return pl.pallas_call(
        functools.partial(home_kernel, size),
        grid=(1,),
        in_specs=[whole(readout.shape)] + specs,
        out_specs=[whole(x.shape) for x in outs],
        out_shape=outs,
        compiler_params=size.params,
        name="home_tokens",
    )(readout, *[x for blocks in homes for x in blocks])


def join_readout_kernel(size, held, *refs):
    blocks, outs = refs[: size.parts], refs[size.parts :]
    rows = half_rows(size, 0)
    per = size.ch // size.halves
    total = tree_sum([held[k, rows].astype(F32) for k in range(size.images)]).astype(BF16)
    for block, out in zip(blocks, outs):
        out[0, : size.home_rows] = block[0]
        for head in range(size.heads):
            first = size.home_rows + head * per
            out[0, first : first + per] = total[:, head * HEAD_DIM : (head + 1) * HEAD_DIM]


def join_readout(size, part, blocks):
    sent = (part + mirror(part, "cfg", 1)).astype(BF16)
    held = lax.all_gather(sent, "img", axis=0)
    shape = (1, size.home_rows + size.heads * size.ch // size.halves, HEAD_DIM)
    return pl.pallas_call(
        functools.partial(join_readout_kernel, size),
        grid=(1,),
        in_specs=[whole(held.shape)] + [whole(x.shape) for x in blocks],
        out_specs=[whole(shape)] * size.parts,
        out_shape=[jax.ShapeDtypeStruct(shape, BF16)] * size.parts,
        compiler_params=size.params,
        name="join_readout_grad",
    )(held, *blocks)


def place_kernel(size, *refs):
    out = refs[-1]
    per = size.ch // size.halves
    for half in range(size.halves):
        for slot in range(size.parts):
            found = refs[half * size.parts + slot]
            for head in range(size.heads):
                lanes = cols((size.base() ^ slot) * size.width + head * HEAD_DIM, HEAD_DIM)
                first = size.home_rows + head * per
                out[half_rows(size, half), lanes] = found[0, first : first + per].astype(F32)


def place_readout(size, found):
    return pl.pallas_call(
        functools.partial(place_kernel, size),
        grid=(1,),
        in_specs=[whole(x.shape) for x in found],
        out_specs=whole((size.ch, size.features)),
        out_shape=jax.ShapeDtypeStruct((size.ch, size.features), F32),
        compiler_params=size.params,
        name="place_readout_grad",
    )(*found)


def on_device(img_qkv, txt_kv, readout, old_velocity, noise, step_ratio, rewards, guidance):
    features, channels = readout.shape
    size = Sizes(img_qkv.shape[2], txt_kv.shape[2], features, channels)
    place = lax.axis_index("seq")
    own = lax.axis_index("img")
    slots = img_qkv[0, 0].transpose(1, 0, 2)
    wide = readout.T
    strength = guidance.reshape(1)
    noise_wide, old_wide = noise[0].T, old_velocity[0].T
    text = txt_kv[0, 0]
    if size.mirrored:
        first = min(2, size.parts - 1)
        rest = [k for k in range(1, size.parts) if k != first]
        packed = {first: slice_tokens(size, slots, text, first)}
        packed.update(zip(rest, pack(size, slots, text, rest, 60 * MIB) if rest else []))
        blocks = [mirror(packed[k], "seq", k) for k in range(1, size.parts)]
    else:
        blocks = exchange(size, pack(size, slots, text, list(range(size.parts)), 48 * MIB))

    mine = jnp.arange(size.images) == own
    stats = lax.psum(jnp.where(mine, rewards[0], 0.0), "img")
    if size.mirrored:
        stats, near, words = lax.optimization_barrier((stats, slots, text))
        blocks = list(pack(size, near, words, [0], 16 * MIB)) + blocks
        blocks = far_first(blocks)

    *saved, part = forward(size, strength, blocks, wide)
    if size.mirrored:
        saved, kept, part = saved[:3], saved[3], part
        other = mirror(part, "cfg", 1)
        sent = combine(size, step_ratio, kept, other, noise_wide, old_wide)
        guided = gather_guided(size, spread(size, [sent] * size.parts))
        given = (step_ratio, strength, stats, [guided, mirror(guided, "cfg", 1)])
    else:
        other = mirror(part, "cfg", 1)
        copy = place % size.copies
        rate = step_ratio[0]
        chosen = jnp.arange(size.copies).reshape(-1, 1, 1) == copy
        guided = lax.psum(jnp.where(chosen, (part + other)[None], 0.0), "seq")
        guided = lax.dynamic_index_in_dim(guided, copy, 0, False)
        mixed = lax.all_gather(noise_wide + rate * old_wide, "seq", axis=0)
        near = lax.dynamic_slice_in_dim(mixed, copy * size.sub, size.sub, 2)
        near = near.transpose(1, 0, 2).reshape(channels, size.queries)
        left = near - rate * guided
        norm = lax.psum(jnp.sum(left * left), "seq") / size.groups
        squares = lax.psum(jnp.sum(noise * noise), "seq")
        every = [stats[k] for k in range(size.images)]
        advantage = relative_reward(every, rewards[0])
        count = size.parts * size.rows * channels
        ratio = jnp.exp((squares - norm) * (0.5 / count))
        gain = surrogate_gain(ratio, advantage)
        given = left * (gain * (rate * branch_weight(guidance)))
    found, readout_part, sent = backward(size, given, blocks, wide, saved)
    if size.mirrored:
        ratio = found
    if size.late:
        homes = [exchange(size, sent[0])]
        homes.append(spread(size, join_readout(size, readout_part, sent[1])))
        joined = homes[1]
        found = joined + [mirror(x, "cfg", 1) for x in joined]
        token_grads, text_grads = home(size, wide, homes)
        token_grads, found = lax.optimization_barrier((token_grads, found))
        readout_grad = place_readout(size, found).T
    else:
        homes = [exchange(size, x) for x in sent]
        token_grads, text_grads = home(size, wide, homes)
        full = jnp.zeros((channels, features), F32)
        start = size.group() * size.width
        full = lax.dynamic_update_slice_in_dim(full, readout_part, start, 1)
        readout_grad = lax.psum(full, ("cfg", "img", "seq")).T
    img_grad = token_grads.transpose(1, 0, 2)[None, None]
    return (img_grad, text_grads[None, None], readout_grad, ratio.reshape(1))


def solution(mesh):
    return jax.shard_map(
        on_device,
        mesh=mesh,
        in_specs=(
            P("cfg", "img", "seq", None, None),
            P("cfg", "img", "seq", None, None),
            P(),
            P("img", "seq", None),
            P("img", "seq", None),
            P("img"),
            P("img"),
            P(),
        ),
        out_specs=(
            P("cfg", "img", "seq", None, None),
            P("cfg", "img", "seq", None, None),
            P(),
            P("img"),
        ),
        check_vma=False,
    )
```

```python
import functools
import math

import jax
import jax.numpy as jnp
from jax import lax
from jax.experimental import pallas as pl
from jax.experimental.pallas import tpu as pltpu
from jax.sharding import PartitionSpec as P

HEADS = 16
HEAD_DIM = 128
SCALE = HEAD_DIM ** (-0.5)
EXP2_SCALE = SCALE * math.log2(math.e)
F32 = jnp.float32
BF16 = jnp.bfloat16
MIB = 1024 * 1024
SMEM = pl.BlockSpec(memory_space=pltpu.SMEM)
ANY = pl.BlockSpec(memory_space=pl.ANY)


def dot(a, b):
    return jnp.dot(a, b, preferred_element_type=F32)


def dot_nt(a, b):
    return lax.dot_general(a, b, (((1,), (1,)), ((), ())), preferred_element_type=F32)


def dot_tn(a, b):
    return lax.dot_general(a, b, (((0,), (0,)), ((), ())), preferred_element_type=F32)


def whole(shape):
    return pl.BlockSpec(shape, lambda *_: (0,) * len(shape))


def at(refs, slot):
    return refs[slot].at[0] if len(refs) > 1 else refs[0].at[slot]


def cols(start, size):
    return pl.ds(pl.multiple_of(start, 128), size)


def tree_sum(terms):
    while len(terms) > 1:
        terms = [terms[k] + terms[k + 1] for k in range(0, len(terms), 2)]
    return terms[0]


def mirror(x, axis, apart):
    count = lax.axis_size(axis)
    return lax.ppermute(x, axis, [(i, i ^ apart) for i in range(count)])


class Sizes:
    def __init__(self, img_rows, txt_rows, features, channels):
        self.parts = lax.axis_size("seq")
        self.images = lax.axis_size("img")
        self.copies = max(1, self.parts // HEADS)
        self.groups = self.parts // self.copies
        self.features = features
        self.ch = channels
        self.width = features // self.groups
        self.heads = self.width // HEAD_DIM
        self.rows = img_rows
        self.txt = txt_rows
        self.sub = img_rows // self.copies
        self.img_keys = self.parts * img_rows
        self.keys = self.img_keys + self.parts * txt_rows
        self.queries = self.parts * self.sub
        power = self.images & (self.images - 1) == 0
        self.mirrored = self.parts in (2, 4, 8) and self.copies == 1
        self.mirrored = self.mirrored and self.heads > 1 and power and lax.axis_size("cfg") == 2
        self.lists = self.parts if self.mirrored else 1
        self.each = self.parts // self.lists
        self.at_keys = self.sub
        self.at_values = self.sub + self.rows
        self.at_text = self.sub + 2 * self.rows
        self.sent_rows = self.at_text + 2 * self.txt
        self.at_pair = self.sub + self.rows
        self.at_small = self.at_pair + 2 * self.txt
        self.home_rows = self.at_small + self.ch
        block = self.queries
        while block % 256 == 0 and self.keys * block > 600_000:
            block //= 2
        self.q_block = block
        self.q_blocks = self.queries // block
        limit = (16 if self.mirrored else 48) * MIB
        self.halves = 2 if self.mirrored else 1
        self.late = 1 if self.mirrored else 0
        self.params = pltpu.CompilerParams(vmem_limit_bytes=limit)

    def tiles(self):
        edges = list(range(0, self.img_keys, self.rows)) + [self.img_keys, self.keys]
        return list(zip(edges[:-1], edges[1:]))

    def shapes(self, rows, width):
        shape = (self.each, rows, width)
        return [jax.ShapeDtypeStruct(shape, BF16) for _ in range(self.lists)]

    def specs(self, rows, width):
        return [whole((self.each, rows, width)) for _ in range(self.lists)]

    def home_widths(self):
        widths = [(self.heads - self.late) * HEAD_DIM]
        return widths + [self.late * HEAD_DIM] * (self.late > 0)

    def grid(self):
        return {} if self.mirrored else {"grid": (self.q_blocks,)}

    def full(self, shape):
        return pl.BlockSpec(memory_space=pltpu.VMEM) if self.mirrored else whole(shape)

    def by_queries(self, *lead):
        if self.mirrored:
            return pl.BlockSpec(memory_space=pltpu.VMEM)
        return pl.BlockSpec(lead + (self.q_block,), lambda b: (0,) * len(lead) + (b,))

    def base(self):
        place = lax.axis_index("seq")
        return place if self.mirrored else jnp.zeros_like(place)

    def group(self):
        return lax.axis_index("seq") // self.copies


def far_first(blocks):
    own, near, *far = blocks
    far, near = lax.optimization_barrier((far, near))
    return [own, near] + list(far)


def spread(size, blocks):
    return [blocks[0]] + [mirror(blocks[k], "seq", k) for k in range(1, size.parts)]


def exchange(size, blocks):
    if size.mirrored:
        own, near, *far = spread(size, blocks)
        far, near = lax.optimization_barrier((far[::-1], near))
        return [own, near] + list(far)[::-1]
    return [lax.all_to_all(blocks[0], "seq", split_axis=0, concat_axis=0, tiled=True)]


def branch_weight(guidance):
    return jnp.where(lax.axis_index("cfg") == 0, guidance, 1.0 - guidance)


def pack_kernel(size, which, slots, text, *refs):
    count = len(which) if size.mirrored else 1
    outs = refs[:count]
    words, block, arrived, left, read = refs[count:]
    incoming = []
    places = []
    for spot, slot in enumerate(which):
        dest = size.base() ^ slot
        place = cols((dest // size.copies) * size.width, size.width)
        places.append(place)
        if size.copies == 1:
            queries = slots.at[0, :, place]
        else:
            first = pl.multiple_of((dest % size.copies) * size.sub, 16)
            queries = slots.at[0, pl.ds(first, size.sub), place]
        ends = (
            (queries, block.at[spot, pl.ds(0, size.sub)]),
            (slots.at[1, :, place], block.at[spot, pl.ds(size.at_keys, size.rows)]),
            (slots.at[2, :, place], block.at[spot, pl.ds(size.at_values, size.rows)]),
        )
        copies = [
            pltpu.make_async_copy(source, target, arrived.at[spot, index])
            for index, (source, target) in enumerate(ends)
        ]
        if not incoming:
            fetch = pltpu.make_async_copy(text, words, read)
            fetch.start()
        for copy in copies:
            copy.start()
        incoming.append(copies)
    fetch.wait()
    outgoing = []
    for spot, (place, copies) in enumerate(zip(places, incoming)):
        pair = words[:, :, place].astype(F32)
        pair = jnp.concatenate([pair[:, 0], pair[:, 1]], axis=0)
        block[spot, size.at_text :] = pair.astype(BF16)
        for copy in copies:
            copy.wait()
        out = outs[spot].at[0] if size.mirrored else outs[0].at[spot]
        outgoing.append(pltpu.make_async_copy(block.at[spot], out, left.at[spot]))
        outgoing[-1].start()
    for copy in outgoing:
        copy.wait()


def pack(size, slots, text, which, limit):
    count = len(which)
    shapes = size.shapes(size.sent_rows, size.width)[: count if size.mirrored else 1]
    return pl.pallas_call(
        functools.partial(pack_kernel, size, which),
        in_specs=[ANY, ANY],
        out_specs=[ANY] * len(shapes),
        out_shape=shapes,
        scratch_shapes=[
            pltpu.VMEM(text.shape, BF16),
            pltpu.VMEM((count, size.sent_rows, size.width), BF16),
            pltpu.SemaphoreType.DMA((count, 3)),
            pltpu.SemaphoreType.DMA((count,)),
            pltpu.SemaphoreType.DMA,
        ],
        compiler_params=pltpu.CompilerParams(vmem_limit_bytes=limit),
        name="pack_tokens",
    )(slots, text)


def slice_tokens(size, slots, text, slot):
    start = (size.base() ^ slot) * size.width
    tokens = lax.dynamic_slice_in_dim(slots, start, size.width, 2)
    words = lax.dynamic_slice_in_dim(text, start, size.width, 2).transpose(1, 0, 2)
    parts = [tokens.reshape(3 * size.rows, size.width), words.reshape(2 * size.txt, size.width)]
    return jnp.concatenate(parts, axis=0)[None]


def lanes_of(head):
    return slice(head * HEAD_DIM, (head + 1) * HEAD_DIM)


def text_rows(size, blocks, head, second):
    found = []
    for slot in range(size.parts):
        block = at(blocks, slot)
        pair = block[size.at_text : size.at_text + 2 * size.txt, lanes_of(head)].astype(F32)
        found.append(pair[size.txt :] if second else pair[: size.txt])
    return jnp.concatenate(found, axis=0).astype(BF16)


def rows_of(size, blocks, head, first, count):
    return [at(blocks, slot)[first : first + count, lanes_of(head)] for slot in range(size.parts)]


def keys_of(size, blocks, head):
    found = rows_of(size, blocks, head, size.at_keys, size.rows)
    return found + [text_rows(size, blocks, head, False)]


def values_of(size, blocks, head):
    found = rows_of(size, blocks, head, size.at_values, size.rows)
    return found + [text_rows(size, blocks, head, True)]


def queries_of(size, blocks, head, step):
    if size.q_blocks == 1:
        return jnp.concatenate(rows_of(size, blocks, head, 0, size.sub), axis=0)
    count = size.q_block // size.sub
    found = [
        blocks[0][step * count + k, : size.sub, lanes_of(head)] for k in range(count)
    ]
    return jnp.concatenate(found, axis=0)


def folded(x, combine):
    return combine(x.reshape(x.shape[0] // 8, 8, x.shape[1]), axis=0)


def forward_kernel(size, guidance, *refs):
    blocks = refs[: size.lists]
    readout, raised, each, inverse = refs[size.lists : size.lists + 4]
    outs = refs[size.lists + 4 : size.lists + 4 + size.halves]
    total, scores = refs[size.lists + 4 + size.halves :]
    step = 0 if size.mirrored else pl.program_id(0)
    weight = branch_weight(guidance[0])
    velocities = []
    for head in range(size.heads):
        query = queries_of(size, blocks, head, step)
        peaks = []
        for (lo, hi), key in zip(size.tiles(), keys_of(size, blocks, head)):
            tile = dot_nt(key, query)
            scores[head, lo:hi] = tile
            peaks.append(folded(tile, jnp.max))
        top = jnp.max(functools.reduce(jnp.maximum, peaks), axis=0, keepdims=True)
        sums = []
        for lo, hi in size.tiles():
            tile = jnp.exp2((scores[head, lo:hi] - top) * EXP2_SCALE)
            sums.append(folded(tile, jnp.sum))
            raised[head, lo:hi] = tile.astype(BF16)
        inverted = 1.0 / jnp.sum(sum(sums[1:], sums[0]), axis=0, keepdims=True)
        held = readout[:, cols(size.group() * size.width + head * HEAD_DIM, HEAD_DIM)]
        projected = [dot_nt(held, value) for value in values_of(size, blocks, head)]
        projected = jnp.concatenate(projected, axis=1).astype(BF16)
        velocity = dot(projected, raised[head]) * inverted
        each[head] = velocity
        inverse[head] = inverted
        velocities.append(velocity)
    total[...] = sum(velocities[1:], velocities[0]) * weight
    for half, out in enumerate(outs):
        out[...] = total[half_rows(size, half)]


def half_rows(size, half):
    per = size.ch // size.halves
    if size.halves == 1:
        return pl.ds(0, per)
    return pl.ds(pl.multiple_of((lax.axis_index("cfg") ^ half) * per, per), per)


def forward(size, guidance, blocks, readout):
    per = size.ch // size.halves
    return pl.pallas_call(
        functools.partial(forward_kernel, size),
        in_specs=[SMEM] + [size.full(x.shape) for x in blocks] + [size.full(readout.shape)],
        out_specs=[
            size.by_queries(size.heads, size.keys),
            size.by_queries(size.heads, size.ch),
            size.by_queries(size.heads, 1),
        ]
        + [size.by_queries(per)] * size.halves,
        out_shape=[
            jax.ShapeDtypeStruct((size.heads, size.keys, size.queries), BF16),
            jax.ShapeDtypeStruct((size.heads, size.ch, size.queries), F32),
            jax.ShapeDtypeStruct((size.heads, 1, size.queries), F32),
        ]
        + [jax.ShapeDtypeStruct((per, size.queries), F32)] * size.halves,
        scratch_shapes=[
            pltpu.VMEM((size.ch, size.q_block), F32),
            pltpu.VMEM((size.heads, size.keys, size.q_block), F32),
        ],
        compiler_params=size.params,
        name="attention_forward",
        **size.grid(),
    )(guidance, *blocks, readout)


def surrogate_gain(ratio, advantage):
    clipped = jnp.clip(ratio, 0.8, 1.2)
    keep = ratio * advantage <= clipped * advantage
    return jnp.where(keep, -ratio * advantage, jnp.zeros_like(ratio))


def relative_reward(every, own):
    count = len(every)
    mean = sum(every[1:], every[0]) / count
    square = sum([x * x for x in every[1:]], every[0] * every[0]) / count
    spread = jnp.sqrt(jnp.maximum(square - mean * mean, 0.0))
    return (own - mean) / jnp.maximum(spread, 1.0)


def combine_kernel(size, rate, part, other, noise, old, out):
    rows = half_rows(size, 0)
    out[:, : size.queries] = (part[...] + other[...]).astype(BF16)
    own = part[:, : size.sub] + other[:, : size.sub]
    own = own - (old[rows] + noise[rows] * (1.0 / rate[0]))
    high = own.astype(BF16)
    low = own - high.astype(F32)
    squares = jnp.sum(noise[rows] * noise[rows], axis=(0, 1), keepdims=True)
    near = squares.astype(BF16).astype(F32)
    far = (squares - near).astype(BF16).astype(F32)
    for index, value in enumerate((near, far, squares - near - far)):
        low = jnp.where(is_place(low.shape, index), value, low)
    out[:, : size.sub] = high
    out[:, size.queries :] = low.astype(BF16)


def is_place(shape, index):
    row = lax.broadcasted_iota(jnp.int32, shape, 0)
    lane = lax.broadcasted_iota(jnp.int32, shape, 1)
    return (row == 0) & (lane == index)


def combine(size, rate, part, other, noise, old):
    arrays = (part, other, noise, old)
    shape = (size.ch // size.halves, size.queries + size.sub)
    return pl.pallas_call(
        functools.partial(combine_kernel, size),
        grid=(1,),
        in_specs=[SMEM] + [whole(x.shape) for x in arrays],
        out_specs=whole(shape),
        out_shape=jax.ShapeDtypeStruct(shape, BF16),
        compiler_params=size.params,
        name="combine_branches",
    )(rate, *arrays)


def gather_guided_kernel(size, *refs):
    gathered, out = refs[:-1], refs[-1]
    per = size.ch // size.halves
    squares, norms = [], []
    for slot in range(size.parts):
        parts = []
        for apart in range(size.parts):
            other = slot ^ apart
            part = gathered[apart][:, other * size.sub : (other + 1) * size.sub].astype(F32)
            if apart == slot:
                low = gathered[apart][:, size.queries :].astype(F32)
                squares.append(low[:1, :1] + low[:1, 1:2] + low[:1, 2:3])
                for index in range(3):
                    low = jnp.where(is_place(low.shape, index), 0.0, low)
                part = part + low
            parts.append(part)
        left = tree_sum(parts)
        norms.append(jnp.sum(left * left, axis=(0, 1), keepdims=True))
        out[:per, slot * size.sub : (slot + 1) * size.sub] = left
    row = lax.broadcasted_iota(jnp.int32, (8, size.queries), 0)
    out[per:] = jnp.where(row == 0, tree_sum(squares), tree_sum(norms))


def gather_guided(size, gathered):
    shape = (size.ch // size.halves + 8, size.queries)
    return pl.pallas_call(
        functools.partial(gather_guided_kernel, size),
        grid=(1,),
        in_specs=[whole(x.shape) for x in gathered],
        out_specs=whole(shape),
        out_shape=jax.ShapeDtypeStruct(shape, F32),
        compiler_params=size.params,
        name="gather_guided",
    )(*gathered)


def velocity_grad(size, rate, guidance, stats, moved, grad, ratio_out):
    per = size.ch // size.halves
    norm = tree_sum([x[per + 1 : per + 2, :1] for x in moved])
    squares = tree_sum([x[per : per + 1, :1] for x in moved])
    own = lax.axis_index("img")
    every = [jnp.full((1, 1), stats[k], F32) for k in range(size.images)]
    advantage = relative_reward(every, jnp.full((1, 1), stats[own], F32))
    exponent = (squares - norm * (rate[0] * rate[0])) * (0.5 / (size.queries * size.ch))
    ratio = jnp.exp(exponent)
    gain = surrogate_gain(ratio, advantage)
    factor = gain * (-rate[0] * rate[0] * branch_weight(guidance[0]))
    for half, x in enumerate(moved):
        grad[half_rows(size, half)] = x[:per] * factor
    ratio_out[...] = ratio


def backward_kernel(size, *refs):
    if size.mirrored:
        rate, guidance, stats = refs[:3]
        moved = refs[3 : 3 + size.halves]
        refs = refs[3 + size.halves :]
    else:
        given, refs = refs[0], refs[1:]
    blocks = refs[: size.lists]
    readout, raised, each, inverse, ratio_out, readout_out = refs[size.lists : size.lists + 6]
    refs = refs[size.lists + 6 :]
    outs, refs = refs[: size.lists], refs[size.lists :]
    if size.late:
        late_outs, refs = refs[: size.lists], refs[size.lists :]
    grad_ref, scores, grad_keys, grad_queries, small = refs
    step = 0 if size.mirrored else pl.program_id(0)
    if size.mirrored:
        velocity_grad(size, rate, guidance, stats, moved, grad_ref, ratio_out)
    else:
        grad_ref[...] = given[...]
        ratio_out[...] = jnp.zeros(ratio_out.shape, F32)

    def add(ref, value):
        if size.q_blocks == 1:
            ref[...] = value
            return

        @pl.when(step == 0)
        def _():
            ref[...] = value

        @pl.when(step > 0)
        def _():
            ref[...] += value

    early = size.heads - size.late
    for head in range(size.heads):
        targets, lanes = (outs, lanes_of(head)) if head < early else (late_outs, lanes_of(head - early))
        query = queries_of(size, blocks, head, step)
        keys = keys_of(size, blocks, head)
        values = values_of(size, blocks, head)
        held = readout[:, cols(size.group() * size.width + head * HEAD_DIM, HEAD_DIM)]
        grad = (grad_ref[...] * inverse[head]).astype(BF16)
        delta = jnp.sum(grad.astype(F32) * each[head], axis=0, keepdims=True)
        little = dot_nt(raised[head], grad).T
        add(small.at[head], little)
        projected = dot_nt(jnp.concatenate(values, axis=0), held).astype(BF16)
        tile = dot(projected, grad) - delta
        scores[head] = (raised[head].astype(F32) * tile).astype(BF16)
        add(grad_keys.at[head], dot(scores[head], query) * SCALE)
        found = dot_tn(jnp.concatenate(keys, axis=0), scores[head]) * SCALE
        if size.mirrored:
            grad_queries[head] = found.astype(BF16).T
        else:
            first = pl.multiple_of(step * size.q_block, 128)
            grad_queries[head, pl.ds(first, size.q_block)] = found.astype(BF16).T

        def write():
            little = small[head].astype(BF16)
            readout_out[:, lanes_of(head)] = dot(little, jnp.concatenate(values, axis=0))
            value_text = dot_tn(little[:, size.img_keys :], held)
            for slot in range(size.parts):
                out = at(targets, slot)
                near = slice(slot * size.rows, (slot + 1) * size.rows)
                out[: size.sub, lanes] = grad_queries[head, slot * size.sub : (slot + 1) * size.sub]
                out[size.sub : size.sub + size.rows, lanes] = grad_keys[head, near].astype(BF16)
                start = size.img_keys + slot * size.txt
                pair = [
                    grad_keys[head, start : start + size.txt],
                    value_text[slot * size.txt : (slot + 1) * size.txt],
                ]
                pair = jnp.concatenate(pair, axis=0).astype(BF16)
                out[size.at_pair : size.at_small, lanes] = pair
                out[size.at_small :, lanes] = little[:, near]

        if size.mirrored:
            write()
        else:
            pl.when(step == size.q_blocks - 1)(write)


def backward(size, given, blocks, readout, saved):
    if size.mirrored:
        rate, guidance, stats, moved = given
        first = [rate, guidance, stats] + moved
        specs = [SMEM] * 3 + [size.full(x.shape) for x in moved]
    else:
        first, specs = [given], [size.by_queries(size.ch)]
    raised, each, inverse = saved
    shapes = [x for width in size.home_widths() for x in size.shapes(size.home_rows, width)]
    shapes = [
        jax.ShapeDtypeStruct((1, 1), F32),
        jax.ShapeDtypeStruct((size.ch, size.width), F32),
    ] + shapes
    outs = pl.pallas_call(
        functools.partial(backward_kernel, size),
        in_specs=specs
        + [size.full(x.shape) for x in blocks]
        + [
            size.full(readout.shape),
            size.by_queries(size.heads, size.keys),
            size.by_queries(size.heads, size.ch),
            size.by_queries(size.heads, 1),
        ],
        out_specs=[size.full(x.shape) for x in shapes],
        out_shape=shapes,
        scratch_shapes=[
            pltpu.VMEM((size.ch, size.q_block), F32),
            pltpu.VMEM((size.heads, size.keys, size.q_block), BF16),
            pltpu.VMEM((size.heads, size.keys, HEAD_DIM), F32),
            pltpu.VMEM((size.heads, size.queries, HEAD_DIM), BF16),
            pltpu.VMEM((size.heads, size.ch, size.keys), F32),
        ],
        compiler_params=size.params,
        name="attention_backward",
        **size.grid(),
    )(*first, *blocks, readout, raised, each, inverse)
    sent = outs[2:]
    return outs[0], outs[1], [sent[k : k + size.lists] for k in range(0, len(sent), size.lists)]


def home_kernel(size, readout, *refs):
    out, text_out = refs[-2:]
    offset = 0
    for index, width in enumerate(size.home_widths()):
        blocks = refs[index * size.lists : (index + 1) * size.lists]
        for group in range(size.groups):
            start = (size.base() ^ group) * size.width + offset
            place = cols(start, width)
            held = [at(blocks, group * size.copies + copy) for copy in range(size.copies)]
            for copy in range(size.copies):
                out[0, copy * size.sub : (copy + 1) * size.sub, place] = held[copy][: size.sub]
            if size.copies == 1:
                rest = held[0][size.sub : size.home_rows]
            else:
                rest = sum([x[size.sub :].astype(F32) for x in held]).astype(BF16)
            out[1, :, place] = rest[: size.rows]
            pair = rest[size.rows : size.rows + 2 * size.txt].astype(F32)
            pair = jnp.stack([pair[: size.txt], pair[size.txt :]], axis=1)
            text_out[:, :, place] = pair.astype(BF16)
            for head in range(width // HEAD_DIM):
                near = cols(start + head * HEAD_DIM, HEAD_DIM)
                lanes = slice(head * size.rows, (head + 1) * size.rows)
                little = rest[size.rows + 2 * size.txt :, lanes]
                out[2, :, near] = dot_tn(little, readout[:, near]).astype(BF16)
        offset += width


def home(size, readout, homes):
    shapes = [(3, size.rows, size.features), (size.txt, 2, size.features)]
    outs = [jax.ShapeDtypeStruct(x, BF16) for x in shapes]
    specs = [whole(x.shape) for blocks in homes for x in blocks]
    return pl.pallas_call(
        functools.partial(home_kernel, size),
        grid=(1,),
        in_specs=[whole(readout.shape)] + specs,
        out_specs=[whole(x.shape) for x in outs],
        out_shape=outs,
        compiler_params=size.params,
        name="home_tokens",
    )(readout, *[x for blocks in homes for x in blocks])


def join_readout_kernel(size, held, *refs):
    blocks, outs = refs[: size.parts], refs[size.parts :]
    rows = half_rows(size, 0)
    per = size.ch // size.halves
    total = tree_sum([held[k, rows].astype(F32) for k in range(size.images)]).astype(BF16)
    for block, out in zip(blocks, outs):
        out[0, : size.home_rows] = block[0]
        for head in range(size.heads):
            first = size.home_rows + head * per
            out[0, first : first + per] = total[:, head * HEAD_DIM : (head + 1) * HEAD_DIM]


def join_readout(size, part, blocks):
    sent = (part + mirror(part, "cfg", 1)).astype(BF16)
    held = lax.all_gather(sent, "img", axis=0)
    shape = (1, size.home_rows + size.heads * size.ch // size.halves, HEAD_DIM)
    return pl.pallas_call(
        functools.partial(join_readout_kernel, size),
        grid=(1,),
        in_specs=[whole(held.shape)] + [whole(x.shape) for x in blocks],
        out_specs=[whole(shape)] * size.parts,
        out_shape=[jax.ShapeDtypeStruct(shape, BF16)] * size.parts,
        compiler_params=size.params,
        name="join_readout_grad",
    )(held, *blocks)


def place_kernel(size, *refs):
    out = refs[-1]
    per = size.ch // size.halves
    for half in range(size.halves):
        for slot in range(size.parts):
            found = refs[half * size.parts + slot]
            for head in range(size.heads):
                lanes = cols((size.base() ^ slot) * size.width + head * HEAD_DIM, HEAD_DIM)
                first = size.home_rows + head * per
                out[half_rows(size, half), lanes] = found[0, first : first + per].astype(F32)


def place_readout(size, found):
    return pl.pallas_call(
        functools.partial(place_kernel, size),
        grid=(1,),
        in_specs=[whole(x.shape) for x in found],
        out_specs=whole((size.ch, size.features)),
        out_shape=jax.ShapeDtypeStruct((size.ch, size.features), F32),
        compiler_params=size.params,
        name="place_readout_grad",
    )(*found)


def on_device(img_qkv, txt_kv, readout, old_velocity, noise, step_ratio, rewards, guidance):
    features, channels = readout.shape
    size = Sizes(img_qkv.shape[2], txt_kv.shape[2], features, channels)
    place = lax.axis_index("seq")
    own = lax.axis_index("img")
    slots = img_qkv[0, 0].transpose(1, 0, 2)
    wide = readout.T
    strength = guidance.reshape(1)
    noise_wide, old_wide = noise[0].T, old_velocity[0].T
    text = txt_kv[0, 0]
    if size.mirrored:
        first = min(2, size.parts - 1)
        far = [first] + [k for k in range(1, size.parts) if k not in (1, first)]
        packed = {k: slice_tokens(size, slots, text, k) for k in far}
        if 1 not in packed:
            packed[1] = pack(size, slots, text, [1], 60 * MIB)[0]
        blocks = [mirror(packed[k], "seq", k) for k in range(1, size.parts)]
    else:
        blocks = exchange(size, pack(size, slots, text, list(range(size.parts)), 48 * MIB))

    mine = jnp.arange(size.images) == own
    stats = lax.psum(jnp.where(mine, rewards[0], 0.0), "img")
    if size.mirrored:
        stats, near, words = lax.optimization_barrier((stats, slots, text))
        blocks = list(pack(size, near, words, [0], 16 * MIB)) + blocks
        blocks = far_first(blocks)

    *saved, part = forward(size, strength, blocks, wide)
    if size.mirrored:
        saved, kept, part = saved[:3], saved[3], part
        other = mirror(part, "cfg", 1)
        sent = combine(size, step_ratio, kept, other, noise_wide, old_wide)
        guided = gather_guided(size, spread(size, [sent] * size.parts))
        given = (step_ratio, strength, stats, [guided, mirror(guided, "cfg", 1)])
    else:
        other = mirror(part, "cfg", 1)
        copy = place % size.copies
        rate = step_ratio[0]
        chosen = jnp.arange(size.copies).reshape(-1, 1, 1) == copy
        guided = lax.psum(jnp.where(chosen, (part + other)[None], 0.0), "seq")
        guided = lax.dynamic_index_in_dim(guided, copy, 0, False)
        mixed = lax.all_gather(noise_wide + rate * old_wide, "seq", axis=0)
        near = lax.dynamic_slice_in_dim(mixed, copy * size.sub, size.sub, 2)
        near = near.transpose(1, 0, 2).reshape(channels, size.queries)
        left = near - rate * guided
        norm = lax.psum(jnp.sum(left * left), "seq") / size.groups
        squares = lax.psum(jnp.sum(noise * noise), "seq")
        every = [stats[k] for k in range(size.images)]
        advantage = relative_reward(every, rewards[0])
        count = size.parts * size.rows * channels
        ratio = jnp.exp((squares - norm) * (0.5 / count))
        gain = surrogate_gain(ratio, advantage)
        given = left * (gain * (rate * branch_weight(guidance)))
    found, readout_part, sent = backward(size, given, blocks, wide, saved)
    if size.mirrored:
        ratio = found
    if size.late:
        homes = [exchange(size, sent[0])]
        homes.append(spread(size, join_readout(size, readout_part, sent[1])))
        joined = homes[1]
        found = joined + [mirror(x, "cfg", 1) for x in joined]
        token_grads, text_grads = home(size, wide, homes)
        token_grads, found = lax.optimization_barrier((token_grads, found))
        readout_grad = place_readout(size, found).T
    else:
        homes = [exchange(size, x) for x in sent]
        token_grads, text_grads = home(size, wide, homes)
        full = jnp.zeros((channels, features), F32)
        start = size.group() * size.width
        full = lax.dynamic_update_slice_in_dim(full, readout_part, start, 1)
        readout_grad = lax.psum(full, ("cfg", "img", "seq")).T
    img_grad = token_grads.transpose(1, 0, 2)[None, None]
    return (img_grad, text_grads[None, None], readout_grad, ratio.reshape(1))


def solution(mesh):
    return jax.shard_map(
        on_device,
        mesh=mesh,
        in_specs=(
            P("cfg", "img", "seq", None, None),
            P("cfg", "img", "seq", None, None),
            P(),
            P("img", "seq", None),
            P("img", "seq", None),
            P("img"),
            P("img"),
            P(),
        ),
        out_specs=(
            P("cfg", "img", "seq", None, None),
            P("cfg", "img", "seq", None, None),
            P(),
            P("img"),
        ),
        check_vma=False,
    )
```
